32 devices in a mesh: seq: 2 (over core), ctx: 8 (over z, y), fsdp: 2 (over x).
Axes of the slice: x: 2, y: 2, z: 4, core: 2. Of those that a mesh axis runs over, the one named last changes fastest.
Arguments:
- tokens: bfloat16 [4, 1024, 1024], P(('seq', 'fsdp'), 'ctx'), may hold values from -6 to 6
- qkv_weight: bfloat16 [1024, 3072], P(('seq', 'ctx', 'fsdp')), may hold values from -0.3125 to 0.3125
- out_weight: bfloat16 [1024, 1024], P(('seq', 'ctx', 'fsdp')), may hold values from -0.1875 to 0.1875
- up_weight: bfloat16 [1024, 4096], P(('seq', 'ctx', 'fsdp')), may hold values from -0.1875 to 0.1875
- down_weight: bfloat16 [4096, 1024], P(('seq', 'ctx', 'fsdp')), may hold values from -0.09375 to 0.09375
- query_bias: bfloat16 [1024], P(('seq', 'ctx', 'fsdp')), may hold values from -3 to 3
- value_bias: bfloat16 [1024], P(('seq', 'ctx', 'fsdp')), may hold values from -3 to 3
- out_bias: bfloat16 [1024], P(('seq', 'ctx', 'fsdp')), may hold values from -3 to 3
- up_bias: bfloat16 [4096], P(('seq', 'ctx', 'fsdp')), may hold values from -3 to 3
- down_bias: bfloat16 [1024], P(('seq', 'ctx', 'fsdp')), may hold values from -3 to 3
- norm1_gain: bfloat16 [1024], P(('seq', 'ctx', 'fsdp')), may hold values from 0.25 to 1.75
- norm1_bias: bfloat16 [1024], P(('seq', 'ctx', 'fsdp')), may hold values from -3 to 3
- norm2_gain: bfloat16 [1024], P(('seq', 'ctx', 'fsdp')), may hold values from 0.25 to 1.75
- norm2_bias: bfloat16 [1024], P(('seq', 'ctx', 'fsdp')), may hold values from -3 to 3
- cotangent: bfloat16 [4, 1024, 1024], P(('seq', 'fsdp'), 'ctx'), may hold values from -6 to 6
Outputs:
- output: bfloat16 [4, 1024, 1024], P(('seq', 'fsdp'), 'ctx')
- input_grad: float32 [4, 1024, 1024], P(('seq', 'fsdp'), 'ctx')
- qkv_weight_grad: float32 [1024, 3072], P(('seq', 'ctx', 'fsdp'))
- out_weight_grad: float32 [1024, 1024], P(('seq', 'ctx', 'fsdp'))
- up_weight_grad: float32 [1024, 4096], P(('seq', 'ctx', 'fsdp'))
- down_weight_grad: float32 [4096, 1024], P(('seq', 'ctx', 'fsdp'))
- query_bias_gradient: float32 [1024], P(('seq', 'ctx', 'fsdp'))
- value_bias_grad: float32 [1024], P(('seq', 'ctx', 'fsdp'))
- out_bias_grad: float32 [1024], P(('seq', 'ctx', 'fsdp'))
- up_bias_grad: float32 [4096], P(('seq', 'ctx', 'fsdp'))
- down_bias_grad: float32 [1024], P(('seq', 'ctx', 'fsdp'))
- norm1_gain_grad: float32 [1024], P(('seq', 'ctx', 'fsdp'))
- norm1_bias_grad: float32 [1024], P(('seq', 'ctx', 'fsdp'))
- norm2_gain_grad: float32 [1024], P(('seq', 'ctx', 'fsdp'))
- norm2_bias_grad: float32 [1024], P(('seq', 'ctx', 'fsdp'))
The draws below stay inside these ranges and needn't reach their ends.
All inputs are finite; a program needn't handle non-finite values.
Results may differ from the reference program's by a relative error of at most 0.019.
The reference program's roundings to bfloat16 on the way count: a program that leaves them out, or rounds other values in their place, can miss the bound.
Values may be sent and summed in bfloat16 or wider, within the bound.
A program may use at most 192 MiB of HBM per device.

```python
import math
import jax
import jax.numpy as jnp
from jax import lax

D = 1024
HEADS = 16
HEAD_DIM = 64
FF = 4096
LENGTH = 1024
SEQS = 4


def raised(entries, rng, source, target, parts, factor):
    owner, partner = [(jnp.arange(entries.shape[dim]) // (entries.shape[dim] // parts)).reshape([-1 if axis == dim else 1 for axis in range(entries.ndim)]) for dim in (source, target)]
    chosen = jax.random.permutation(rng, parts)[partner]
    strong = (owner == chosen) | (owner == (partner + parts // 2) % parts)
    return jnp.where(strong, factor * entries, entries)


def shard_levels(stream_key, dims, shards, low, top_value):
    level = 1.0
    for axis_at, shards_of in shards:
        heights = jax.random.uniform(jax.random.fold_in(jax.random.fold_in(stream_key, 6), axis_at), (shards_of,), jnp.float32, low / len(shards), top_value / len(shards))
        level = level * jnp.repeat(jnp.exp(heights), dims[axis_at] // shards_of).reshape((-1,) + (1,) * (len(dims) - 1 - axis_at))
    return level


def centred(stream_key, dims, scale, reach, shards=(), kind=jnp.bfloat16):
    values = scale * jax.random.normal(stream_key, dims, jnp.float32)
    if shards:
        values = values * shard_levels(stream_key, dims, shards, -0.22, 0.18)
    return jnp.clip(values, -reach, reach).astype(kind)


def gaussian_with(rng, shape, scale, reach, pieces, heavy, held_as=jnp.bfloat16):
    drawn = scale * jax.random.normal(rng, shape, jnp.float32)
    if pieces:
        drawn = drawn * shard_levels(rng, shape, pieces, -0.22, 0.18)
    return jnp.clip(raised(drawn, jax.random.fold_in(rng, 3), *heavy), -reach, reach).astype(held_as)


def setup_inputs(seed: int = 0) -> dict:
    splits = jax.random.split(jax.random.key(seed), 16)
    tokens = gaussian_with(splits[0], (SEQS, LENGTH, D), 1.0, 6.0, ((0, 4), (1, 8)), (1, 2, 8, 2.0))
    qkv_weight = centred(splits[1], (D, 3 * D), (D // 3) ** -0.5, 0.3125, ((0, 32),))
    out_weight = centred(splits[2], (D, D), D ** -0.5, 0.1875, ((0, 32),))
    up_weight = centred(splits[3], (D, FF), D ** -0.5, 0.1875, ((0, 32),))
    down_weight = centred(splits[4], (FF, D), FF ** -0.5, 0.09375, ((0, 32),))
    query_bias = centred(splits[5], (D,), 0.5, 3.0, ((0, 32),))
    value_bias = centred(splits[6], (D,), 0.5, 3.0, ((0, 32),))
    out_bias = centred(splits[7], (D,), 0.4, 3.0, ((0, 32),))
    up_bias = centred(splits[8], (FF,), 0.5, 3.0, ((0, 32),))
    down_bias = centred(splits[9], (D,), 0.4, 3.0, ((0, 32),))
    norm1_gain = jnp.clip(1.0 + 0.15 * jax.random.normal(splits[10], (D,), jnp.float32), 0.25, 1.75).astype(jnp.bfloat16)
    norm1_bias = centred(splits[11], (D,), 0.4, 3.0, ((0, 32),))
    norm2_gain = jnp.clip(1.0 + 0.15 * jax.random.normal(splits[12], (D,), jnp.float32), 0.25, 1.75).astype(jnp.bfloat16)
    norm2_bias = centred(splits[13], (D,), 0.4, 3.0, ((0, 32),))
    cotangent = centred(splits[14], (SEQS, LENGTH, D), 1.0, 6.0, ((0, 4), (1, 8)))
    return {"tokens": tokens, "qkv_weight": qkv_weight, "out_weight": out_weight, "up_weight": up_weight, "down_weight": down_weight, "query_bias": query_bias, "value_bias": value_bias, "out_bias": out_bias, "up_bias": up_bias, "down_bias": down_bias, "norm1_gain": norm1_gain, "norm1_bias": norm1_bias, "norm2_gain": norm2_gain, "norm2_bias": norm2_bias, "cotangent": cotangent}


epsilon = 1e-05
highest_precision_mode = lax.Precision.HIGHEST

@jax.custom_vjp
def low(v):
    return lax.optimization_barrier(v.astype(jnp.bfloat16)).astype(jnp.float32)

@jax.custom_vjp
def low_back(v):
    return v

def low_keep(v):
    return (low(v), None)

def low_pass(kept, grad):
    return (grad,)

def back_keep(v):
    return (v, None)

def back_low(kept, grad):
    return (low(grad),)
low.defvjp(low_keep, low_pass)
low_back.defvjp(back_keep, back_low)

def layer_norm(values, gain, shift):
    centered = values - lax.optimization_barrier(jnp.mean(values, axis=-1, keepdims=True))
    variance = lax.optimization_barrier(jnp.mean(centered * centered, axis=-1, keepdims=True))
    return centered * lax.rsqrt(variance + epsilon) * gain + shift

def attend_block(query_block, keys, values):
    scores = low_back(jnp.einsum('qhe,khe->hqk', query_block, keys, precision=highest_precision_mode) * HEAD_DIM ** (-0.5))
    weights = low(jax.nn.softmax(scores, axis=-1))
    return jnp.einsum('hqk,khe->qhe', weights, values, precision=highest_precision_mode)

def attend_sequence(triple):
    queries, keys, values = triple
    length = queries.shape[0]
    block = math.gcd(length, 512)
    blocks = queries.reshape(length // block, block, HEADS, HEAD_DIM)
    stepper = jax.checkpoint(lambda query_block: attend_block(query_block, keys, values))
    return lax.map(stepper, blocks).reshape(length, HEADS * HEAD_DIM)

def dense(left_neighbor, right_neighbor):
    return jnp.einsum('iru,uw->irw', left_neighbor, right_neighbor, precision=highest_precision_mode)

def forward(inputs, qkv_w, out_w, up_w, down_projection_weight, q_bias, v_bias, o_bias, u_bias, d_bias, gain_one, shift_one, gain_two, shift_two):
    seqs, length, width = inputs.shape
    joined_bias = jnp.concatenate([q_bias, jnp.zeros_like(q_bias), v_bias])
    qkv = low_back(low(dense(inputs, qkv_w) + joined_bias))
    queries = qkv[..., :width].reshape(seqs, length, HEADS, HEAD_DIM)
    keys = qkv[..., width:2 * width].reshape(seqs, length, HEADS, HEAD_DIM)
    values = qkv[..., 2 * width:].reshape(seqs, length, HEADS, HEAD_DIM)
    attended = lax.map(attend_sequence, (queries, keys, values))
    attended = low_back(low(attended))
    branch = low_back(dense(attended, out_w) + o_bias)
    first_norm = layer_norm(inputs + branch, gain_one, shift_one)
    hidden_pre = low_back(dense(low(first_norm), up_w) + u_bias)
    activated = low(jax.nn.gelu(hidden_pre, approximate=False))
    feed = low_back(dense(activated, down_projection_weight) + d_bias)
    return layer_norm(first_norm + feed, gain_two, shift_two)

def reference(tokens, qkv_weight, out_weight, up_weight, down_weight, query_bias, value_bias, out_bias, up_bias, down_bias, norm1_gain, norm1_bias, norm2_gain, norm2_bias, cotangent):
    primals = tuple((arr.astype(jnp.float32) for arr in (tokens, qkv_weight, out_weight, up_weight, down_weight, query_bias, value_bias, out_bias, up_bias, down_bias, norm1_gain, norm1_bias, norm2_gain, norm2_bias)))
    final, pullback = jax.vjp(forward, *primals)
    grads = pullback(cotangent.astype(jnp.float32))
    return (final.astype(jnp.bfloat16), grads[0], grads[1], grads[2], grads[3], grads[4], grads[5], grads[6], grads[7], grads[8], grads[9], grads[10], grads[11], grads[12], grads[13])
```

```python
import functools
import itertools
import math

import jax
import jax.numpy as jnp
from jax import lax
from jax.experimental import pallas as pl
from jax.experimental.pallas import tpu as pltpu
from jax.sharding import PartitionSpec as P

HEADS = 16
HEAD_DIM = 64


epsilon = 1e-05
MESH = pl.DeviceIdType.MESH
F32 = jnp.float32
BF16 = jnp.bfloat16
TILE = 256


def split_blocks(piece):
    rows = piece.shape[0]
    block = math.gcd(rows, 512)
    return (piece.reshape(rows // block, block, HEADS, HEAD_DIM), block)


def norm_forward(values, gain, shift):
    centered = values - jnp.mean(values, axis=-1, keepdims=True)
    recip = lax.rsqrt(jnp.mean(centered * centered, axis=-1, keepdims=True) + epsilon)
    normal = centered * recip
    return (normal * gain + shift, normal, recip)


def norm_backward(upstream, normal, recip, gain):
    gain_grad = jnp.sum(upstream * normal, axis=0)
    shift_grad = jnp.sum(upstream, axis=0)
    scaled = upstream * gain
    inner = (
        scaled
        - jnp.mean(scaled, axis=-1, keepdims=True)
        - normal * jnp.mean(scaled * normal, axis=-1, keepdims=True)
    )
    return (recip * inner, gain_grad, shift_grad)


def matmul(left_neighbor, right_neighbor):
    return jnp.dot(left_neighbor, right_neighbor, preferred_element_type=jnp.float32)


def on_device(
    tokens,
    qkv_weight,
    out_weight,
    up_weight,
    down_weight,
    query_bias,
    value_bias,
    out_bias,
    up_bias,
    down_bias,
    norm1_gain,
    norm1_bias,
    norm2_gain,
    norm2_bias,
    cotangent,
):
    gathered = (
        lax.all_gather(qkv_weight, ("seq", "ctx", "fsdp"), axis=0, tiled=True),
        lax.all_gather(out_weight, ("seq", "ctx", "fsdp"), axis=0, tiled=True),
        lax.all_gather(up_weight, ("seq", "ctx", "fsdp"), axis=0, tiled=True),
        lax.all_gather(down_weight, ("seq", "ctx", "fsdp"), axis=0, tiled=True),
        lax.all_gather(query_bias, ("seq", "ctx", "fsdp"), axis=0, tiled=True),
        lax.all_gather(value_bias, ("seq", "ctx", "fsdp"), axis=0, tiled=True),
        lax.all_gather(out_bias, ("seq", "ctx", "fsdp"), axis=0, tiled=True),
        lax.all_gather(up_bias, ("seq", "ctx", "fsdp"), axis=0, tiled=True),
        lax.all_gather(down_bias, ("seq", "ctx", "fsdp"), axis=0, tiled=True),
        lax.all_gather(norm1_gain, ("seq", "ctx", "fsdp"), axis=0, tiled=True),
        lax.all_gather(norm1_bias, ("seq", "ctx", "fsdp"), axis=0, tiled=True),
        lax.all_gather(norm2_gain, ("seq", "ctx", "fsdp"), axis=0, tiled=True),
        lax.all_gather(norm2_bias, ("seq", "ctx", "fsdp"), axis=0, tiled=True),
    )
    qkv_full, out_full, up_full, down_full = (gathered[0], gathered[1], gathered[2], gathered[3])
    small = tuple((item.astype(jnp.float32) for item in gathered[4:]))
    q_shift, v_shift, o_shift, u_shift, d_shift, gain_one, shift_one, gain_two, shift_two = small
    scale = HEAD_DIM ** (-0.5)
    inputs = tokens[0]
    rows = inputs.shape[0]
    width = inputs.shape[1]
    joined_bias = jnp.concatenate([q_shift, jnp.zeros_like(q_shift), v_shift])
    qkv_low = (matmul(inputs, qkv_full) + joined_bias).astype(jnp.bfloat16)
    queries = qkv_low[:, :width].reshape(rows, HEADS, HEAD_DIM)
    keys_own = qkv_low[:, width : 2 * width]
    values_own = qkv_low[:, 2 * width :]
    start_state = (
        jnp.full((HEADS, rows), -1e30, jnp.float32),
        jnp.zeros((HEADS, rows), jnp.float32),
        jnp.zeros((rows, HEADS, HEAD_DIM), jnp.float32),
    )
    piece = (
        lax.all_gather(keys_own, "ctx", axis=0, tiled=True),
        lax.all_gather(values_own, "ctx", axis=0, tiled=True),
    )
    key_blocks, block = split_blocks(piece[0])
    value_blocks, block = split_blocks(piece[1])

    def inner(state, pair):
        run_max, run_sum, accum = state
        key_tile_rows, value_block = pair
        scores = (
            jnp.einsum("qhe,khe->hqk", queries, key_tile_rows, preferred_element_type=jnp.float32)
            * scale
        )
        new_max = jnp.maximum(run_max, jnp.max(scores, axis=-1))
        factor = jnp.exp(run_max - new_max)
        weights = jnp.exp(scores - new_max[..., None])
        run_sum = run_sum * factor + jnp.sum(weights, axis=-1)
        accum = accum * factor.T[..., None] + jnp.einsum(
            "hqk,khe->qhe",
            weights.astype(jnp.bfloat16),
            value_block,
            preferred_element_type=jnp.float32,
        )
        return ((new_max, run_sum, accum), None)

    result, unused = lax.scan(inner, start_state, (key_blocks, value_blocks))
    run_max, run_sum, accum = result
    attended = accum / run_sum.T[..., None]
    log_total = run_max + jnp.log(run_sum)
    attended_low = attended.reshape(rows, width).astype(jnp.bfloat16)
    first_sum = inputs.astype(jnp.float32) + matmul(attended_low, out_full) + o_shift
    first_norm, normal_one, recip_one = norm_forward(first_sum, gain_one, shift_one)
    normed_low = first_norm.astype(jnp.bfloat16)
    hidden_pre = matmul(normed_low, up_full) + u_shift
    activated_full, gelu_pull = jax.vjp(lambda pre: jax.nn.gelu(pre, approximate=False), hidden_pre)
    activated = activated_full.astype(jnp.bfloat16)
    second_sum = first_norm + matmul(activated, down_full) + d_shift
    final, normal_two, recip_two = norm_forward(second_sum, gain_two, shift_two)
    upstream = cotangent[0].astype(jnp.float32)
    d_second, gain_two_grad, shift_two_grad = norm_backward(
        upstream, normal_two, recip_two, gain_two
    )
    d_feed = d_second.astype(jnp.bfloat16)
    down_grad = matmul(activated.T, d_feed)
    down_bias_grad = jnp.sum(d_feed.astype(jnp.float32), axis=0)
    d_hidden = gelu_pull(matmul(d_feed, down_full.T))[0].astype(jnp.bfloat16)
    up_grad = matmul(normed_low.T, d_hidden)
    up_bias_grad = jnp.sum(d_hidden.astype(jnp.float32), axis=0)
    first_input_gradient = d_second + matmul(d_hidden, up_full.T)
    d_sum_one, gain_one_grad, first_shift_gradient = norm_backward(
        first_input_gradient, normal_one, recip_one, gain_one
    )
    d_branch = d_sum_one.astype(jnp.bfloat16)
    out_grad = matmul(attended_low.T, d_branch)
    out_bias_grad = jnp.sum(d_branch.astype(jnp.float32), axis=0)
    d_attended = matmul(d_branch, out_full.T).astype(jnp.bfloat16).reshape(rows, HEADS, HEAD_DIM)
    delta = jnp.sum(d_attended.astype(jnp.float32) * attended, axis=-1).T
    total_rows = rows * lax.axis_size("ctx")
    zero_query = jnp.zeros((rows, HEADS, HEAD_DIM), jnp.float32)
    start_back = (zero_query, jnp.zeros((total_rows, 2 * width), jnp.float32))
    piece = (
        lax.all_gather(keys_own, "ctx", axis=0, tiled=True),
        lax.all_gather(values_own, "ctx", axis=0, tiled=True),
    )
    key_blocks, block = split_blocks(piece[0])
    value_blocks, block = split_blocks(piece[1])
    counter = jnp.arange(key_blocks.shape[0], dtype=jnp.int32)

    def inner(state, triple):
        key_tile_rows, value_block, number = triple
        scores = (
            jnp.einsum("qhe,khe->hqk", queries, key_tile_rows, preferred_element_type=jnp.float32)
            * scale
        )
        weights = jnp.exp(scores - log_total[..., None])
        d_probs = jnp.einsum(
            "qhe,khe->hqk", d_attended, value_block, preferred_element_type=jnp.float32
        )
        d_scores = (weights * (d_probs - delta[..., None]) * scale).astype(jnp.bfloat16)
        d_query = state[0] + jnp.einsum(
            "hqk,khe->qhe", d_scores, key_tile_rows, preferred_element_type=jnp.float32
        )
        d_key = jnp.einsum(
            "hqk,qhe->khe", d_scores, queries, preferred_element_type=jnp.float32
        ).reshape(block, width)
        d_value = jnp.einsum(
            "hqk,qhe->khe",
            weights.astype(jnp.bfloat16),
            d_attended,
            preferred_element_type=jnp.float32,
        ).reshape(block, width)
        offset = number * block
        current = lax.dynamic_slice_in_dim(state[1], offset, block, 0)
        updated = lax.dynamic_update_slice_in_dim(
            state[1], current + jnp.concatenate([d_key, d_value], axis=1), offset, 0
        )
        return ((d_query, updated), None)

    result, unused = lax.scan(inner, start_back, (key_blocks, value_blocks, counter))
    d_query = result[0].reshape(rows, width)
    summed = lax.psum_scatter(result[1], "ctx", scatter_dimension=0, tiled=True)
    d_key = summed[:, :width]
    d_value = summed[:, width:]
    d_qkv = jnp.concatenate([d_query, d_key, d_value], axis=1).astype(jnp.bfloat16)
    qkv_grad = matmul(inputs.T, d_qkv)
    d_qkv_wide = d_qkv.astype(jnp.float32)
    query_bias_gradient = jnp.sum(d_qkv_wide[:, :width], axis=0)
    value_bias_grad = jnp.sum(d_qkv_wide[:, 2 * width :], axis=0)
    input_grad = matmul(d_qkv, qkv_full.T) + d_sum_one
    sharded = (
        lax.psum_scatter(qkv_grad, ("seq", "ctx", "fsdp"), scatter_dimension=0, tiled=True),
        lax.psum_scatter(out_grad, ("seq", "ctx", "fsdp"), scatter_dimension=0, tiled=True),
        lax.psum_scatter(up_grad, ("seq", "ctx", "fsdp"), scatter_dimension=0, tiled=True),
        lax.psum_scatter(down_grad, ("seq", "ctx", "fsdp"), scatter_dimension=0, tiled=True),
        lax.psum_scatter(
            query_bias_gradient, ("seq", "ctx", "fsdp"), scatter_dimension=0, tiled=True
        ),
        lax.psum_scatter(value_bias_grad, ("seq", "ctx", "fsdp"), scatter_dimension=0, tiled=True),
        lax.psum_scatter(out_bias_grad, ("seq", "ctx", "fsdp"), scatter_dimension=0, tiled=True),
        lax.psum_scatter(up_bias_grad, ("seq", "ctx", "fsdp"), scatter_dimension=0, tiled=True),
        lax.psum_scatter(down_bias_grad, ("seq", "ctx", "fsdp"), scatter_dimension=0, tiled=True),
        lax.psum_scatter(gain_one_grad, ("seq", "ctx", "fsdp"), scatter_dimension=0, tiled=True),
        lax.psum_scatter(
            first_shift_gradient, ("seq", "ctx", "fsdp"), scatter_dimension=0, tiled=True
        ),
        lax.psum_scatter(gain_two_grad, ("seq", "ctx", "fsdp"), scatter_dimension=0, tiled=True),
        lax.psum_scatter(shift_two_grad, ("seq", "ctx", "fsdp"), scatter_dimension=0, tiled=True),
    )
    return (
        final.astype(jnp.bfloat16)[None],
        input_grad[None],
        sharded[0],
        sharded[1],
        sharded[2],
        sharded[3],
        sharded[4],
        sharded[5],
        sharded[6],
        sharded[7],
        sharded[8],
        sharded[9],
        sharded[10],
        sharded[11],
        sharded[12],
    )


def dot(left, right, left_dim=1, right_dim=0):
    return lax.dot_general(
        left, right, (((left_dim,), (right_dim,)), ((), ())), preferred_element_type=F32
    )


def loop(count, body):
    def step(i, carry):
        body(i)
        return carry

    lax.fori_loop(0, count, step, 0)


def spread_matrix(width, piece, at):
    lane = lax.broadcasted_iota(jnp.int32, (128, width), 0)
    column = lax.broadcasted_iota(jnp.int32, (128, width), 1)
    return jnp.where(lane == at * piece + column % piece, 1.0, 0.0)


def own_columns(blocks, width):
    row = lax.broadcasted_iota(jnp.int32, (blocks, width), 0)
    column = lax.broadcasted_iota(jnp.int32, (blocks, width), 1)
    return column // (width // blocks) == row


def layer_kernel(
    tok, qkvw, outw, upw, downw, pack, cot,
    out_o, ig_o, qkvg_o, outg_o, upg_o, downg_o, small_o,
    X16, WP, WH, G, OW, UW, DW,
    QN, KN, VN, QKVT, OT, OTB, LSE, AS, AT, A4,
    R1A, R1B, R1C, R1D, R2A, R2B, R2C, R2D, KR,
    N4, N4T, C4, C4T, GP, DF4,
    FN, NORM1, DSEC,
    DS, DR, DA, DAT, DKV, DQT, DQKV, DQKVT,
    USA, URA, USB, URB, USC, URC, UK, UF,
    DSA, DRA, DSB, DRB, DSC, DRC, DK,
    OSA, ORA, OSB, ORB, OSC, ORC, OK,
    IRA, ISB, IRB, ISC, IRC, ISD, IRD, IK,
    QSA, QRA, QK, QSB, QG,
    VEC, UB, VG, SG, RG,
    ssem, rsem, wss, wrs, gss, grs, hss, hrs,
):
    s = lax.axis_index("seq")
    c = lax.axis_index("ctx")
    x = lax.axis_index("fsdp")
    h, l, y = c // 4, (c // 2) % 2, c % 2
    here = {"s": s, "h": h, "l": l, "y": y, "x": x}
    me = s * 16 + c * 2 + x
    head = s * 8 + c
    width = tok.shape[1]
    tiles = width // TILE
    counter = itertools.count()
    sends = []

    def at(flips):
        return {k: (1 - v if k in flips else v) for k, v in here.items()}

    def device(flips):
        p = at(flips)
        return {"seq": p["s"], "ctx": p["h"] * 4 + p["l"] * 2 + p["y"], "fsdp": p["x"]}

    def ids(n=1):
        return [next(counter) for _ in range(n)][0]

    def copy(src, dst, sem, flips):
        return pltpu.make_async_remote_copy(
            src_ref=src, dst_ref=dst, send_sem=ssem.at[sem], recv_sem=rsem.at[sem],
            device_id=device(flips), device_id_type=MESH,
        )

    def settle(since):
        for d in sends[since:]:
            d.wait_send()
        del sends[since:]

    def send(src, dst, sem, flips):
        d = copy(src, dst, sem, flips)
        d.start()
        sends.append(d)

    def wait(ref, sem, flips):
        copy(ref, ref, sem, flips).wait_recv()

    class Gather:
        def __init__(self, order, block):
            self.order, self.block, self.sem = order, block, {}
            for n in range(1, len(order) + 1):
                for k in itertools.combinations(order, n):
                    self.sem[frozenset(k)] = ids()

        def push(self, *have):
            have = frozenset(have)
            last = max([self.order.index(d) for d in have], default=-1)
            for d in self.order[last + 1 :]:
                ref = self.block(at(have))
                send(ref, ref, self.sem[have | {d}], (d,))

        def pull(self, *have):
            have = frozenset(have)
            last = max(have, key=self.order.index)
            wait(self.block(at(have)), self.sem[have], (last,))

        def pass_on(self, *have):
            self.pull(*have)
            self.push(*have)

    barrier = pltpu.get_barrier_semaphore()

    def peer(j):
        b = (me + j) % 32
        return {"seq": b // 16, "ctx": (b // 2) % 8, "fsdp": b % 2}

    loop(31, lambda j: pl.semaphore_signal(barrier, inc=1, device_id=peer(j + 1), device_id_type=MESH))

    X16[s, h, l, y] = tok[...]
    for k in range(HEADS):
        parts = [qkvw[:, j * width + k * HEAD_DIM : j * width + (k + 1) * HEAD_DIM] for j in range(3)]
        WP[k, :, 0 : 3 * HEAD_DIM] = jnp.concatenate(parts, axis=1)
    WH[me] = WP[head]
    G[me] = pack[...]
    OW[h, y, x] = outw[...]
    DW[h, y, x] = downw[...]

    def quarter(sp, hp, lp):
        return pl.ds(pl.multiple_of(sp * 2048 + hp * 1024 + lp * 512, 512), 512)

    for hp in range(2):
        UW[s, h, l, y, x, :, hp * 512 : (hp + 1) * 512] = upw[:, quarter(s, hp, l)]

    pl.semaphore_wait(barrier, 31)

    half = width // 2

    def token_block(k):
        return lambda p: X16.at[p["s"], p["h"], p["l"], p["y"], :, pl.ds(k * half, half)]

    xg = [Gather("hyls", token_block(0)), Gather("hlys", token_block(1))]
    for g in xg:
        g.push()

    def small_copy(j, dst):
        b = (me + j) % 32
        return [
            pltpu.make_async_remote_copy(
                src_ref=WP.at[b // 2], dst_ref=WH.at[dst], send_sem=wss.at[j], recv_sem=wrs.at[j],
                device_id=peer(j), device_id_type=MESH),
            pltpu.make_async_remote_copy(
                src_ref=pack, dst_ref=G.at[dst], send_sem=gss.at[j], recv_sem=grs.at[j],
                device_id=peer(j), device_id_type=MESH),
        ]

    loop(31, lambda j: [d.start() for d in small_copy(j + 1, me)])

    up_sem = {}
    for flips in (("s",), ("l",), ("s", "l")):
        p = at(flips)
        for hp in range(2):
            up_sem[flips, hp] = ids()
            send(
                upw.at[:, quarter(p["s"], hp, p["l"])],
                UW.at[s, h, l, y, x, :, pl.ds(hp * 512, 512)],
                up_sem[flips, hp], flips,
            )
    og = Gather("hyx", lambda p: OW.at[p["h"], p["y"], p["x"]])
    ug = Gather("hyx", lambda p: UW.at[:, p["h"], :, p["y"], p["x"]])
    dg = Gather("hyx", lambda p: DW.at[p["h"], p["y"], p["x"]])
    og.push()

    for g, a, b in ((xg[0], "y", "l"), (xg[1], "l", "y")):
        g.pass_on("h")
    for flips in (("s",), ("l",), ("s", "l")):
        p = at(flips)
        for hp in range(2):
            wait(UW.at[p["s"], h, p["l"], y, x, :, pl.ds(hp * 512, 512)], up_sem[flips, hp], flips)
    ug.push()
    xg[0].pass_on("y")
    xg[1].pass_on("l")
    xg[0].pass_on("h", "y")
    xg[1].pass_on("h", "l")
    og.pass_on("h")
    og.pass_on("y")
    og.pass_on("h", "y")
    dg.push()
    for have in (("l",), ("h", "l"), ("y", "l"), ("h", "y", "l")):
        xg[0].pass_on(*have)
    for have in (("y",), ("h", "y"), ("l", "y"), ("h", "l", "y")):
        xg[1].pass_on(*have)
    ug.pass_on("h")
    ug.pass_on("y")
    ug.pass_on("h", "y")

    def wait_small(j):
        for d in small_copy(j + 1, (me + 31 - j) % 32):
            d.wait_recv()

    loop(31, wait_small)

    spread = [spread_matrix(width, 32, j).astype(BF16) for j in range(4)]
    mine = own_columns(32, width)
    for row, j, to in ((0, 2, 0), (0, 3, 1), (1, 0, 2), (1, 1, 3), (1, 2, 4), (1, 3, 5)):
        rows = G[:, row, :].astype(BF16)
        VEC[to : to + 1, :] = jnp.sum(jnp.where(mine, dot(rows, spread[j]), 0.0), axis=0, keepdims=True)
    for hp, yp, xp in itertools.product(range(2), repeat=3):
        r = hp * 4 + yp * 2 + xp
        UB[0:1, r * 128 : (r + 1) * 128] = G[s * 16 + hp * 8 + l * 4 + yp * 2 + xp, 2:3, :]
    out_bias, down_bias = VEC[0:1, :], VEC[1:2, :]
    gain_one, shift_one, gain_two, shift_two = (VEC[k : k + 1, :] for k in range(2, 6))
    first, second = G[head * 2, 0:1, :], G[head * 2 + 1, 0:1, :]
    head_bias = jnp.concatenate(
        [first[:, 0:32], second[:, 0:32], jnp.zeros((1, 64), F32), first[:, 32:64], second[:, 32:64]], axis=1
    )
    head_weight = WH[...].reshape(width, WH.shape[2])[:, 0 : 3 * HEAD_DIM]

    length = 8 * tok.shape[0]
    qtiles = length // TILE
    scale = HEAD_DIM ** (-0.5)
    DH4, DB4, DSUM = C4, N4, FN

    def project(j):
        sp = s if j == 0 else 1 - s

        def body(i):
            hl = X16[sp, i // 2, i % 2].reshape(TILE, width)
            res = (dot(hl, head_weight) + head_bias).astype(BF16).astype(F32)
            rows = pl.ds(pl.multiple_of(i * TILE, TILE), TILE)
            QN[j, rows, :] = res[:, 0:64].astype(BF16)
            KN[j, rows, :] = res[:, 64:128].astype(BF16)
            VN[j, rows, :] = res[:, 128:192].astype(BF16)
            QKVT[j, :, rows] = res.T.astype(BF16)

        loop(qtiles, body)

    def attend(j):
        def body(i):
            cols = pl.ds(pl.multiple_of(i * TILE, TILE), TILE)
            q = QKVT[j, 0:64, cols] * jnp.asarray(scale, BF16)
            st = dot(KN[j], q)
            top = jnp.max(st, axis=0, keepdims=True)
            e = jnp.exp(st - top)
            total = jnp.sum(e, axis=0, keepdims=True)
            o = dot(QKVT[j, 128:192, :], e.astype(BF16)) / total
            OT[j, :, cols] = o
            OTB[j, :, cols] = o.astype(BF16)
            LSE[j, 0:1, cols] = top + jnp.log(total)

        loop(qtiles, body)

    project(0)
    attend(0)
    for have in (("s",), ("h", "s"), ("y", "s"), ("h", "y", "s"), ("l", "s"), ("h", "l", "s"), ("y", "l", "s"), ("h", "y", "l", "s")):
        for g in xg:
            g.pull(*have)
    project(1)
    attend(1)
    dg.pass_on("h")
    dg.pass_on("y")
    dg.pass_on("h", "y")

    tokens = tok.shape[0]

    def tok_cols(hp, lp, yp):
        return pl.ds(pl.multiple_of((hp * 4 + lp * 2 + yp) * tokens, tokens), tokens)

    others = (("h",), ("y",), ("h", "y"))
    a_sem = {f: ids() for f in others}
    for k, flips in enumerate(((),) + others):
        p = at(flips)
        for sp, lp in itertools.product(range(2), repeat=2):
            j = s if sp == 0 else 1 - s
            to = pl.ds((sp * 2 + lp) * tokens, tokens)
            piece = OTB[j, :, tok_cols(p["h"], lp, p["y"])]
            if flips:
                AS[k, :, to] = piece
            else:
                AT[h, y, :, to] = piece
        if flips:
            send(AS.at[k], AT.at[h, y], a_sem[flips], flips)
    for have in (("x",), ("h", "x"), ("y", "x"), ("h", "y", "x")):
        og.pull(*have)
    for flips in others:
        p = at(flips)
        wait(AT.at[p["h"], p["y"]], a_sem[flips], flips)

    group = 4 * tokens
    A4[...] = AT[...].reshape(4 * HEAD_DIM, group).astype(F32).T.astype(BF16)

    def group_sum(bufs, tile_fn):
        sa, ra, sb, rb = bufs
        base_a, base_b = [ids() for _ in range(tiles)][0], [ids() for _ in range(tiles)][0]

        def a(i):
            sa[i] = tile_fn(1 - s, i).astype(BF16)
            copy(sa.at[i], ra.at[i], base_a + i, ("s",)).start()

        loop(tiles, a)

        def b(i):
            v = tile_fn(s, i)
            wait(ra.at[i], base_a + i, ("s",))
            KR[i] = (v + ra[i].astype(F32)).reshape(2, tokens, TILE)
            sb[i] = KR[i, 1 - l].astype(BF16)
            copy(sb.at[i], rb.at[i], base_b + i, ("l",)).start()

        loop(tiles, b)
        for i in range(tiles):
            wait(rb.at[i], base_b + i, ("l",))
        for i in range(tiles):
            sends.append(copy(sa.at[i], ra.at[i], base_a + i, ("s",)))
            sends.append(copy(sb.at[i], rb.at[i], base_b + i, ("l",)))
        return jnp.concatenate([KR[i, l] + rb[i].astype(F32) for i in range(tiles)], axis=1)

    def group_rows(sp):
        return pl.ds(pl.multiple_of(sp * 2 * tokens, 2 * tokens), 2 * tokens)

    def col_tile(i):
        return pl.ds(pl.multiple_of(i * TILE, TILE), TILE)

    mark = len(sends)
    branch = group_sum(
        (R1A, R1B, R1C, R1D),
        lambda sp, i: dot(A4[group_rows(sp), :], OW[:, :, :, :, col_tile(i)].reshape(4 * HEAD_DIM, TILE)),
    )

    def norm_forward(values, gain, shift):
        centered = values - jnp.mean(values, axis=-1, keepdims=True)
        recip = lax.rsqrt(jnp.mean(centered * centered, axis=-1, keepdims=True) + epsilon)
        normal = centered * recip
        return normal * gain + shift, normal, recip

    def norm_backward(upstream, normal, recip, gain):
        gain_grad = jnp.sum(upstream * normal, axis=0, keepdims=True)
        shift_grad = jnp.sum(upstream, axis=0, keepdims=True)
        scaled = upstream * gain
        inner = (
            scaled
            - jnp.mean(scaled, axis=-1, keepdims=True)
            - normal * jnp.mean(scaled * normal, axis=-1, keepdims=True)
        )
        return recip * inner, gain_grad, shift_grad

    first_norm, normal_one, recip_one = norm_forward(
        tok[...].astype(F32) + branch + out_bias, gain_one, shift_one
    )
    FN[...] = first_norm
    NORM1[...] = normal_one

    def group_gather(ref, value, meanwhile=None):
        g = Gather("ls", lambda p: ref.at[p["s"], p["l"]])
        ref[s, l] = value
        g.push()
        if meanwhile is not None:
            meanwhile()
        g.pass_on("l")
        g.pull("s")
        g.pull("l", "s")

    group_gather(N4, first_norm.astype(BF16))
    settle(mark)

    for have in (("x",), ("h", "x"), ("y", "x"), ("h", "y", "x")):
        ug.pull(*have)
    hidden = UB.shape[1]

    def all_rows(ref):
        return ref[...].reshape(group, ref.shape[-1])

    def up(i):
        cols = col_tile(i)
        w = UW[:, :, :, :, :, :, cols].reshape(width, TILE)
        pre = dot(all_rows(N4), w) + UB[0:1, cols]
        phi = 0.5 * (1.0 + lax.erf(pre * (2.0 ** -0.5)))
        act = pre * phi
        GP[:, cols] = phi + pre * (jnp.exp(-0.5 * pre * pre) * ((2.0 * math.pi) ** -0.5))
        C4[:, cols] = act.astype(BF16)

    loop(hidden // TILE, up)
    for have in (("x",), ("h", "x"), ("y", "x"), ("h", "y", "x")):
        dg.pull(*have)
    feed = group_sum(
        (R2A, R2B, R2C, R2D),
        lambda sp, i: dot(C4[group_rows(sp), :], DW[:, :, :, :, col_tile(i)].reshape(hidden, TILE)),
    )
    final, normal_two, recip_two = norm_forward(FN[...] + feed + down_bias, gain_two, shift_two)
    out_o[...] = final.astype(BF16)
    d_second, gain_two_grad, shift_two_grad = norm_backward(
        cot[...].astype(F32), normal_two, recip_two, gain_two
    )
    DSEC[...] = d_second
    d_feed = d_second.astype(BF16)
    VG[1:2, :] = jnp.sum(d_feed.astype(F32), axis=0, keepdims=True)
    VG[4:5, :] = gain_two_grad
    VG[5:6, :] = shift_two_grad

    def transpose_rows(i):
        cols = pl.ds(pl.multiple_of(i * 128, 128), 128)
        t = N4[:, :, :, cols].reshape(group, 128)
        t = t.astype(F32).T.astype(BF16).reshape(2, 2, 32, group)
        for yp, xp in itertools.product(range(2), repeat=2):
            to = pl.ds(pl.multiple_of((i // 4 * 2 + i % 2) * 32, 32), 32)
            N4T[(i // 2) % 2, yp, xp, to, :] = t[yp, xp]
        C4T[i // 4, (i // 2) % 2, i % 2] = C4[:, cols].astype(F32).T.astype(BF16)

    group_gather(DF4, d_feed, lambda: loop(8, transpose_rows))

    def d_hidden(i):
        rows = DW[i // 2, i % 2].reshape(TILE, width)
        cols = col_tile(i)
        v = (dot(all_rows(DF4), rows, 1, 1) * GP[:, cols]).astype(BF16)
        DH4[:, cols] = v
        UB[1:2, cols] = jnp.sum(v.astype(F32), axis=0, keepdims=True)

    loop(hidden // TILE, d_hidden)

    def up_rows(i):
        return UW[i // 2, i % 2].reshape(TILE, hidden)

    d_first = group_sum(
        (R1A, R1B, R1C, R1D), lambda sp, i: dot(DH4[group_rows(sp), :], up_rows(i), 1, 1)
    )
    d_sum_one, gain_one_grad, shift_one_grad = norm_backward(
        DSEC[...] + d_first, NORM1[...], recip_one, gain_one
    )
    DSUM[...] = d_sum_one
    d_branch = d_sum_one.astype(BF16)
    VG[0:1, :] = jnp.sum(d_branch.astype(F32), axis=0, keepdims=True)
    VG[2:3, :] = gain_one_grad
    VG[3:4, :] = shift_one_grad
    group_gather(DB4, d_branch)

    d_att = dot(all_rows(DB4), OW[...].reshape(4 * HEAD_DIM, width), 1, 1).astype(BF16)
    d_att = d_att.astype(F32).T.astype(BF16).reshape(2, 2, HEAD_DIM, group)
    DS[...] = d_att
    d_sem = {f: ids() for f in others}
    for flips in others:
        p = at(flips)
        send(DS.at[p["h"], p["y"]], DR.at[h, y], d_sem[flips], flips)
    DR[h, y] = DS[h, y]

    class Scatter:
        def __init__(self, bufs, product):
            self.sa, self.ra, self.sb, self.rb, self.sc, self.rc, self.keep = bufs
            self.product = product
            self.a, self.b, self.c = ([ids() for _ in range(tiles)][0] for _ in range(3))
            self.shape = self.sa.shape[1:]

        def done(self, src, dst, base, dim):
            for i in range(tiles):
                sends.append(copy(src.at[i], dst.at[i], base + i, (dim,)))

        def first(self):
            def body(i):
                self.sa[i] = self.product(1 - x, i).reshape(self.shape).astype(BF16)
                copy(self.sa.at[i], self.ra.at[i], self.a + i, ("x",)).start()

            loop(tiles, body)
            self.done(self.sa, self.ra, self.a, "x")

        def second(self):
            def body(i):
                v = self.product(x, i).reshape(self.shape)
                wait(self.ra.at[i], self.a + i, ("x",))
                self.keep[i] = v + self.ra[i].astype(F32)
                self.sb[i] = self.keep[i, :, 1 - y].astype(BF16)
                copy(self.sb.at[i], self.rb.at[i], self.b + i, ("y",)).start()

            loop(tiles, body)
            self.done(self.sb, self.rb, self.b, "y")

        def third(self):
            def body(i):
                wait(self.rb.at[i], self.b + i, ("y",))
                self.keep[i, :, 0] = self.keep[i, :, y] + self.rb[i].astype(F32)
                self.sc[i] = self.keep[i, 1 - h, 0].astype(BF16)
                copy(self.sc.at[i], self.rc.at[i], self.c + i, ("h",)).start()

            loop(tiles, body)
            self.done(self.sc, self.rc, self.c, "h")

        def last(self, out):
            def body(i):
                wait(self.rc.at[i], self.c + i, ("h",))
                out[:, col_tile(i)] = self.keep[i, h, 0] + self.rc[i].astype(F32)

            loop(tiles, body)

    def up_product(xp, i):
        return dot(N4T[:, :, xp].reshape(group, group), DH4[:, col_tile(i)])

    def down_product(xp, i):
        return dot(
            C4T[:, :, xp].reshape(group, group),
            DF4[:, :, :, col_tile(i)].reshape(group, TILE),
        )

    def out_product(xp, i):
        rows = pl.ds(pl.multiple_of(xp * 32, 32), 32)
        return dot(
            AT[:, :, rows, :].reshape(128, group),
            DB4[:, :, :, col_tile(i)].reshape(group, TILE),
        )

    down_s = Scatter((DSA, DRA, DSB, DRB, DSC, DRC, DK), down_product)
    up_s = Scatter((USA, URA, USB, URB, USC, URC, UK), up_product)
    out_s = Scatter((OSA, ORA, OSB, ORB, OSC, ORC, OK), out_product)
    down_s.first()
    up_s.first()
    out_s.first()

    for flips in others:
        p = at(flips)
        wait(DR.at[p["h"], p["y"]], d_sem[flips], flips)
    for sp in range(2):
        j = s if sp == 0 else 1 - s
        for hp, lp, yp in itertools.product(range(2), repeat=3):
            part = DR[hp, yp, :, (sp * 2 + lp) * tokens : (sp * 2 + lp + 1) * tokens]
            at_tok = (hp * 4 + lp * 2 + yp) * tokens
            DAT[j, :, at_tok : at_tok + tokens] = part
            DA[j, at_tok : at_tok + tokens, :] = part.astype(F32).T.astype(BF16)

    def attend_back(j):
        DKV[...] = jnp.zeros_like(DKV)

        def body(i):
            cols = col_tile(i)
            q = QKVT[j, 0:64, cols] * jnp.asarray(scale, BF16)
            p = jnp.exp(dot(KN[j], q) - LSE[j, 0:1, cols])
            da = DAT[j, :, cols]
            delta = jnp.sum(da.astype(F32) * OT[j, :, cols], axis=0, keepdims=True)
            dp = dot(VN[j], da)
            ds = (p * (dp - delta) * scale).astype(BF16)
            DQT[j, :, cols] = dot(QKVT[j, 64:128, :], ds)
            DKV[0] += dot(ds, QN[j, cols, :])
            DKV[1] += dot(p.astype(BF16), DA[j, cols, :])

        loop(qtiles, body)
        dqt = DQT[j].astype(BF16).astype(F32)
        dq = dqt.T
        dk, dv = DKV[0].astype(BF16).astype(F32), DKV[1].astype(BF16).astype(F32)
        DQKV[j] = jnp.concatenate([dq, dk, dv], axis=1).astype(BF16)
        DQKVT[j, 0:64, :] = dqt.astype(BF16)
        DQKVT[j, 64:128, :] = dk.T.astype(BF16)
        DQKVT[j, 128:192, :] = dv.T.astype(BF16)
        return jnp.sum(dq, axis=0, keepdims=True), jnp.sum(dv, axis=0, keepdims=True)

    q0, v0 = attend_back(0)
    down_s.second()
    q1, v1 = attend_back(1)
    up_s.second()
    out_s.second()
    down_s.third()
    up_s.third()

    def input_tile(j, i):
        w = WH[pl.ds(pl.multiple_of(i * 8, 8), 8)].reshape(TILE, WH.shape[2])[:, 0 : 3 * HEAD_DIM]
        return dot(DQKV[j], w, 1, 1).reshape(2, 2, 2, tokens, TILE)

    ia, ib, ic, id_ = ([ids() for _ in range(tiles)][0] for _ in range(4))

    def in_sent(i):
        return (C4T if i < tiles // 2 else N4T).at[:, :, :, :, pl.ds(i % 2 * TILE, TILE)]

    for i in range(tiles):
        in_sent(i)[...] = input_tile(1, i).astype(BF16)
        send(in_sent(i), IRA.at[i], ia + i, ("s",))

    qa = [ids() for _ in range(tiles)][0]

    def q_first(i):
        cols = col_tile(i)
        v = dot(DQKVT[0], X16[s, :, :, :, :, cols].reshape(length, TILE))
        v += dot(DQKVT[1], X16[1 - s, :, :, :, :, cols].reshape(length, TILE))
        v = v.T.reshape(2, 2, 2, 32, 3 * HEAD_DIM)
        for xp in range(2):
            QK[i, xp] = v[:, :, xp]
        QSA[i, :, :, :, 0 : 3 * HEAD_DIM] = QK[i, 1 - x].astype(BF16)
        copy(QSA.at[i], QRA.at[i], qa + i, ("x",)).start()

    for i in range(tiles):
        dims = ("l", "y") if i < tiles // 2 else ("y", "l")
        wait(IRA.at[i], ia + i, ("s",))
        IK[i] = input_tile(0, i) + IRA[i].astype(F32)
        ISB[i] = (IK[i, :, 1 - l] if dims[0] == "l" else IK[i, :, :, 1 - y]).astype(BF16)
        send(ISB.at[i], IRB.at[i], ib + i, (dims[0],))
    loop(tiles, q_first)
    out_s.third()

    bq, bv = q0 + q1, v0 + v1
    VG[6:8, :] = jnp.zeros((2, width), F32)
    picked = [spread_matrix(width, 32, j) for j in range(4)]

    def exact_pick(row, j):
        a = jnp.where(mine, VG[row : row + 1, :], 0.0)
        hi = a.astype(BF16)
        rest = a - hi.astype(F32)
        mid = rest.astype(BF16)
        low = (rest - mid.astype(F32)).astype(BF16)
        r = picked[j].astype(BF16)
        return dot(hi, r, 1, 1) + dot(mid, r, 1, 1) + dot(low, r, 1, 1)

    SG[...] = jnp.zeros_like(SG)
    SG[:, 0, :] = exact_pick(0, 2) + exact_pick(1, 3)
    SG[:, 1, :] = exact_pick(2, 0) + exact_pick(3, 1) + exact_pick(4, 2) + exact_pick(5, 3)
    for k in range(2):
        b = head * 2 + k
        lanes = slice(k * 32, k * 32 + 32)
        SG[b, 0:1, :] += jnp.concatenate([bq[:, lanes], bv[:, lanes], jnp.zeros((1, 64), F32)], axis=1)
    for hp, yp, xp in itertools.product(range(2), repeat=3):
        r = hp * 4 + yp * 2 + xp
        SG[s * 16 + hp * 8 + l * 4 + yp * 2 + xp, 2:3, :] = UB[1:2, r * 128 : (r + 1) * 128]

    def grad_copy(j):
        b = (me + j) % 32
        return pltpu.make_async_remote_copy(
            src_ref=SG.at[b], dst_ref=RG.at[j], send_sem=hss.at[j], recv_sem=hrs.at[j],
            device_id=peer(j), device_id_type=MESH)

    loop(31, lambda j: grad_copy(j + 1).start())
    RG[0] = SG[me]

    for i in range(tiles):
        dims = ("l", "y") if i < tiles // 2 else ("y", "l")
        wait(IRB.at[i], ib + i, (dims[0],))
        if dims[0] == "l":
            u = IK[i, :, l] + IRB[i].astype(F32)
            IK[i, :, 0] = u
            ISC[i] = IK[i, :, 0, 1 - y].astype(BF16)
        else:
            u = IK[i, :, :, y] + IRB[i].astype(F32)
            IK[i, :, 0] = u
            ISC[i] = IK[i, :, 0, 1 - l].astype(BF16)
        send(ISC.at[i], IRC.at[i], ic + i, (dims[1],))

    def q_second(i):
        wait(QRA.at[i], qa + i, ("x",))
        v = QK[i, x] + QRA[i, :, :, :, 0 : 3 * HEAD_DIM].astype(F32)
        QSB[i // 2, i % 2, :, :, :, 0 : 3 * HEAD_DIM] = v.astype(BF16)

    loop(tiles, q_second)
    for i in range(tiles):
        sends.append(copy(QSA.at[i], QRA.at[i], qa + i, ("x",)))

    def piece_copy(j):
        to = (head + j) % 16
        return pltpu.make_async_remote_copy(
            src_ref=QSB.at[to // 8, (to // 4) % 2, (to // 2) % 2, to % 2], dst_ref=QG.at[head],
            send_sem=hss.at[32 + j], recv_sem=hrs.at[32 + j],
            device_id={"seq": to // 8, "ctx": to % 8, "fsdp": x}, device_id_type=MESH)

    loop(15, lambda j: piece_copy(j + 1).start())
    QG[head] = QSB[s, h, l, y]

    down_s.last(downg_o)
    up_s.last(UF)
    uf_sem = {}
    for flips in (("s",), ("l",), ("s", "l")):
        p = at(flips)
        for hp in range(2):
            uf_sem[flips, hp] = ids()
            send(
                UF.at[pl.ds(pl.multiple_of((p["s"] * 2 + p["l"]) * 32, 32), 32), pl.ds(hp * 512, 512)],
                upg_o.at[:, quarter(s, hp, l)], uf_sem[flips, hp], flips,
            )
    for hp in range(2):
        upg_o[:, quarter(s, hp, l)] = UF[pl.ds(pl.multiple_of((s * 2 + l) * 32, 32), 32), hp * 512 : (hp + 1) * 512]

    for i in range(tiles):
        dims = ("l", "y") if i < tiles // 2 else ("y", "l")
        wait(IRC.at[i], ic + i, (dims[1],))
        mine_at = y if dims[0] == "l" else l
        IK[i, :, 1, 0] = IK[i, :, 0, mine_at] + IRC[i].astype(F32)
        ISD[i] = IK[i, 1 - h, 1, 0].astype(BF16)
        send(ISD.at[i], IRD.at[i], id_ + i, ("h",))
    out_s.last(outg_o)

    loop(31, lambda j: grad_copy(j + 1).wait_recv())
    small_o[...] = jnp.sum(RG[...], axis=0)

    loop(15, lambda j: piece_copy(j + 1).wait_recv())
    for k in range(HEADS // 2):
        a, b = QG[2 * k].astype(F32), QG[2 * k + 1].astype(F32)
        for part in range(3):
            lanes = slice(part * 64, part * 64 + 64)
            to = part * width + k * 128
            qkvg_o[:, to : to + 128] = jnp.concatenate([a[:, lanes], b[:, lanes]], axis=1)

    for i in range(tiles):
        wait(IRD.at[i], id_ + i, ("h",))
        cols = slice(i * TILE, (i + 1) * TILE)
        ig_o[:, cols] = IK[i, h, 1, 0] + IRD[i].astype(F32) + DSUM[:, cols]

    for flips in (("s",), ("l",), ("s", "l")):
        p = at(flips)
        for hp in range(2):
            wait(upg_o.at[:, quarter(p["s"], hp, p["l"])], uf_sem[flips, hp], flips)

    for d in sends:
        d.wait_send()

    def small_sent(j):
        for d in small_copy(j + 1, me):
            d.wait_send()
        grad_copy(j + 1).wait_send()

    loop(31, small_sent)
    loop(15, lambda j: piece_copy(j + 1).wait_send())


def on_block(
    tokens, qkv_weight, out_weight, up_weight, down_weight,
    query_bias, value_bias, out_bias, up_bias, down_bias,
    norm1_gain, norm1_bias, norm2_gain, norm2_bias, cotangent,
):
    n, width = tokens.shape[1], tokens.shape[2]
    hidden = up_weight.shape[1] // 4
    group = 4 * n
    length = 8 * n
    tiles = width // TILE
    small = jnp.concatenate(
        [query_bias, value_bias, out_bias, down_bias, norm1_gain, norm1_bias, norm2_gain, norm2_bias, up_bias]
    ).astype(F32).reshape(3, 128)
    pack = jnp.pad(small, ((0, 5), (0, 0)))

    def b(*shape):
        return pltpu.VMEM(shape, BF16)

    def f(*shape):
        return pltpu.VMEM(shape, F32)

    group_bufs = [b(tiles, 2 * n, TILE), b(tiles, 2 * n, TILE), b(tiles, n, TILE), b(tiles, n, TILE)]

    def scatter_bufs(rows):
        return [
            b(tiles, 2, 2, rows, TILE), b(tiles, 2, 2, rows, TILE),
            b(tiles, 2, rows, TILE), b(tiles, 2, rows, TILE),
            b(tiles, rows, TILE), b(tiles, rows, TILE),
            f(tiles, 2, 2, rows, TILE),
        ]

    sem = pltpu.SemaphoreType.DMA
    scratch = [
        b(2, 2, 2, 2, n, width), b(HEADS, 32, 256), b(32, 32, 256), f(32, 8, 128),
        b(2, 2, 2, 32, width), b(2, 2, 2, 2, 2, 32, hidden), b(2, 2, 2, 128, width),
        b(2, length, 64), b(2, length, 64), b(2, length, 64), b(2, 192, length), f(2, 64, length), b(2, 64, length),
        f(2, 8, length), b(4, 64, group), b(2, 2, 64, group), b(group, 256),
        *group_bufs, *group_bufs, f(tiles, 2, n, TILE),
        b(2, 2, n, width), b(2, 2, 2, 128, group), b(group, hidden), b(2, 2, 2, 128, group), f(group, hidden),
        b(2, 2, n, width),
        f(n, width), f(n, width), f(n, width),
        b(2, 2, 64, group), b(2, 2, 64, group), b(2, length, 64), b(2, 64, length), f(2, length, 64), f(2, 64, length),
        b(2, length, 192), b(2, 192, length),
        *scatter_bufs(128), f(128, width),
        *scatter_bufs(128),
        *scatter_bufs(32),
        b(tiles, 2, 2, 2, n, TILE), b(tiles, 2, 2, n, TILE), b(tiles, 2, 2, n, TILE),
        b(tiles, 2, n, TILE), b(tiles, 2, n, TILE), b(tiles, n, TILE), b(tiles, n, TILE), f(tiles, 2, 2, 2, n, TILE),
        b(tiles, 2, 2, 32, 256), b(tiles, 2, 2, 32, 256), f(tiles, 2, 2, 2, 32, 192), b(2, 2, 2, 2, 32, 256), b(HEADS, 32, 256),
        f(8, width), f(8, hidden), f(8, width), f(32, 8, 128), f(32, 8, 128),
        sem((256,)), sem((256,)), sem((32,)), sem((32,)), sem((32,)), sem((32,)), sem((48,)), sem((48,)),
    ]
    vmem = pl.BlockSpec(memory_space=pltpu.VMEM)
    shapes = [
        jax.ShapeDtypeStruct((n, width), BF16),
        jax.ShapeDtypeStruct((n, width), F32),
        jax.ShapeDtypeStruct((32, 3 * width), F32),
        jax.ShapeDtypeStruct((32, width), F32),
        jax.ShapeDtypeStruct((32, 4 * hidden), F32),
        jax.ShapeDtypeStruct((128, width), F32),
        jax.ShapeDtypeStruct((8, 128), F32),
    ]
    out, ig, qkvg, outg, upg, downg, sm = pl.pallas_call(
        layer_kernel,
        out_shape=shapes,
        in_specs=[vmem] * 7,
        out_specs=[vmem] * 7,
        scratch_shapes=scratch,
        compiler_params=pltpu.CompilerParams(
            collective_id=0, has_side_effects=True, vmem_limit_bytes=63 * 2**20
        ),
        name="layer",
    )(tokens[0], qkv_weight, out_weight, up_weight, down_weight, pack, cotangent[0])
    row0, row1 = sm[0], sm[1]
    return (
        out[None], ig[None], qkvg, outg, upg, downg,
        row0[0:32], row0[32:64], row0[64:96], sm[2], row0[96:128],
        row1[0:32], row1[32:64], row1[64:96], row1[96:128],
    )


def solution(mesh):
    placed = (
        P(("seq", "fsdp"), "ctx", None),
        P(("seq", "ctx", "fsdp"), None),
        P(("seq", "ctx", "fsdp"), None),
        P(("seq", "ctx", "fsdp"), None),
        P(("seq", "ctx", "fsdp"), None),
        P(("seq", "ctx", "fsdp")),
        P(("seq", "ctx", "fsdp")),
        P(("seq", "ctx", "fsdp")),
        P(("seq", "ctx", "fsdp")),
        P(("seq", "ctx", "fsdp")),
        P(("seq", "ctx", "fsdp")),
        P(("seq", "ctx", "fsdp")),
        P(("seq", "ctx", "fsdp")),
        P(("seq", "ctx", "fsdp")),
        P(("seq", "fsdp"), "ctx", None),
    )
    fast = dict(mesh.shape) == {"seq": 2, "ctx": 8, "fsdp": 2}
    return jax.shard_map(
        on_block if fast else on_device,
        mesh=mesh,
        in_specs=placed,
        out_specs=(
            P(("seq", "fsdp"), "ctx", None),
            P(("seq", "fsdp"), "ctx", None),
            P(("seq", "ctx", "fsdp"), None),
            P(("seq", "ctx", "fsdp"), None),
            P(("seq", "ctx", "fsdp"), None),
            P(("seq", "ctx", "fsdp"), None),
            P(("seq", "ctx", "fsdp")),
            P(("seq", "ctx", "fsdp")),
            P(("seq", "ctx", "fsdp")),
            P(("seq", "ctx", "fsdp")),
            P(("seq", "ctx", "fsdp")),
            P(("seq", "ctx", "fsdp")),
            P(("seq", "ctx", "fsdp")),
            P(("seq", "ctx", "fsdp")),
            P(("seq", "ctx", "fsdp")),
        ),
        check_vma=False,
    )
```

```python
import functools
import itertools
import math

import jax
import jax.numpy as jnp
from jax import lax
from jax.experimental import pallas as pl
from jax.experimental.pallas import tpu as pltpu
from jax.sharding import PartitionSpec as P

HEADS = 16
HEAD_DIM = 64


epsilon = 1e-05
MESH = pl.DeviceIdType.MESH
F32 = jnp.float32
BF16 = jnp.bfloat16
TILE = 256


def split_blocks(piece):
    rows = piece.shape[0]
    block = math.gcd(rows, 512)
    return (piece.reshape(rows // block, block, HEADS, HEAD_DIM), block)


def norm_forward(values, gain, shift):
    centered = values - jnp.mean(values, axis=-1, keepdims=True)
    recip = lax.rsqrt(jnp.mean(centered * centered, axis=-1, keepdims=True) + epsilon)
    normal = centered * recip
    return (normal * gain + shift, normal, recip)


def norm_backward(upstream, normal, recip, gain):
    gain_grad = jnp.sum(upstream * normal, axis=0)
    shift_grad = jnp.sum(upstream, axis=0)
    scaled = upstream * gain
    inner = (
        scaled
        - jnp.mean(scaled, axis=-1, keepdims=True)
        - normal * jnp.mean(scaled * normal, axis=-1, keepdims=True)
    )
    return (recip * inner, gain_grad, shift_grad)


def matmul(left_neighbor, right_neighbor):
    return jnp.dot(left_neighbor, right_neighbor, preferred_element_type=jnp.float32)


def on_device(
    tokens,
    qkv_weight,
    out_weight,
    up_weight,
    down_weight,
    query_bias,
    value_bias,
    out_bias,
    up_bias,
    down_bias,
    norm1_gain,
    norm1_bias,
    norm2_gain,
    norm2_bias,
    cotangent,
):
    gathered = (
        lax.all_gather(qkv_weight, ("seq", "ctx", "fsdp"), axis=0, tiled=True),
        lax.all_gather(out_weight, ("seq", "ctx", "fsdp"), axis=0, tiled=True),
        lax.all_gather(up_weight, ("seq", "ctx", "fsdp"), axis=0, tiled=True),
        lax.all_gather(down_weight, ("seq", "ctx", "fsdp"), axis=0, tiled=True),
        lax.all_gather(query_bias, ("seq", "ctx", "fsdp"), axis=0, tiled=True),
        lax.all_gather(value_bias, ("seq", "ctx", "fsdp"), axis=0, tiled=True),
        lax.all_gather(out_bias, ("seq", "ctx", "fsdp"), axis=0, tiled=True),
        lax.all_gather(up_bias, ("seq", "ctx", "fsdp"), axis=0, tiled=True),
        lax.all_gather(down_bias, ("seq", "ctx", "fsdp"), axis=0, tiled=True),
        lax.all_gather(norm1_gain, ("seq", "ctx", "fsdp"), axis=0, tiled=True),
        lax.all_gather(norm1_bias, ("seq", "ctx", "fsdp"), axis=0, tiled=True),
        lax.all_gather(norm2_gain, ("seq", "ctx", "fsdp"), axis=0, tiled=True),
        lax.all_gather(norm2_bias, ("seq", "ctx", "fsdp"), axis=0, tiled=True),
    )
    qkv_full, out_full, up_full, down_full = (gathered[0], gathered[1], gathered[2], gathered[3])
    small = tuple((item.astype(jnp.float32) for item in gathered[4:]))
    q_shift, v_shift, o_shift, u_shift, d_shift, gain_one, shift_one, gain_two, shift_two = small
    scale = HEAD_DIM ** (-0.5)
    inputs = tokens[0]
    rows = inputs.shape[0]
    width = inputs.shape[1]
    joined_bias = jnp.concatenate([q_shift, jnp.zeros_like(q_shift), v_shift])
    qkv_low = (matmul(inputs, qkv_full) + joined_bias).astype(jnp.bfloat16)
    queries = qkv_low[:, :width].reshape(rows, HEADS, HEAD_DIM)
    keys_own = qkv_low[:, width : 2 * width]
    values_own = qkv_low[:, 2 * width :]
    start_state = (
        jnp.full((HEADS, rows), -1e30, jnp.float32),
        jnp.zeros((HEADS, rows), jnp.float32),
        jnp.zeros((rows, HEADS, HEAD_DIM), jnp.float32),
    )
    piece = (
        lax.all_gather(keys_own, "ctx", axis=0, tiled=True),
        lax.all_gather(values_own, "ctx", axis=0, tiled=True),
    )
    key_blocks, block = split_blocks(piece[0])
    value_blocks, block = split_blocks(piece[1])

    def inner(state, pair):
        run_max, run_sum, accum = state
        key_tile_rows, value_block = pair
        scores = (
            jnp.einsum("qhe,khe->hqk", queries, key_tile_rows, preferred_element_type=jnp.float32)
            * scale
        )
        new_max = jnp.maximum(run_max, jnp.max(scores, axis=-1))
        factor = jnp.exp(run_max - new_max)
        weights = jnp.exp(scores - new_max[..., None])
        run_sum = run_sum * factor + jnp.sum(weights, axis=-1)
        accum = accum * factor.T[..., None] + jnp.einsum(
            "hqk,khe->qhe",
            weights.astype(jnp.bfloat16),
            value_block,
            preferred_element_type=jnp.float32,
        )
        return ((new_max, run_sum, accum), None)

    result, unused = lax.scan(inner, start_state, (key_blocks, value_blocks))
    run_max, run_sum, accum = result
    attended = accum / run_sum.T[..., None]
    log_total = run_max + jnp.log(run_sum)
    attended_low = attended.reshape(rows, width).astype(jnp.bfloat16)
    first_sum = inputs.astype(jnp.float32) + matmul(attended_low, out_full) + o_shift
    first_norm, normal_one, recip_one = norm_forward(first_sum, gain_one, shift_one)
    normed_low = first_norm.astype(jnp.bfloat16)
    hidden_pre = matmul(normed_low, up_full) + u_shift
    activated_full, gelu_pull = jax.vjp(lambda pre: jax.nn.gelu(pre, approximate=False), hidden_pre)
    activated = activated_full.astype(jnp.bfloat16)
    second_sum = first_norm + matmul(activated, down_full) + d_shift
    final, normal_two, recip_two = norm_forward(second_sum, gain_two, shift_two)
    upstream = cotangent[0].astype(jnp.float32)
    d_second, gain_two_grad, shift_two_grad = norm_backward(
        upstream, normal_two, recip_two, gain_two
    )
    d_feed = d_second.astype(jnp.bfloat16)
    down_grad = matmul(activated.T, d_feed)
    down_bias_grad = jnp.sum(d_feed.astype(jnp.float32), axis=0)
    d_hidden = gelu_pull(matmul(d_feed, down_full.T))[0].astype(jnp.bfloat16)
    up_grad = matmul(normed_low.T, d_hidden)
    up_bias_grad = jnp.sum(d_hidden.astype(jnp.float32), axis=0)
    first_input_gradient = d_second + matmul(d_hidden, up_full.T)
    d_sum_one, gain_one_grad, first_shift_gradient = norm_backward(
        first_input_gradient, normal_one, recip_one, gain_one
    )
    d_branch = d_sum_one.astype(jnp.bfloat16)
    out_grad = matmul(attended_low.T, d_branch)
    out_bias_grad = jnp.sum(d_branch.astype(jnp.float32), axis=0)
    d_attended = matmul(d_branch, out_full.T).astype(jnp.bfloat16).reshape(rows, HEADS, HEAD_DIM)
    delta = jnp.sum(d_attended.astype(jnp.float32) * attended, axis=-1).T
    total_rows = rows * lax.axis_size("ctx")
    zero_query = jnp.zeros((rows, HEADS, HEAD_DIM), jnp.float32)
    start_back = (zero_query, jnp.zeros((total_rows, 2 * width), jnp.float32))
    piece = (
        lax.all_gather(keys_own, "ctx", axis=0, tiled=True),
        lax.all_gather(values_own, "ctx", axis=0, tiled=True),
    )
    key_blocks, block = split_blocks(piece[0])
    value_blocks, block = split_blocks(piece[1])
    counter = jnp.arange(key_blocks.shape[0], dtype=jnp.int32)

    def inner(state, triple):
        key_tile_rows, value_block, number = triple
        scores = (
            jnp.einsum("qhe,khe->hqk", queries, key_tile_rows, preferred_element_type=jnp.float32)
            * scale
        )
        weights = jnp.exp(scores - log_total[..., None])
        d_probs = jnp.einsum(
            "qhe,khe->hqk", d_attended, value_block, preferred_element_type=jnp.float32
        )
        d_scores = (weights * (d_probs - delta[..., None]) * scale).astype(jnp.bfloat16)
        d_query = state[0] + jnp.einsum(
            "hqk,khe->qhe", d_scores, key_tile_rows, preferred_element_type=jnp.float32
        )
        d_key = jnp.einsum(
            "hqk,qhe->khe", d_scores, queries, preferred_element_type=jnp.float32
        ).reshape(block, width)
        d_value = jnp.einsum(
            "hqk,qhe->khe",
            weights.astype(jnp.bfloat16),
            d_attended,
            preferred_element_type=jnp.float32,
        ).reshape(block, width)
        offset = number * block
        current = lax.dynamic_slice_in_dim(state[1], offset, block, 0)
        updated = lax.dynamic_update_slice_in_dim(
            state[1], current + jnp.concatenate([d_key, d_value], axis=1), offset, 0
        )
        return ((d_query, updated), None)

    result, unused = lax.scan(inner, start_back, (key_blocks, value_blocks, counter))
    d_query = result[0].reshape(rows, width)
    summed = lax.psum_scatter(result[1], "ctx", scatter_dimension=0, tiled=True)
    d_key = summed[:, :width]
    d_value = summed[:, width:]
    d_qkv = jnp.concatenate([d_query, d_key, d_value], axis=1).astype(jnp.bfloat16)
    qkv_grad = matmul(inputs.T, d_qkv)
    d_qkv_wide = d_qkv.astype(jnp.float32)
    query_bias_gradient = jnp.sum(d_qkv_wide[:, :width], axis=0)
    value_bias_grad = jnp.sum(d_qkv_wide[:, 2 * width :], axis=0)
    input_grad = matmul(d_qkv, qkv_full.T) + d_sum_one
    sharded = (
        lax.psum_scatter(qkv_grad, ("seq", "ctx", "fsdp"), scatter_dimension=0, tiled=True),
        lax.psum_scatter(out_grad, ("seq", "ctx", "fsdp"), scatter_dimension=0, tiled=True),
        lax.psum_scatter(up_grad, ("seq", "ctx", "fsdp"), scatter_dimension=0, tiled=True),
        lax.psum_scatter(down_grad, ("seq", "ctx", "fsdp"), scatter_dimension=0, tiled=True),
        lax.psum_scatter(
            query_bias_gradient, ("seq", "ctx", "fsdp"), scatter_dimension=0, tiled=True
        ),
        lax.psum_scatter(value_bias_grad, ("seq", "ctx", "fsdp"), scatter_dimension=0, tiled=True),
        lax.psum_scatter(out_bias_grad, ("seq", "ctx", "fsdp"), scatter_dimension=0, tiled=True),
        lax.psum_scatter(up_bias_grad, ("seq", "ctx", "fsdp"), scatter_dimension=0, tiled=True),
        lax.psum_scatter(down_bias_grad, ("seq", "ctx", "fsdp"), scatter_dimension=0, tiled=True),
        lax.psum_scatter(gain_one_grad, ("seq", "ctx", "fsdp"), scatter_dimension=0, tiled=True),
        lax.psum_scatter(
            first_shift_gradient, ("seq", "ctx", "fsdp"), scatter_dimension=0, tiled=True
        ),
        lax.psum_scatter(gain_two_grad, ("seq", "ctx", "fsdp"), scatter_dimension=0, tiled=True),
        lax.psum_scatter(shift_two_grad, ("seq", "ctx", "fsdp"), scatter_dimension=0, tiled=True),
    )
    return (
        final.astype(jnp.bfloat16)[None],
        input_grad[None],
        sharded[0],
        sharded[1],
        sharded[2],
        sharded[3],
        sharded[4],
        sharded[5],
        sharded[6],
        sharded[7],
        sharded[8],
        sharded[9],
        sharded[10],
        sharded[11],
        sharded[12],
    )


def dot(left, right, left_dim=1, right_dim=0):
    return lax.dot_general(
        left, right, (((left_dim,), (right_dim,)), ((), ())), preferred_element_type=F32
    )


def loop(count, body):
    def step(i, carry):
        body(i)
        return carry

    lax.fori_loop(0, count, step, 0)


def spread_matrix(width, piece, at):
    lane = lax.broadcasted_iota(jnp.int32, (128, width), 0)
    column = lax.broadcasted_iota(jnp.int32, (128, width), 1)
    return jnp.where(lane == at * piece + column % piece, 1.0, 0.0)


def own_columns(blocks, width):
    row = lax.broadcasted_iota(jnp.int32, (blocks, width), 0)
    column = lax.broadcasted_iota(jnp.int32, (blocks, width), 1)
    return column // (width // blocks), row


def layer_kernel(
    tok, qkvw, outw, upw, downw, qb, vb, ob, ub, db, g1, b1, g2, b2, cot,
    out_o, ig_o, qkvg_o, outg_o, upg_o, downg_o, small_o,
    PK, X16, WP, WH, G, OW, UW, DW,
    QN, KN, VN, QKVT, OT, OTB, LSE, AS, AT, A4,
    R1A, R1B, R1C, R1D, R2A, R2B, R2C, R2D, KR,
    N4, N4T, C4, C4T, GP, DF4,
    FN, NORM1, DSEC,
    DS, DR, DA, DAT, DKV, DQT, DQKV, DQKVT,
    USA, URA, USB, URB, USC, URC, UK, UF,
    DSA, DRA, DSB, DRB, DSC, DRC, DK,
    OSA, ORA, OSB, ORB, OSC, ORC, OK,
    IRA, ISB, IRB, ISC, IRC, ISD, IRD, IK,
    QSA, QRA, QK, QSB, QG,
    VEC, UB, VG, SG, RG, SX, RX,
    ssem, rsem, wss, wrs, gss, grs, hss, hrs,
):
    s = lax.axis_index("seq")
    c = lax.axis_index("ctx")
    x = lax.axis_index("fsdp")
    h, l, y = c // 4, (c // 2) % 2, c % 2
    here = {"s": s, "h": h, "l": l, "y": y, "x": x}
    me = s * 16 + c * 2 + x
    head = s * 8 + c
    width = tok.shape[1]
    tiles = width // TILE
    counter = itertools.count()
    sends = []

    def at(flips):
        return {k: (1 - v if k in flips else v) for k, v in here.items()}

    def device(flips):
        p = at(flips)
        return {"seq": p["s"], "ctx": p["h"] * 4 + p["l"] * 2 + p["y"], "fsdp": p["x"]}

    def ids(n=1):
        return [next(counter) for _ in range(n)][0]

    def copy(src, dst, sem, flips):
        return pltpu.make_async_remote_copy(
            src_ref=src, dst_ref=dst, send_sem=ssem.at[sem], recv_sem=rsem.at[sem],
            device_id=device(flips), device_id_type=MESH,
        )

    def settle(since):
        for d in sends[since:]:
            d.wait_send()
        del sends[since:]

    def send(src, dst, sem, flips):
        d = copy(src, dst, sem, flips)
        d.start()
        sends.append(d)

    def wait(ref, sem, flips):
        copy(ref, ref, sem, flips).wait_recv()

    class Tiles:
        def __init__(self, src, dst, dim, of):
            self.src, self.dst, self.dim, self.of = src, dst, dim, of
            self.base = [ids() for _ in of][0] - of[0]
            self.listed = False

        def each(self, i):
            return copy(self.src.at[i], self.dst.at[i], self.base + i, (self.dim,))

        def send(self, i):
            self.each(i).start()
            if not self.listed:
                sends.append(self)
                self.listed = True

        def wait(self, i):
            self.each(i).wait_recv()

        def wait_send(self):
            for i in self.of:
                self.each(i).wait_send()

    class Gather:
        def __init__(self, order, block):
            self.order, self.block, self.sem = order, block, {}
            for n in range(1, len(order) + 1):
                for k in itertools.combinations(order, n):
                    self.sem[frozenset(k)] = ids()

        def push(self, *have, along=None):
            have = frozenset(have)
            last = max([self.order.index(d) for d in have], default=-1)
            for d in self.order[last + 1 :]:
                if along and d not in along:
                    continue
                ref = self.block(at(have))
                send(ref, ref, self.sem[have | {d}], (d,))

        def pull(self, *have):
            have = frozenset(have)
            last = max(have, key=self.order.index)
            wait(self.block(at(have)), self.sem[have], (last,))

        def pass_on(self, *have):
            self.pull(*have)
            self.push(*have)

    barrier = pltpu.get_barrier_semaphore()

    def peer(j):
        to = (head + j) % 16
        return {"seq": to // 8, "ctx": to % 8, "fsdp": x}

    def peer_copy(src, dst, sems, j):
        return pltpu.make_async_remote_copy(
            src_ref=src, dst_ref=dst, send_sem=sems[0].at[j], recv_sem=sems[1].at[j],
            device_id=peer(j % 16), device_id_type=MESH)

    loop(15, lambda j: pl.semaphore_signal(barrier, inc=1, device_id=peer(j + 1), device_id_type=MESH))
    pl.semaphore_signal(barrier, inc=1, device_id=device("x"), device_id_type=MESH)

    X16[s, h, l, y] = tok[...]
    PK[...] = jnp.zeros_like(PK)
    for k, vector in enumerate((qb, vb, ob, db, g1, b1, g2, b2)):
        PK[k // 4, k % 4 * 32 : k % 4 * 32 + 32] = vector[0, :].astype(F32)
    PK[2, :] = ub[0, :].astype(F32)
    for k in range(HEADS):
        parts = [qkvw[:, j * width + k * HEAD_DIM : j * width + (k + 1) * HEAD_DIM] for j in range(3)]
        WP[k, :, 0 : 3 * HEAD_DIM] = jnp.concatenate(parts, axis=1)
    WH[head, x] = WP[head]
    G[head, x] = PK[...]
    OW[h, y, x] = outw[...]
    DW[h, y, x] = downw[...]

    def quarter(sp, hp, lp):
        return pl.ds(pl.multiple_of(sp * 2048 + hp * 1024 + lp * 512, 512), 512)

    for hp in range(2):
        UW[s, h, l, y, x, :, hp * 512 : (hp + 1) * 512] = upw[:, quarter(s, hp, l)]

    pl.semaphore_wait(barrier, 16)

    half = width // 2

    def token_block(k):
        return lambda p: X16.at[p["s"], p["h"], p["l"], p["y"], :, pl.ds(k * half, half)]

    xg = [Gather("hlys", token_block(k)) for k in range(2)]
    for g in xg:
        g.push()

    def small_copy(j, dst):
        return [
            peer_copy(WP.at[(head + j) % 16], WH.at[dst, x], (wss, wrs), j),
            peer_copy(PK, G.at[dst, x], (gss, grs), j),
        ]

    loop(15, lambda j: [d.start() for d in small_copy(j + 1, head)])

    up_sem = {}
    for flips in (("s",), ("l",), ("s", "l")):
        p = at(flips)
        for hp in range(2):
            up_sem[flips, hp] = ids()
            send(
                upw.at[:, quarter(p["s"], hp, p["l"])],
                UW.at[s, h, l, y, x, :, pl.ds(hp * 512, 512)],
                up_sem[flips, hp], flips,
            )

    def up_block(k):
        cols = pl.ds(k * (UW.shape[-1] // 2), UW.shape[-1] // 2)
        return lambda p: UW.at[:, p["h"], :, p["y"], p["x"], :, cols]

    def down_block(k):
        rows = pl.ds(k * (DW.shape[-2] // 2), DW.shape[-2] // 2)
        return lambda p: DW.at[p["h"], p["y"], p["x"], rows]

    og = Gather("hyx", lambda p: OW.at[p["h"], p["y"], p["x"]])
    ug = [Gather("hyx", up_block(0)), Gather("hxy", up_block(1))]
    dg = [Gather("hyx", down_block(0)), Gather("hxy", down_block(1))]
    for g in dg:
        g.push(along="x")
    og.push()

    for g in xg:
        g.pass_on("h")
    for flips in (("s",), ("l",), ("s", "l")):
        p = at(flips)
        for hp in range(2):
            wait(UW.at[p["s"], h, p["l"], y, x, :, pl.ds(hp * 512, 512)], up_sem[flips, hp], flips)
    for g in ug:
        g.push()
    for g in xg:
        g.pass_on("l")

    def wait_small(j):
        for d in small_copy(j + 1, (head + 15 - j) % 16):
            d.wait_recv()

    loop(15, wait_small)
    small_sem = [ids(), ids()]
    send(WH.at[:, x], WH.at[:, x], small_sem[0], ("x",))
    send(G.at[:, x], G.at[:, x], small_sem[1], ("x",))
    for g in xg:
        g.pass_on("h", "l")
    for g in dg:
        g.push(along="hy")
    og.pass_on("h")
    og.pass_on("y")
    og.pass_on("h", "y")
    for have in (("y",), ("l", "y"), ("h", "y"), ("h", "l", "y")):
        for g in xg:
            g.pass_on(*have)
    for g in ug:
        g.pass_on("h")
    ug[0].pass_on("y")
    ug[1].pass_on("x")

    wait(WH.at[:, 1 - x], small_sem[0], ("x",))
    wait(G.at[:, 1 - x], small_sem[1], ("x",))

    spread = [spread_matrix(width, 32, j).astype(BF16) for j in range(4)]
    block_of, row_at = own_columns(32, width)
    mine = block_of == row_at
    arrived = block_of == row_at % 16 * 2 + row_at // 16
    for row, j, to in ((0, 2, 0), (0, 3, 1), (1, 0, 2), (1, 1, 3), (1, 2, 4), (1, 3, 5)):
        rows = jnp.concatenate([G[:, 0, row, :], G[:, 1, row, :]], axis=0).astype(BF16)
        VEC[to : to + 1, :] = jnp.sum(jnp.where(arrived, dot(rows, spread[j]), 0.0), axis=0, keepdims=True)
    for hp, yp, xp in itertools.product(range(2), repeat=3):
        r = hp * 4 + yp * 2 + xp
        UB[0:1, r * 128 : (r + 1) * 128] = G[s * 8 + hp * 4 + l * 2 + yp, xp, 2:3, :]
    out_bias, down_bias = VEC[0:1, :], VEC[1:2, :]
    gain_one, shift_one, gain_two, shift_two = (VEC[k : k + 1, :] for k in range(2, 6))
    first, second = G[head, 0, 0:1, :], G[head, 1, 0:1, :]
    head_bias = jnp.concatenate(
        [first[:, 0:32], second[:, 0:32], jnp.zeros((1, 64), F32), first[:, 32:64], second[:, 32:64]], axis=1
    )
    head_weight = WH[...].reshape(width, WH.shape[-1])[:, 0 : 3 * HEAD_DIM]

    length = 8 * tok.shape[0]
    qtiles = length // TILE
    scale = HEAD_DIM ** (-0.5)
    DH4, DB4, DSUM = C4, N4, FN

    def project(j):
        sp = s if j == 0 else 1 - s

        def body(i):
            hl = X16[sp, i // 2, i % 2].reshape(TILE, width)
            res = (dot(hl, head_weight) + head_bias).astype(BF16).astype(F32)
            rows = pl.ds(pl.multiple_of(i * TILE, TILE), TILE)
            QN[j, rows, :] = res[:, 0:64].astype(BF16)
            KN[j, rows, :] = res[:, 64:128].astype(BF16)
            VN[j, rows, :] = res[:, 128:192].astype(BF16)
            QKVT[j, :, rows] = res.T.astype(BF16)

        loop(qtiles, body)

    def attend(j):
        def body(i):
            cols = pl.ds(pl.multiple_of(i * TILE, TILE), TILE)
            q = QKVT[j, 0:64, cols] * jnp.asarray(scale, BF16)
            st = dot(KN[j], q)
            top = jnp.max(st, axis=0, keepdims=True)
            e = jnp.exp(st - top)
            total = jnp.sum(e, axis=0, keepdims=True)
            o = dot(QKVT[j, 128:192, :], e.astype(BF16)) / total
            OT[j, :, cols] = o
            OTB[j, :, cols] = o.astype(BF16)
            LSE[j, 0:1, cols] = top + jnp.log(total)

        loop(qtiles, body)

    tokens = tok.shape[0]

    def tok_cols(hp, lp, yp):
        return pl.ds(pl.multiple_of((hp * 4 + lp * 2 + yp) * tokens, tokens), tokens)

    others = (("h",), ("y",), ("h", "y"))
    a_sem = {(f, j): ids() for f in others for j in range(2)}

    def seq_cols(j):
        sp = s if j == 0 else 1 - s
        return pl.ds(pl.multiple_of(sp * 2 * tokens, 2 * tokens), 2 * tokens)

    def hand_out(j):
        for k, flips in enumerate(((),) + others):
            p = at(flips)
            piece = jnp.concatenate([OTB[j, :, tok_cols(p["h"], lp, p["y"])] for lp in range(2)], axis=1)
            if flips:
                AS[k, j] = piece
                send(AS.at[k, j], AT.at[h, y, :, seq_cols(j)], a_sem[flips, j], flips)
            else:
                AT[h, y, :, seq_cols(j)] = piece

    project(0)
    attend(0)
    hand_out(0)
    ug[0].pass_on("h", "y")
    ug[1].pass_on("h", "x")
    for have in (("s",), ("h", "s"), ("l", "s"), ("h", "l", "s"), ("y", "s"), ("h", "y", "s"), ("l", "y", "s"), ("h", "l", "y", "s")):
        for g in xg:
            g.pull(*have)
    project(1)
    attend(1)
    hand_out(1)
    for g in dg:
        g.pass_on("h")
    dg[0].pass_on("y")
    dg[1].pass_on("x")
    dg[0].pass_on("h", "y")
    dg[1].pass_on("h", "x")
    for have in (("x",), ("h", "x"), ("y", "x"), ("h", "y", "x")):
        og.pull(*have)
    for flips in others:
        p = at(flips)
        for j in range(2):
            wait(AT.at[p["h"], p["y"], :, seq_cols(j)], a_sem[flips, j], flips)

    group = 4 * tokens
    A4[...] = AT[...].reshape(4 * HEAD_DIM, group).astype(F32).T.astype(BF16)

    def group_sum(bufs, tile_fn, meanwhile=None):
        sa, ra, sb, rb = bufs
        to_core, to_pair = Tiles(sa, ra, "s", range(tiles)), Tiles(sb, rb, "l", range(tiles))

        def a(i):
            sa[i] = tile_fn(1 - s, i).astype(BF16)
            to_core.send(i)

        loop(tiles, a)

        def b(i):
            v = tile_fn(s, i)
            to_core.wait(i)
            KR[i] = (v + ra[i].astype(F32)).reshape(2, tokens, TILE)
            sb[i] = KR[i, 1 - l].astype(BF16)
            to_pair.send(i)

        loop(tiles, b)
        if meanwhile is not None:
            meanwhile()
        for i in range(tiles):
            to_pair.wait(i)
        return jnp.concatenate([KR[i, l] + rb[i].astype(F32) for i in range(tiles)], axis=1)

    def group_rows(sp):
        return pl.ds(pl.multiple_of(sp * 2 * tokens, 2 * tokens), 2 * tokens)

    def col_tile(i):
        return pl.ds(pl.multiple_of(i * TILE, TILE), TILE)

    mark = len(sends)
    branch = group_sum(
        (R1A, R1B, R1C, R1D),
        lambda sp, i: dot(A4[group_rows(sp), :], OW[:, :, :, :, col_tile(i)].reshape(4 * HEAD_DIM, TILE)),
    )

    def norm_forward(values, gain, shift):
        centered = values - jnp.mean(values, axis=-1, keepdims=True)
        recip = lax.rsqrt(jnp.mean(centered * centered, axis=-1, keepdims=True) + epsilon)
        normal = centered * recip
        return normal * gain + shift, normal, recip

    def norm_backward(upstream, normal, recip, gain):
        gain_grad = jnp.sum(upstream * normal, axis=0, keepdims=True)
        shift_grad = jnp.sum(upstream, axis=0, keepdims=True)
        scaled = upstream * gain
        inner = (
            scaled
            - jnp.mean(scaled, axis=-1, keepdims=True)
            - normal * jnp.mean(scaled * normal, axis=-1, keepdims=True)
        )
        return recip * inner, gain_grad, shift_grad

    first_norm, normal_one, recip_one = norm_forward(
        tok[...].astype(F32) + branch + out_bias, gain_one, shift_one
    )
    FN[...] = first_norm
    NORM1[...] = normal_one

    def group_gather(ref, value, meanwhile=None):
        g = Gather("ls", lambda p: ref.at[p["s"], p["l"]])
        ref[s, l] = value
        g.push()
        if meanwhile is not None:
            meanwhile()
        g.pass_on("l")
        g.pull("s")
        g.pull("l", "s")

    group_gather(N4, first_norm.astype(BF16))
    settle(mark)

    def pull_rest(pair):
        for have in (("x",), ("h", "x"), ("y", "x"), ("h", "y", "x")):
            pair[0].pull(*have)
        for have in (("y",), ("h", "y"), ("x", "y"), ("h", "x", "y")):
            pair[1].pull(*have)

    pull_rest(ug)
    hidden = UB.shape[1]

    def all_rows(ref):
        return ref[...].reshape(group, ref.shape[-1])

    def up(i):
        cols = col_tile(i)
        w = UW[:, :, :, :, :, :, cols].reshape(width, TILE)
        pre = dot(all_rows(N4), w) + UB[0:1, cols]
        phi = 0.5 * (1.0 + lax.erf(pre * (2.0 ** -0.5)))
        act = pre * phi
        GP[:, cols] = phi + pre * (jnp.exp(-0.5 * pre * pre) * ((2.0 * math.pi) ** -0.5))
        C4[:, cols] = act.astype(BF16)

    loop(hidden // TILE, up)
    pull_rest(dg)
    feed = group_sum(
        (R2A, R2B, R2C, R2D),
        lambda sp, i: dot(C4[group_rows(sp), :], DW[:, :, :, :, col_tile(i)].reshape(hidden, TILE)),
    )
    final, normal_two, recip_two = norm_forward(FN[...] + feed + down_bias, gain_two, shift_two)
    out_o[...] = final.astype(BF16)
    d_second, gain_two_grad, shift_two_grad = norm_backward(
        cot[...].astype(F32), normal_two, recip_two, gain_two
    )
    DSEC[...] = d_second
    d_feed = d_second.astype(BF16)
    VG[1:2, :] = jnp.sum(d_feed.astype(F32), axis=0, keepdims=True)
    VG[4:5, :] = gain_two_grad
    VG[5:6, :] = shift_two_grad

    def transpose_rows(i):
        cols = pl.ds(pl.multiple_of(i * 128, 128), 128)
        t = N4[:, :, :, cols].reshape(group, 128)
        t = t.astype(F32).T.astype(BF16).reshape(2, 2, 32, group)
        for yp, xp in itertools.product(range(2), repeat=2):
            to = pl.ds(pl.multiple_of((i // 4 * 2 + i % 2) * 32, 32), 32)
            N4T[(i // 2) % 2, yp, xp, to, :] = t[yp, xp]
        C4T[i // 4, (i // 2) % 2, i % 2] = C4[:, cols].astype(F32).T.astype(BF16)

    group_gather(DF4, d_feed, lambda: loop(8, transpose_rows))

    def d_hidden(i):
        rows = DW[i // 2, i % 2].reshape(TILE, width)
        cols = col_tile(i)
        v = (dot(all_rows(DF4), rows, 1, 1) * GP[:, cols]).astype(BF16)
        DH4[:, cols] = v
        UB[1:2, cols] = jnp.sum(v.astype(F32), axis=0, keepdims=True)

    class Scatter:
        def __init__(self, bufs, product):
            self.sa, self.ra, self.sb, self.rb, self.sc, self.rc, self.keep = bufs
            self.product = product
            self.shape = self.sa.shape[1:]
            self.parts = []
            for k, (one, two) in enumerate((("x", "y"), ("y", "x"))):
                of = range(k * tiles // 2, (k + 1) * tiles // 2)
                self.parts.append((
                    one, two, of,
                    Tiles(self.sa, self.ra, one, of), Tiles(self.sb, self.rb, two, of), Tiles(self.sc, self.rc, "h", of),
                ))

        def first(self):
            for one, two, of, a, b, c in self.parts:
                def body(i, one=one, of=of, a=a):
                    i = of[0] + i
                    self.sa[i] = self.product(one, 1 - here[one], i).reshape(self.shape).astype(BF16)
                    a.send(i)

                loop(len(of), body)

        def second(self):
            for one, two, of, a, b, c in self.parts:
                def body(i, one=one, two=two, of=of, a=a, b=b):
                    i = of[0] + i
                    v = self.product(one, here[one], i).reshape(self.shape)
                    a.wait(i)
                    self.keep[i] = v + self.ra[i].astype(F32)
                    self.sb[i] = self.keep[i, :, 1 - here[two]].astype(BF16)
                    b.send(i)

                loop(len(of), body)

        def third(self):
            for one, two, of, a, b, c in self.parts:
                def body(i, two=two, of=of, b=b, c=c):
                    i = of[0] + i
                    b.wait(i)
                    self.keep[i, :, 0] = self.keep[i, :, here[two]] + self.rb[i].astype(F32)
                    self.sc[i] = self.keep[i, 1 - h, 0].astype(BF16)
                    c.send(i)

                loop(len(of), body)

        def last(self, out):
            for one, two, of, a, b, c in self.parts:
                def body(i, of=of, c=c):
                    i = of[0] + i
                    c.wait(i)
                    out[:, col_tile(i)] = self.keep[i, h, 0] + self.rc[i].astype(F32)

                loop(len(of), body)

    def up_product(dim, v, i):
        rows = N4T[:, :, v] if dim == "x" else N4T[:, v]
        return dot(rows.reshape(group, group), DH4[:, col_tile(i)])

    def down_product(dim, v, i):
        rows = C4T[:, :, v] if dim == "x" else C4T[:, v]
        return dot(rows.reshape(group, group), DF4[:, :, :, col_tile(i)].reshape(group, TILE))

    def out_product(dim, v, i):
        rows = AT[:, :, pl.ds(pl.multiple_of(v * 32, 32), 32), :] if dim == "x" else AT[:, v]
        return dot(rows.reshape(128, group), DB4[:, :, :, col_tile(i)].reshape(group, TILE))

    down_s = Scatter((DSA, DRA, DSB, DRB, DSC, DRC, DK), down_product)
    up_s = Scatter((USA, URA, USB, URB, USC, URC, UK), up_product)
    out_s = Scatter((OSA, ORA, OSB, ORB, OSC, ORC, OK), out_product)

    loop(hidden // TILE, d_hidden)

    def up_rows(i):
        return UW[i // 2, i % 2].reshape(TILE, hidden)

    d_first = group_sum(
        (R1A, R1B, R1C, R1D), lambda sp, i: dot(DH4[group_rows(sp), :], up_rows(i), 1, 1), down_s.first
    )
    d_sum_one, gain_one_grad, shift_one_grad = norm_backward(
        DSEC[...] + d_first, NORM1[...], recip_one, gain_one
    )
    DSUM[...] = d_sum_one
    d_branch = d_sum_one.astype(BF16)
    VG[0:1, :] = jnp.sum(d_branch.astype(F32), axis=0, keepdims=True)
    VG[2:3, :] = gain_one_grad
    VG[3:4, :] = shift_one_grad
    group_gather(DB4, d_branch, up_s.first)

    d_att = dot(all_rows(DB4), OW[...].reshape(4 * HEAD_DIM, width), 1, 1).astype(BF16)
    d_att = d_att.astype(F32).T.astype(BF16).reshape(2, 2, HEAD_DIM, group)
    DS[...] = d_att
    d_sem = {f: ids() for f in others}
    for flips in others:
        p = at(flips)
        send(DS.at[p["h"], p["y"]], DR.at[h, y], d_sem[flips], flips)
    DR[h, y] = DS[h, y]

    out_s.first()
    down_s.second()

    for flips in others:
        p = at(flips)
        wait(DR.at[p["h"], p["y"]], d_sem[flips], flips)
    for sp in range(2):
        j = s if sp == 0 else 1 - s
        for hp, lp, yp in itertools.product(range(2), repeat=3):
            part = DR[hp, yp, :, (sp * 2 + lp) * tokens : (sp * 2 + lp + 1) * tokens]
            at_tok = (hp * 4 + lp * 2 + yp) * tokens
            DAT[j, :, at_tok : at_tok + tokens] = part
            DA[j, at_tok : at_tok + tokens, :] = part.astype(F32).T.astype(BF16)

    def attend_back(j):
        DKV[...] = jnp.zeros_like(DKV)

        def body(i):
            cols = col_tile(i)
            q = QKVT[j, 0:64, cols] * jnp.asarray(scale, BF16)
            p = jnp.exp(dot(KN[j], q) - LSE[j, 0:1, cols])
            da = DAT[j, :, cols]
            delta = jnp.sum(da.astype(F32) * OT[j, :, cols], axis=0, keepdims=True)
            dp = dot(VN[j], da)
            ds = (p * (dp - delta) * scale).astype(BF16)
            DQT[j, :, cols] = dot(QKVT[j, 64:128, :], ds)
            DKV[0] += dot(ds, QN[j, cols, :])
            DKV[1] += dot(p.astype(BF16), DA[j, cols, :])

        loop(qtiles, body)
        dqt = DQT[j].astype(BF16).astype(F32)
        dq = dqt.T
        dk, dv = DKV[0].astype(BF16).astype(F32), DKV[1].astype(BF16).astype(F32)
        DQKV[j] = jnp.concatenate([dq, dk, dv], axis=1).astype(BF16)
        DQKVT[j, 0:64, :] = dqt.astype(BF16)
        DQKVT[j, 64:128, :] = dk.T.astype(BF16)
        DQKVT[j, 128:192, :] = dv.T.astype(BF16)
        return jnp.sum(dq, axis=0, keepdims=True), jnp.sum(dv, axis=0, keepdims=True)

    def input_tile(j, i):
        w = WH[pl.ds(pl.multiple_of(i * 4, 4), 4)].reshape(TILE, WH.shape[-1])[:, 0 : 3 * HEAD_DIM]
        return dot(DQKV[j], w, 1, 1).reshape(2, 2, 2, tokens, TILE)

    ia, ib, ic, id_ = ([ids() for _ in range(tiles)][0] for _ in range(4))

    def in_sent(i):
        return (C4T if i < tiles // 2 else N4T).at[:, :, :, :, pl.ds(i % 2 * TILE, TILE)]

    q1, v1 = attend_back(1)
    up_s.second()
    for i in range(tiles):
        in_sent(i)[...] = input_tile(1, i).astype(BF16)
        send(in_sent(i), IRA.at[i], ia + i, ("s",))
    q0, v0 = attend_back(0)
    out_s.second()

    to_x = Tiles(QSA, QRA, "x", range(tiles))

    def q_first(i):
        cols = col_tile(i)
        v = dot(DQKVT[0], X16[s, :, :, :, :, cols].reshape(length, TILE))
        v += dot(DQKVT[1], X16[1 - s, :, :, :, :, cols].reshape(length, TILE))
        v = v.T.reshape(2, 2, 2, 32, 3 * HEAD_DIM)
        for xp in range(2):
            QK[i, xp] = v[:, :, xp]
        QSA[i, :, :, :, 0 : 3 * HEAD_DIM] = QK[i, 1 - x].astype(BF16)
        to_x.send(i)

    for i in range(tiles):
        dims = ("l", "y") if i < tiles // 2 else ("y", "l")
        wait(IRA.at[i], ia + i, ("s",))
        IK[i] = input_tile(0, i) + IRA[i].astype(F32)
        ISB[i] = (IK[i, :, 1 - l] if dims[0] == "l" else IK[i, :, :, 1 - y]).astype(BF16)
        send(ISB.at[i], IRB.at[i], ib + i, (dims[0],))
    loop(tiles, q_first)
    down_s.third()

    bq, bv = q0 + q1, v0 + v1
    VG[6:8, :] = jnp.zeros((2, width), F32)
    picked = [spread_matrix(width, 32, j) for j in range(4)]

    def exact_pick(row, j):
        a = jnp.where(mine, VG[row : row + 1, :], 0.0)
        hi = a.astype(BF16)
        rest = a - hi.astype(F32)
        mid = rest.astype(BF16)
        low = (rest - mid.astype(F32)).astype(BF16)
        r = picked[j].astype(BF16)
        return dot(hi, r, 1, 1) + dot(mid, r, 1, 1) + dot(low, r, 1, 1)

    SG[...] = jnp.zeros_like(SG)
    SG[:, 0, :] = exact_pick(0, 2) + exact_pick(1, 3)
    SG[:, 1, :] = exact_pick(2, 0) + exact_pick(3, 1) + exact_pick(4, 2) + exact_pick(5, 3)
    for k in range(2):
        b = head * 2 + k
        lanes = slice(k * 32, k * 32 + 32)
        SG[b, 0:1, :] += jnp.concatenate([bq[:, lanes], bv[:, lanes], jnp.zeros((1, 64), F32)], axis=1)
    for hp, yp, xp in itertools.product(range(2), repeat=3):
        r = hp * 4 + yp * 2 + xp
        SG[(s * 8 + hp * 4 + l * 2 + yp) * 2 + xp, 2:3, :] = UB[1:2, r * 128 : (r + 1) * 128]

    def grad_copy(j):
        return peer_copy(SG.at[pl.ds((head + j) % 16 * 2, 2)], RG.at[j], (hss, hrs), j)

    loop(15, lambda j: grad_copy(j + 1).start())
    RG[0] = SG[pl.ds(head * 2, 2)]

    for i in range(tiles):
        dims = ("l", "y") if i < tiles // 2 else ("y", "l")
        wait(IRB.at[i], ib + i, (dims[0],))
        if dims[0] == "l":
            u = IK[i, :, l] + IRB[i].astype(F32)
            IK[i, :, 0] = u
            ISC[i] = IK[i, :, 0, 1 - y].astype(BF16)
        else:
            u = IK[i, :, :, y] + IRB[i].astype(F32)
            IK[i, :, 0] = u
            ISC[i] = IK[i, :, 0, 1 - l].astype(BF16)
        send(ISC.at[i], IRC.at[i], ic + i, (dims[1],))

    def q_second(i):
        to_x.wait(i)
        v = QK[i, x] + QRA[i, :, :, :, 0 : 3 * HEAD_DIM].astype(F32)
        QSB[i // 2, i % 2, :, :, :, 0 : 3 * HEAD_DIM] = v.astype(BF16)

    loop(tiles, q_second)

    def piece_copy(j):
        to = (head + j) % 16
        return peer_copy(
            QSB.at[to // 8, (to // 4) % 2, (to // 2) % 2, to % 2], QG.at[head], (hss, hrs), 16 + j
        )

    loop(15, lambda j: piece_copy(j + 1).start())
    QG[head] = QSB[s, h, l, y]

    up_s.third()
    out_s.third()
    down_s.last(downg_o)
    loop(15, lambda j: grad_copy(j + 1).wait_recv())
    small_sum = jnp.sum(RG[...], axis=0)
    SX[0:2] = small_sum
    x_sem = ids()
    send(SX.at[1 - x], RX, x_sem, ("x",))
    up_s.last(UF)
    uf_sem = {}
    for flips in (("s",), ("l",), ("s", "l")):
        p = at(flips)
        for hp in range(2):
            uf_sem[flips, hp] = ids()
            send(
                UF.at[pl.ds(pl.multiple_of((p["s"] * 2 + p["l"]) * 32, 32), 32), pl.ds(hp * 512, 512)],
                upg_o.at[:, quarter(s, hp, l)], uf_sem[flips, hp], flips,
            )
    for hp in range(2):
        upg_o[:, quarter(s, hp, l)] = UF[pl.ds(pl.multiple_of((s * 2 + l) * 32, 32), 32), hp * 512 : (hp + 1) * 512]

    for i in range(tiles):
        dims = ("l", "y") if i < tiles // 2 else ("y", "l")
        wait(IRC.at[i], ic + i, (dims[1],))
        mine_at = y if dims[0] == "l" else l
        IK[i, :, 1, 0] = IK[i, :, 0, mine_at] + IRC[i].astype(F32)
        ISD[i] = IK[i, 1 - h, 1, 0].astype(BF16)
        send(ISD.at[i], IRD.at[i], id_ + i, ("h",))
    out_s.last(outg_o)

    wait(RX, x_sem, ("x",))
    small_o[...] = SX[x] + RX[...]

    loop(15, lambda j: piece_copy(j + 1).wait_recv())
    for k in range(HEADS // 2):
        a, b = QG[2 * k].astype(F32), QG[2 * k + 1].astype(F32)
        for part in range(3):
            lanes = slice(part * 64, part * 64 + 64)
            to = part * width + k * 128
            qkvg_o[:, to : to + 128] = jnp.concatenate([a[:, lanes], b[:, lanes]], axis=1)

    for i in range(tiles):
        wait(IRD.at[i], id_ + i, ("h",))
        cols = slice(i * TILE, (i + 1) * TILE)
        ig_o[:, cols] = IK[i, h, 1, 0] + IRD[i].astype(F32) + DSUM[:, cols]

    for flips in (("s",), ("l",), ("s", "l")):
        p = at(flips)
        for hp in range(2):
            wait(upg_o.at[:, quarter(p["s"], hp, p["l"])], uf_sem[flips, hp], flips)

    for d in sends:
        d.wait_send()

    def small_sent(j):
        for d in small_copy(j + 1, head):
            d.wait_send()
        grad_copy(j + 1).wait_send()

    loop(15, small_sent)
    loop(15, lambda j: piece_copy(j + 1).wait_send())


def hand_over(*refs):
    large, small, outs, sems = refs[:6], refs[6], refs[7:22], refs[22]
    copies = [pltpu.make_async_copy(a, b, sems.at[k]) for k, (a, b) in enumerate(zip(large, outs))]
    for c in copies:
        c.start()
    places = ((0, 0, 32), (0, 32, 32), (0, 64, 32), (2, 0, 128), (0, 96, 32), (1, 0, 32), (1, 32, 32), (1, 64, 32), (1, 96, 32))
    for ref, (row, lane, count) in zip(outs[6:], places):
        ref[...] = small[row : row + 1, lane : lane + count]
    for c in copies:
        c.wait()


def on_block(
    tokens, qkv_weight, out_weight, up_weight, down_weight,
    query_bias, value_bias, out_bias, up_bias, down_bias,
    norm1_gain, norm1_bias, norm2_gain, norm2_bias, cotangent,
):
    n, width = tokens.shape[1], tokens.shape[2]
    hidden = up_weight.shape[1] // 4
    group = 4 * n
    length = 8 * n
    tiles = width // TILE
    vectors = [
        v.reshape(1, -1)
        for v in (query_bias, value_bias, out_bias, up_bias, down_bias, norm1_gain, norm1_bias, norm2_gain, norm2_bias)
    ]

    def b(*shape):
        return pltpu.VMEM(shape, BF16)

    def f(*shape):
        return pltpu.VMEM(shape, F32)

    group_bufs = [b(tiles, 2 * n, TILE), b(tiles, 2 * n, TILE), b(tiles, n, TILE), b(tiles, n, TILE)]

    def scatter_bufs(rows):
        return [
            b(tiles, 2, 2, rows, TILE), b(tiles, 2, 2, rows, TILE),
            b(tiles, 2, rows, TILE), b(tiles, 2, rows, TILE),
            b(tiles, rows, TILE), b(tiles, rows, TILE),
            f(tiles, 2, 2, rows, TILE),
        ]

    sem = pltpu.SemaphoreType.DMA
    scratch = [
        f(8, 128), b(2, 2, 2, 2, n, width), b(HEADS, 32, 256), b(HEADS, 2, 32, 256), f(HEADS, 2, 8, 128),
        b(2, 2, 2, 32, width), b(2, 2, 2, 2, 2, 32, hidden), b(2, 2, 2, 128, width),
        b(2, length, 64), b(2, length, 64), b(2, length, 64), b(2, 192, length), f(2, 64, length), b(2, 64, length),
        f(2, 8, length), b(4, 2, 64, group // 2), b(2, 2, 64, group), b(group, 256),
        *group_bufs, *group_bufs, f(tiles, 2, n, TILE),
        b(2, 2, n, width), b(2, 2, 2, 128, group), b(group, hidden), b(2, 2, 2, 128, group), f(group, hidden),
        b(2, 2, n, width),
        f(n, width), f(n, width), f(n, width),
        b(2, 2, 64, group), b(2, 2, 64, group), b(2, length, 64), b(2, 64, length), f(2, length, 64), f(2, 64, length),
        b(2, length, 192), b(2, 192, length),
        *scatter_bufs(128), f(128, width),
        *scatter_bufs(128),
        *scatter_bufs(32),
        b(tiles, 2, 2, 2, n, TILE), b(tiles, 2, 2, n, TILE), b(tiles, 2, 2, n, TILE),
        b(tiles, 2, n, TILE), b(tiles, 2, n, TILE), b(tiles, n, TILE), b(tiles, n, TILE), f(tiles, 2, 2, 2, n, TILE),
        b(tiles, 2, 2, 32, 256), b(tiles, 2, 2, 32, 256), f(tiles, 2, 2, 2, 32, 192), b(2, 2, 2, 2, 32, 256), b(HEADS, 32, 256),
        f(8, width), f(8, hidden), f(8, width), f(32, 8, 128), f(HEADS, 2, 8, 128), f(2, 8, 128), f(8, 128),
        sem((300,)), sem((300,)), sem((16,)), sem((16,)), sem((16,)), sem((16,)), sem((32,)), sem((32,)),
    ]
    vmem = pl.BlockSpec(memory_space=pltpu.VMEM)
    shapes = [
        jax.ShapeDtypeStruct((n, width), BF16),
        jax.ShapeDtypeStruct((n, width), F32),
        jax.ShapeDtypeStruct((32, 3 * width), F32),
        jax.ShapeDtypeStruct((32, width), F32),
        jax.ShapeDtypeStruct((32, 4 * hidden), F32),
        jax.ShapeDtypeStruct((128, width), F32),
        jax.ShapeDtypeStruct((8, 128), F32),
    ]
    results = pl.pallas_call(
        layer_kernel,
        out_shape=shapes,
        in_specs=[vmem] * 15,
        out_specs=[vmem] * 7,
        scratch_shapes=scratch,
        compiler_params=pltpu.CompilerParams(
            collective_id=0, has_side_effects=True, vmem_limit_bytes=63 * 2**20
        ),
        name="layer",
    )(tokens[0], qkv_weight, out_weight, up_weight, down_weight, *vectors, cotangent[0])
    lengths = [v.shape[1] for v in vectors]
    everywhere = pl.BlockSpec(memory_space=pl.ANY)
    done = pl.pallas_call(
        hand_over,
        out_shape=shapes[:6] + [jax.ShapeDtypeStruct((1, k), F32) for k in lengths],
        in_specs=[vmem] * 7,
        out_specs=[everywhere] * 6 + [vmem] * 9,
        scratch_shapes=[sem((6,))],
        name="results",
    )(*results)
    return (
        done[0][None], done[1][None], *done[2:6], *(v.reshape(-1) for v in done[6:]),
    )


def solution(mesh):
    placed = (
        P(("seq", "fsdp"), "ctx", None),
        P(("seq", "ctx", "fsdp"), None),
        P(("seq", "ctx", "fsdp"), None),
        P(("seq", "ctx", "fsdp"), None),
        P(("seq", "ctx", "fsdp"), None),
        P(("seq", "ctx", "fsdp")),
        P(("seq", "ctx", "fsdp")),
        P(("seq", "ctx", "fsdp")),
        P(("seq", "ctx", "fsdp")),
        P(("seq", "ctx", "fsdp")),
        P(("seq", "ctx", "fsdp")),
        P(("seq", "ctx", "fsdp")),
        P(("seq", "ctx", "fsdp")),
        P(("seq", "ctx", "fsdp")),
        P(("seq", "fsdp"), "ctx", None),
    )
    fast = dict(mesh.shape) == {"seq": 2, "ctx": 8, "fsdp": 2}
    return jax.shard_map(
        on_block if fast else on_device,
        mesh=mesh,
        in_specs=placed,
        out_specs=(
            P(("seq", "fsdp"), "ctx", None),
            P(("seq", "fsdp"), "ctx", None),
            P(("seq", "ctx", "fsdp"), None),
            P(("seq", "ctx", "fsdp"), None),
            P(("seq", "ctx", "fsdp"), None),
            P(("seq", "ctx", "fsdp"), None),
            P(("seq", "ctx", "fsdp")),
            P(("seq", "ctx", "fsdp")),
            P(("seq", "ctx", "fsdp")),
            P(("seq", "ctx", "fsdp")),
            P(("seq", "ctx", "fsdp")),
            P(("seq", "ctx", "fsdp")),
            P(("seq", "ctx", "fsdp")),
            P(("seq", "ctx", "fsdp")),
            P(("seq", "ctx", "fsdp")),
        ),
        check_vma=False,
    )
```

```python
import functools
import itertools
import math

import jax
import jax.numpy as jnp
from jax import lax
from jax.experimental import pallas as pl
from jax.experimental.pallas import tpu as pltpu
from jax.sharding import PartitionSpec as P

HEADS = 16
HEAD_DIM = 64


epsilon = 1e-05
MESH = pl.DeviceIdType.MESH
F32 = jnp.float32
BF16 = jnp.bfloat16
TILE = 256


def split_blocks(piece):
    rows = piece.shape[0]
    block = math.gcd(rows, 512)
    return (piece.reshape(rows // block, block, HEADS, HEAD_DIM), block)


def norm_forward(values, gain, shift):
    centered = values - jnp.mean(values, axis=-1, keepdims=True)
    recip = lax.rsqrt(jnp.mean(centered * centered, axis=-1, keepdims=True) + epsilon)
    normal = centered * recip
    return (normal * gain + shift, normal, recip)


def norm_backward(upstream, normal, recip, gain):
    gain_grad = jnp.sum(upstream * normal, axis=0)
    shift_grad = jnp.sum(upstream, axis=0)
    scaled = upstream * gain
    inner = (
        scaled
        - jnp.mean(scaled, axis=-1, keepdims=True)
        - normal * jnp.mean(scaled * normal, axis=-1, keepdims=True)
    )
    return (recip * inner, gain_grad, shift_grad)


def matmul(left_neighbor, right_neighbor):
    return jnp.dot(left_neighbor, right_neighbor, preferred_element_type=jnp.float32)


def on_device(
    tokens,
    qkv_weight,
    out_weight,
    up_weight,
    down_weight,
    query_bias,
    value_bias,
    out_bias,
    up_bias,
    down_bias,
    norm1_gain,
    norm1_bias,
    norm2_gain,
    norm2_bias,
    cotangent,
):
    gathered = (
        lax.all_gather(qkv_weight, ("seq", "ctx", "fsdp"), axis=0, tiled=True),
        lax.all_gather(out_weight, ("seq", "ctx", "fsdp"), axis=0, tiled=True),
        lax.all_gather(up_weight, ("seq", "ctx", "fsdp"), axis=0, tiled=True),
        lax.all_gather(down_weight, ("seq", "ctx", "fsdp"), axis=0, tiled=True),
        lax.all_gather(query_bias, ("seq", "ctx", "fsdp"), axis=0, tiled=True),
        lax.all_gather(value_bias, ("seq", "ctx", "fsdp"), axis=0, tiled=True),
        lax.all_gather(out_bias, ("seq", "ctx", "fsdp"), axis=0, tiled=True),
        lax.all_gather(up_bias, ("seq", "ctx", "fsdp"), axis=0, tiled=True),
        lax.all_gather(down_bias, ("seq", "ctx", "fsdp"), axis=0, tiled=True),
        lax.all_gather(norm1_gain, ("seq", "ctx", "fsdp"), axis=0, tiled=True),
        lax.all_gather(norm1_bias, ("seq", "ctx", "fsdp"), axis=0, tiled=True),
        lax.all_gather(norm2_gain, ("seq", "ctx", "fsdp"), axis=0, tiled=True),
        lax.all_gather(norm2_bias, ("seq", "ctx", "fsdp"), axis=0, tiled=True),
    )
    qkv_full, out_full, up_full, down_full = (gathered[0], gathered[1], gathered[2], gathered[3])
    small = tuple((item.astype(jnp.float32) for item in gathered[4:]))
    q_shift, v_shift, o_shift, u_shift, d_shift, gain_one, shift_one, gain_two, shift_two = small
    scale = HEAD_DIM ** (-0.5)
    inputs = tokens[0]
    rows = inputs.shape[0]
    width = inputs.shape[1]
    joined_bias = jnp.concatenate([q_shift, jnp.zeros_like(q_shift), v_shift])
    qkv_low = (matmul(inputs, qkv_full) + joined_bias).astype(jnp.bfloat16)
    queries = qkv_low[:, :width].reshape(rows, HEADS, HEAD_DIM)
    keys_own = qkv_low[:, width : 2 * width]
    values_own = qkv_low[:, 2 * width :]
    start_state = (
        jnp.full((HEADS, rows), -1e30, jnp.float32),
        jnp.zeros((HEADS, rows), jnp.float32),
        jnp.zeros((rows, HEADS, HEAD_DIM), jnp.float32),
    )
    piece = (
        lax.all_gather(keys_own, "ctx", axis=0, tiled=True),
        lax.all_gather(values_own, "ctx", axis=0, tiled=True),
    )
    key_blocks, block = split_blocks(piece[0])
    value_blocks, block = split_blocks(piece[1])

    def inner(state, pair):
        run_max, run_sum, accum = state
        key_tile_rows, value_block = pair
        scores = (
            jnp.einsum("qhe,khe->hqk", queries, key_tile_rows, preferred_element_type=jnp.float32)
            * scale
        )
        new_max = jnp.maximum(run_max, jnp.max(scores, axis=-1))
        factor = jnp.exp(run_max - new_max)
        weights = jnp.exp(scores - new_max[..., None])
        run_sum = run_sum * factor + jnp.sum(weights, axis=-1)
        accum = accum * factor.T[..., None] + jnp.einsum(
            "hqk,khe->qhe",
            weights.astype(jnp.bfloat16),
            value_block,
            preferred_element_type=jnp.float32,
        )
        return ((new_max, run_sum, accum), None)

    result, unused = lax.scan(inner, start_state, (key_blocks, value_blocks))
    run_max, run_sum, accum = result
    attended = accum / run_sum.T[..., None]
    log_total = run_max + jnp.log(run_sum)
    attended_low = attended.reshape(rows, width).astype(jnp.bfloat16)
    first_sum = inputs.astype(jnp.float32) + matmul(attended_low, out_full) + o_shift
    first_norm, normal_one, recip_one = norm_forward(first_sum, gain_one, shift_one)
    normed_low = first_norm.astype(jnp.bfloat16)
    hidden_pre = matmul(normed_low, up_full) + u_shift
    activated_full, gelu_pull = jax.vjp(lambda pre: jax.nn.gelu(pre, approximate=False), hidden_pre)
    activated = activated_full.astype(jnp.bfloat16)
    second_sum = first_norm + matmul(activated, down_full) + d_shift
    final, normal_two, recip_two = norm_forward(second_sum, gain_two, shift_two)
    upstream = cotangent[0].astype(jnp.float32)
    d_second, gain_two_grad, shift_two_grad = norm_backward(
        upstream, normal_two, recip_two, gain_two
    )
    d_feed = d_second.astype(jnp.bfloat16)
    down_grad = matmul(activated.T, d_feed)
    down_bias_grad = jnp.sum(d_feed.astype(jnp.float32), axis=0)
    d_hidden = gelu_pull(matmul(d_feed, down_full.T))[0].astype(jnp.bfloat16)
    up_grad = matmul(normed_low.T, d_hidden)
    up_bias_grad = jnp.sum(d_hidden.astype(jnp.float32), axis=0)
    first_input_gradient = d_second + matmul(d_hidden, up_full.T)
    d_sum_one, gain_one_grad, first_shift_gradient = norm_backward(
        first_input_gradient, normal_one, recip_one, gain_one
    )
    d_branch = d_sum_one.astype(jnp.bfloat16)
    out_grad = matmul(attended_low.T, d_branch)
    out_bias_grad = jnp.sum(d_branch.astype(jnp.float32), axis=0)
    d_attended = matmul(d_branch, out_full.T).astype(jnp.bfloat16).reshape(rows, HEADS, HEAD_DIM)
    delta = jnp.sum(d_attended.astype(jnp.float32) * attended, axis=-1).T
    total_rows = rows * lax.axis_size("ctx")
    zero_query = jnp.zeros((rows, HEADS, HEAD_DIM), jnp.float32)
    start_back = (zero_query, jnp.zeros((total_rows, 2 * width), jnp.float32))
    piece = (
        lax.all_gather(keys_own, "ctx", axis=0, tiled=True),
        lax.all_gather(values_own, "ctx", axis=0, tiled=True),
    )
    key_blocks, block = split_blocks(piece[0])
    value_blocks, block = split_blocks(piece[1])
    counter = jnp.arange(key_blocks.shape[0], dtype=jnp.int32)

    def inner(state, triple):
        key_tile_rows, value_block, number = triple
        scores = (
            jnp.einsum("qhe,khe->hqk", queries, key_tile_rows, preferred_element_type=jnp.float32)
            * scale
        )
        weights = jnp.exp(scores - log_total[..., None])
        d_probs = jnp.einsum(
            "qhe,khe->hqk", d_attended, value_block, preferred_element_type=jnp.float32
        )
        d_scores = (weights * (d_probs - delta[..., None]) * scale).astype(jnp.bfloat16)
        d_query = state[0] + jnp.einsum(
            "hqk,khe->qhe", d_scores, key_tile_rows, preferred_element_type=jnp.float32
        )
        d_key = jnp.einsum(
            "hqk,qhe->khe", d_scores, queries, preferred_element_type=jnp.float32
        ).reshape(block, width)
        d_value = jnp.einsum(
            "hqk,qhe->khe",
            weights.astype(jnp.bfloat16),
            d_attended,
            preferred_element_type=jnp.float32,
        ).reshape(block, width)
        offset = number * block
        current = lax.dynamic_slice_in_dim(state[1], offset, block, 0)
        updated = lax.dynamic_update_slice_in_dim(
            state[1], current + jnp.concatenate([d_key, d_value], axis=1), offset, 0
        )
        return ((d_query, updated), None)

    result, unused = lax.scan(inner, start_back, (key_blocks, value_blocks, counter))
    d_query = result[0].reshape(rows, width)
    summed = lax.psum_scatter(result[1], "ctx", scatter_dimension=0, tiled=True)
    d_key = summed[:, :width]
    d_value = summed[:, width:]
    d_qkv = jnp.concatenate([d_query, d_key, d_value], axis=1).astype(jnp.bfloat16)
    qkv_grad = matmul(inputs.T, d_qkv)
    d_qkv_wide = d_qkv.astype(jnp.float32)
    query_bias_gradient = jnp.sum(d_qkv_wide[:, :width], axis=0)
    value_bias_grad = jnp.sum(d_qkv_wide[:, 2 * width :], axis=0)
    input_grad = matmul(d_qkv, qkv_full.T) + d_sum_one
    sharded = (
        lax.psum_scatter(qkv_grad, ("seq", "ctx", "fsdp"), scatter_dimension=0, tiled=True),
        lax.psum_scatter(out_grad, ("seq", "ctx", "fsdp"), scatter_dimension=0, tiled=True),
        lax.psum_scatter(up_grad, ("seq", "ctx", "fsdp"), scatter_dimension=0, tiled=True),
        lax.psum_scatter(down_grad, ("seq", "ctx", "fsdp"), scatter_dimension=0, tiled=True),
        lax.psum_scatter(
            query_bias_gradient, ("seq", "ctx", "fsdp"), scatter_dimension=0, tiled=True
        ),
        lax.psum_scatter(value_bias_grad, ("seq", "ctx", "fsdp"), scatter_dimension=0, tiled=True),
        lax.psum_scatter(out_bias_grad, ("seq", "ctx", "fsdp"), scatter_dimension=0, tiled=True),
        lax.psum_scatter(up_bias_grad, ("seq", "ctx", "fsdp"), scatter_dimension=0, tiled=True),
        lax.psum_scatter(down_bias_grad, ("seq", "ctx", "fsdp"), scatter_dimension=0, tiled=True),
        lax.psum_scatter(gain_one_grad, ("seq", "ctx", "fsdp"), scatter_dimension=0, tiled=True),
        lax.psum_scatter(
            first_shift_gradient, ("seq", "ctx", "fsdp"), scatter_dimension=0, tiled=True
        ),
        lax.psum_scatter(gain_two_grad, ("seq", "ctx", "fsdp"), scatter_dimension=0, tiled=True),
        lax.psum_scatter(shift_two_grad, ("seq", "ctx", "fsdp"), scatter_dimension=0, tiled=True),
    )
    return (
        final.astype(jnp.bfloat16)[None],
        input_grad[None],
        sharded[0],
        sharded[1],
        sharded[2],
        sharded[3],
        sharded[4],
        sharded[5],
        sharded[6],
        sharded[7],
        sharded[8],
        sharded[9],
        sharded[10],
        sharded[11],
        sharded[12],
    )


def dot(left, right, left_dim=1, right_dim=0):
    return lax.dot_general(
        left, right, (((left_dim,), (right_dim,)), ((), ())), preferred_element_type=F32
    )


def loop(count, body):
    def step(i, carry):
        body(i)
        return carry

    lax.fori_loop(0, count, step, 0)


def spread_matrix(width, piece, at):
    lane = lax.broadcasted_iota(jnp.int32, (128, width), 0)
    column = lax.broadcasted_iota(jnp.int32, (128, width), 1)
    return jnp.where(lane == at * piece + column % piece, 1.0, 0.0)


def own_columns(blocks, width):
    row = lax.broadcasted_iota(jnp.int32, (blocks, width), 0)
    column = lax.broadcasted_iota(jnp.int32, (blocks, width), 1)
    return column // (width // blocks), row


def layer_kernel(
    tok, qkvw, outw, upw, downw, qb, vb, ob, ub, db, g1, b1, g2, b2, cot,
    out_o, ig_o, qkvg_o, outg_o, upg_o, downg_o, small_o,
    PK, X16, WP, WH, G, OW, UW, DW,
    QN, KN, VN, QKVT, OT, OTB, LSE, AS, AT, A4,
    R1A, R1B, R1C, R1D, R2A, R2B, R2C, R2D, KR,
    N4, N4T, C4, C4T, GP, DF4,
    FN, NORM1, DSEC,
    DS, DR, DA, DAT, DKV, DQT, DQKV, DQKVT,
    USA, URA, USB, URB, USC, URC, UK, UF,
    DSA, DRA, DSB, DRB, DSC, DRC, DK,
    OSA, ORA, OSB, ORB, OSC, ORC, OK,
    IRA, ISB, IRB, ISC, IRC, ISD, IRD, IK,
    QSA, QRA, QK, QSB, QG,
    VEC, UB, VG, SG, RG, SX, RX,
    ssem, rsem, wss, wrs, gss, grs, hss, hrs,
):
    s = lax.axis_index("seq")
    c = lax.axis_index("ctx")
    x = lax.axis_index("fsdp")
    h, l, y = c // 4, (c // 2) % 2, c % 2
    here = {"s": s, "h": h, "l": l, "y": y, "x": x}
    me = s * 16 + c * 2 + x
    head = s * 8 + c
    width = tok.shape[1]
    tiles = width // TILE
    counter = itertools.count()
    sends = []

    def at(flips):
        return {k: (1 - v if k in flips else v) for k, v in here.items()}

    def device(flips):
        p = at(flips)
        return {"seq": p["s"], "ctx": p["h"] * 4 + p["l"] * 2 + p["y"], "fsdp": p["x"]}

    def ids(n=1):
        return [next(counter) for _ in range(n)][0]

    def copy(src, dst, sem, flips):
        return pltpu.make_async_remote_copy(
            src_ref=src, dst_ref=dst, send_sem=ssem.at[sem], recv_sem=rsem.at[sem],
            device_id=device(flips), device_id_type=MESH,
        )

    def settle(since):
        for d in sends[since:]:
            d.wait_send()
        del sends[since:]

    def send(src, dst, sem, flips):
        d = copy(src, dst, sem, flips)
        d.start()
        sends.append(d)

    def wait(ref, sem, flips):
        copy(ref, ref, sem, flips).wait_recv()

    class Tiles:
        def __init__(self, src, dst, dim, of):
            self.src, self.dst, self.dim, self.of = src, dst, dim, of
            self.base = [ids() for _ in of][0] - of[0]
            self.listed = False

        def each(self, i):
            return copy(self.src.at[i], self.dst.at[i], self.base + i, (self.dim,))

        def send(self, i):
            self.each(i).start()
            if not self.listed:
                sends.append(self)
                self.listed = True

        def wait(self, i):
            self.each(i).wait_recv()

        def wait_send(self):
            for i in self.of:
                self.each(i).wait_send()

    class Gather:
        def __init__(self, order, block):
            self.order, self.block, self.sem = order, block, {}
            for n in range(1, len(order) + 1):
                for k in itertools.combinations(order, n):
                    self.sem[frozenset(k)] = ids()

        def push(self, *have, along=None):
            have = frozenset(have)
            last = max([self.order.index(d) for d in have], default=-1)
            for d in self.order[last + 1 :]:
                if along and d not in along:
                    continue
                ref = self.block(at(have))
                send(ref, ref, self.sem[have | {d}], (d,))

        def pull(self, *have):
            have = frozenset(have)
            last = max(have, key=self.order.index)
            wait(self.block(at(have)), self.sem[have], (last,))

        def pass_on(self, *have):
            self.pull(*have)
            self.push(*have)

    barrier = pltpu.get_barrier_semaphore()

    def peer(j):
        to = (head + j) % 16
        return {"seq": to // 8, "ctx": to % 8, "fsdp": x}

    def peer_copy(src, dst, sems, j):
        return pltpu.make_async_remote_copy(
            src_ref=src, dst_ref=dst, send_sem=sems[0].at[j], recv_sem=sems[1].at[j],
            device_id=peer(j % 16), device_id_type=MESH)

    loop(15, lambda j: pl.semaphore_signal(barrier, inc=1, device_id=peer(j + 1), device_id_type=MESH))
    pl.semaphore_signal(barrier, inc=1, device_id=device("x"), device_id_type=MESH)

    X16[s, h, l, y] = tok[...]
    PK[...] = jnp.zeros_like(PK)
    for k, vector in enumerate((qb, vb, ob, db, g1, b1, g2, b2)):
        PK[k // 4, k % 4 * 32 : k % 4 * 32 + 32] = vector[0, :].astype(F32)
    PK[2, :] = ub[0, :].astype(F32)
    for k in range(HEADS):
        parts = [qkvw[:, j * width + k * HEAD_DIM : j * width + (k + 1) * HEAD_DIM] for j in range(3)]
        WP[k, :, 0 : 3 * HEAD_DIM] = jnp.concatenate(parts, axis=1)
    WH[head, x] = WP[head]
    G[head, x] = PK[...]
    OW[h, y, x] = outw[...]
    DW[h, y, x] = downw[...]

    def quarter(sp, hp, lp):
        return pl.ds(pl.multiple_of(sp * 2048 + hp * 1024 + lp * 512, 512), 512)

    for hp in range(2):
        UW[s, h, l, y, x, :, hp * 512 : (hp + 1) * 512] = upw[:, quarter(s, hp, l)]

    pl.semaphore_wait(barrier, 16)

    half = width // 2

    def token_block(k):
        return lambda p: X16.at[p["s"], p["h"], p["l"], p["y"], :, pl.ds(k * half, half)]

    xg = [Gather("hlys", token_block(0)), Gather("hyls", token_block(1))]
    for g in xg:
        g.push()

    def small_copy(j, dst):
        return [
            peer_copy(WP.at[(head + j) % 16], WH.at[dst, x], (wss, wrs), j),
            peer_copy(PK, G.at[dst, x], (gss, grs), j),
        ]

    loop(15, lambda j: [d.start() for d in small_copy(j + 1, head)])

    up_sem = {}
    for flips in (("s",), ("l",), ("s", "l")):
        p = at(flips)
        for hp in range(2):
            up_sem[flips, hp] = ids()
            send(
                upw.at[:, quarter(p["s"], hp, p["l"])],
                UW.at[s, h, l, y, x, :, pl.ds(hp * 512, 512)],
                up_sem[flips, hp], flips,
            )

    def up_block(k):
        cols = (pl.ds(0, UW.shape[-1] // 2), pl.ds(UW.shape[-1] // 2, UW.shape[-1] // 2))[k]
        return lambda p: UW.at[:, p["h"], :, p["y"], p["x"], :, cols]

    def down_block(k):
        rows = (pl.ds(0, DW.shape[-2] // 2), pl.ds(DW.shape[-2] // 2, DW.shape[-2] // 2))[k]
        return lambda p: DW.at[p["h"], p["y"], p["x"], rows]

    og = Gather("hyx", lambda p: OW.at[p["h"], p["y"], p["x"]])
    ug = [Gather("hyx", up_block(0)), Gather("hxy", up_block(1))]
    dg = [Gather("hyx", down_block(0)), Gather("hxy", down_block(1))]
    for g in dg:
        g.push(along="x")
    og.push()

    for g in xg:
        g.pass_on("h")
    for flips in (("s",), ("l",), ("s", "l")):
        p = at(flips)
        for hp in range(2):
            wait(UW.at[p["s"], h, p["l"], y, x, :, pl.ds(hp * 512, 512)], up_sem[flips, hp], flips)
    for g in ug:
        g.push()
    xg[0].pass_on("l")
    xg[1].pass_on("y")

    def wait_small(j):
        for d in small_copy(j + 1, (head + 15 - j) % 16):
            d.wait_recv()

    loop(15, wait_small)
    small_sem = [ids(), ids()]
    send(WH.at[:, x], WH.at[:, x], small_sem[0], ("x",))
    send(G.at[:, x], G.at[:, x], small_sem[1], ("x",))
    xg[0].pass_on("h", "l")
    xg[1].pass_on("h", "y")
    for g in dg:
        g.push(along="hy")
    og.pass_on("h")
    og.pass_on("y")
    og.pass_on("h", "y")
    for a, b in (("y", "l"), ("l", "y")):
        g = xg[0] if a == "y" else xg[1]
        for have in ((a,), ("h", a), (b, a), ("h", b, a)):
            g.pass_on(*have)
    for g in ug:
        g.pass_on("h")
    ug[0].pass_on("y")
    ug[1].pass_on("x")

    wait(WH.at[:, 1 - x], small_sem[0], ("x",))
    wait(G.at[:, 1 - x], small_sem[1], ("x",))

    spread = [spread_matrix(width, 32, j).astype(BF16) for j in range(4)]
    block_of, row_at = own_columns(32, width)
    mine = block_of == row_at
    arrived = block_of == row_at % 16 * 2 + row_at // 16
    for row, j, to in ((0, 2, 0), (0, 3, 1), (1, 0, 2), (1, 1, 3), (1, 2, 4), (1, 3, 5)):
        rows = jnp.concatenate([G[:, 0, row, :], G[:, 1, row, :]], axis=0).astype(BF16)
        VEC[to : to + 1, :] = jnp.sum(jnp.where(arrived, dot(rows, spread[j]), 0.0), axis=0, keepdims=True)
    for hp, yp, xp in itertools.product(range(2), repeat=3):
        r = hp * 4 + yp * 2 + xp
        UB[0:1, r * 128 : (r + 1) * 128] = G[s * 8 + hp * 4 + l * 2 + yp, xp, 2:3, :]
    out_bias, down_bias = VEC[0:1, :], VEC[1:2, :]
    gain_one, shift_one, gain_two, shift_two = (VEC[k : k + 1, :] for k in range(2, 6))
    first, second = G[head, 0, 0:1, :], G[head, 1, 0:1, :]
    head_bias = jnp.concatenate(
        [first[:, 0:32], second[:, 0:32], jnp.zeros((1, 64), F32), first[:, 32:64], second[:, 32:64]], axis=1
    )
    head_weight = WH[...].reshape(width, WH.shape[-1])[:, 0 : 3 * HEAD_DIM]

    length = 8 * tok.shape[0]
    qtiles = length // TILE
    scale = HEAD_DIM ** (-0.5)
    DH4, DB4, DSUM = C4, N4, FN

    def project(j):
        sp = s if j == 0 else 1 - s

        def body(i):
            hl = X16[sp, i // 2, i % 2].reshape(TILE, width)
            res = (dot(hl, head_weight) + head_bias).astype(BF16).astype(F32)
            rows = pl.ds(pl.multiple_of(i * TILE, TILE), TILE)
            QN[j, rows, :] = res[:, 0:64].astype(BF16)
            KN[j, rows, :] = res[:, 64:128].astype(BF16)
            VN[j, rows, :] = res[:, 128:192].astype(BF16)
            QKVT[j, :, rows] = res.T.astype(BF16)

        loop(qtiles, body)

    def attend(j):
        def body(i):
            cols = pl.ds(pl.multiple_of(i * TILE, TILE), TILE)
            q = QKVT[j, 0:64, cols] * jnp.asarray(scale, BF16)
            st = dot(KN[j], q)
            top = jnp.max(st, axis=0, keepdims=True)
            e = jnp.exp(st - top)
            total = jnp.sum(e, axis=0, keepdims=True)
            o = dot(QKVT[j, 128:192, :], e.astype(BF16)) / total
            OT[j, :, cols] = o
            OTB[j, :, cols] = o.astype(BF16)
            LSE[j, 0:1, cols] = top + jnp.log(total)

        loop(qtiles, body)

    tokens = tok.shape[0]

    def tok_cols(hp, lp, yp):
        return pl.ds(pl.multiple_of((hp * 4 + lp * 2 + yp) * tokens, tokens), tokens)

    others = (("h",), ("y",), ("h", "y"))
    a_sem = {(f, j): ids() for f in others for j in range(2)}

    def seq_cols(j):
        sp = s if j == 0 else 1 - s
        return pl.ds(pl.multiple_of(sp * 2 * tokens, 2 * tokens), 2 * tokens)

    def hand_out(j):
        for k, flips in enumerate(((),) + others):
            p = at(flips)
            piece = jnp.concatenate([OTB[j, :, tok_cols(p["h"], lp, p["y"])] for lp in range(2)], axis=1)
            if flips:
                AS[k, j] = piece
                send(AS.at[k, j], AT.at[h, y, :, seq_cols(j)], a_sem[flips, j], flips)
            else:
                AT[h, y, :, seq_cols(j)] = piece

    project(0)
    attend(0)
    hand_out(0)
    ug[0].pass_on("h", "y")
    ug[1].pass_on("h", "x")
    for have in (("s",), ("h", "s"), ("l", "s"), ("h", "l", "s"), ("y", "s"), ("h", "y", "s"), ("l", "y", "s"), ("h", "l", "y", "s")):
        for g in xg:
            g.pull(*have)
    project(1)
    attend(1)
    hand_out(1)
    for g in dg:
        g.pass_on("h")
    dg[0].pass_on("y")
    dg[1].pass_on("x")
    dg[0].pass_on("h", "y")
    dg[1].pass_on("h", "x")
    for have in (("x",), ("h", "x"), ("y", "x"), ("h", "y", "x")):
        og.pull(*have)
    for flips in others:
        p = at(flips)
        for j in range(2):
            wait(AT.at[p["h"], p["y"], :, seq_cols(j)], a_sem[flips, j], flips)

    group = 4 * tokens
    half_n = tokens // 2
    A4[...] = AT[...].reshape(4 * HEAD_DIM, group).astype(F32).T.astype(BF16).reshape(A4.shape)

    def rows_of(k):
        return slice(k * half_n, (k + 1) * half_n)

    def half_rows(ref, k):
        return ref[:, :, rows_of(k), :].reshape(4 * half_n, ref.shape[-1])

    def core_rows(ref, k, sp):
        return ref[sp, :, rows_of(k), :].reshape(2 * half_n, ref.shape[-1])

    class GroupSum:
        def __init__(self, bufs, ref, product):
            self.sa, self.ra, self.sb, self.rb = bufs
            self.ref, self.product = ref, product
            self.to_core = [Tiles(self.sa.at[k], self.ra.at[k], "s", range(tiles)) for k in range(2)]
            self.to_pair = [Tiles(self.sb.at[k], self.rb.at[k], "l", range(tiles)) for k in range(2)]

        def start(self, k):
            def body(i):
                left = jnp.concatenate([core_rows(self.ref, k, 1 - s), core_rows(self.ref, k, s)], axis=0)
                v = self.product(left, i).reshape(2, 2, half_n, TILE)
                self.sa[k, i] = v[0].astype(BF16)
                self.to_core[k].send(i)
                KR[k, i] = v[1]

            loop(tiles, body)

        def relay(self, k):
            def body(i):
                self.to_core[k].wait(i)
                KR[k, i] += self.ra[k, i].astype(F32)
                self.sb[k, i] = KR[k, i, 1 - l].astype(BF16)
                self.to_pair[k].send(i)

            loop(tiles, body)

        def finish(self, k):
            for i in range(tiles):
                self.to_pair[k].wait(i)
            return jnp.concatenate([KR[k, i, l] + self.rb[k, i].astype(F32) for i in range(tiles)], axis=1)

    class GroupGather:
        def __init__(self, ref):
            self.ref = ref
            self.half = [
                Gather("ls", lambda p, k=k: ref.at[p["s"], p["l"], pl.ds(k * half_n, half_n)]) for k in range(2)
            ]

        def push(self, k, value):
            self.ref[s, l, rows_of(k)] = value
            self.half[k].push()

        def relay(self, k):
            self.half[k].pass_on("l")

        def pull(self, k):
            self.half[k].pull("s")
            self.half[k].pull("l", "s")

    def col_tile(i):
        return pl.ds(pl.multiple_of(i * TILE, TILE), TILE)

    def norm_forward(values, gain, shift):
        centered = values - jnp.mean(values, axis=-1, keepdims=True)
        recip = lax.rsqrt(jnp.mean(centered * centered, axis=-1, keepdims=True) + epsilon)
        normal = centered * recip
        return normal * gain + shift, normal, recip

    def norm_backward(upstream, normal, recip, gain):
        gain_grad = jnp.sum(upstream * normal, axis=0, keepdims=True)
        shift_grad = jnp.sum(upstream, axis=0, keepdims=True)
        scaled = upstream * gain
        inner = (
            scaled
            - jnp.mean(scaled, axis=-1, keepdims=True)
            - normal * jnp.mean(scaled * normal, axis=-1, keepdims=True)
        )
        return recip * inner, gain_grad, shift_grad

    def add_vectors(k, first_row, *rows):
        for at_row, row in zip(first_row, rows):
            VG[at_row : at_row + 1, :] = row if k == 0 else VG[at_row : at_row + 1, :] + row

    mark = len(sends)
    branch = GroupSum(
        (R1A, R1B, R1C, R1D), A4,
        lambda left, i: dot(left, OW[:, :, :, :, col_tile(i)].reshape(4 * HEAD_DIM, TILE)),
    )
    branch.start(0)
    branch.start(1)
    branch.relay(0)
    branch.relay(1)

    normed = GroupGather(N4)
    recips = []
    for k in range(2):
        r = rows_of(k)
        first_norm, normal_one, recip_one = norm_forward(
            tok[r, :].astype(F32) + branch.finish(k) + out_bias, gain_one, shift_one
        )
        FN[r, :] = first_norm
        NORM1[r, :] = normal_one
        recips.append(recip_one)
        normed.push(k, first_norm.astype(BF16))

    def pull_rest(pair):
        for have in (("x",), ("h", "x"), ("y", "x"), ("h", "y", "x")):
            pair[0].pull(*have)
        for have in (("y",), ("h", "y"), ("x", "y"), ("h", "x", "y")):
            pair[1].pull(*have)

    hidden = UB.shape[1]

    def up(k):
        def body(i):
            cols = col_tile(i)
            w = UW[:, :, :, :, :, :, cols].reshape(width, TILE)
            pre = dot(half_rows(N4, k), w) + UB[0:1, cols]
            phi = 0.5 * (1.0 + lax.erf(pre * (2.0 ** -0.5)))
            slope = phi + pre * (jnp.exp(-0.5 * pre * pre) * ((2.0 * math.pi) ** -0.5))
            GP[:, :, rows_of(k), cols] = slope.reshape(2, 2, half_n, TILE)
            C4[:, :, rows_of(k), cols] = (pre * phi).astype(BF16).reshape(2, 2, half_n, TILE)

        loop(hidden // TILE, body)

    feed = GroupSum(
        (R2A, R2B, R2C, R2D), C4,
        lambda left, i: dot(left, DW[:, :, :, :, col_tile(i)].reshape(hidden, TILE)),
    )
    normed.relay(0)
    pull_rest(ug)
    normed.pull(0)
    up(0)
    normed.relay(1)
    pull_rest(dg)
    feed.start(0)
    normed.pull(1)
    up(1)
    feed.relay(0)
    feed.start(1)
    feed.relay(1)
    settle(mark)

    d_feeds = GroupGather(DF4)
    for k in range(2):
        r = rows_of(k)
        final, normal_two, recip_two = norm_forward(
            FN[r, :] + feed.finish(k) + down_bias, gain_two, shift_two
        )
        out_o[r, :] = final.astype(BF16)
        d_second, gain_two_grad, shift_two_grad = norm_backward(
            cot[r, :].astype(F32), normal_two, recip_two, gain_two
        )
        DSEC[r, :] = d_second
        d_feed = d_second.astype(BF16)
        d_feeds.push(k, d_feed)
        add_vectors(
            k, (1, 4, 5), jnp.sum(d_feed.astype(F32), axis=0, keepdims=True), gain_two_grad, shift_two_grad
        )

    def transpose_rows(i):
        cols = pl.ds(pl.multiple_of(i * 128, 128), 128)
        t = N4[:, :, :, cols].reshape(group, 128)
        t = t.astype(F32).T.astype(BF16).reshape(2, 2, 32, group)
        for yp, xp in itertools.product(range(2), repeat=2):
            to = pl.ds(pl.multiple_of((i // 4 * 2 + i % 2) * 32, 32), 32)
            N4T[(i // 2) % 2, yp, xp, to, :] = t[yp, xp]
        C4T[i // 4, (i // 2) % 2, i % 2] = C4[:, :, :, cols].reshape(group, 128).astype(F32).T.astype(BF16)

    loop(8, transpose_rows)

    def d_hidden(k):
        def body(i):
            rows = DW[i // 2, i % 2].reshape(TILE, width)
            cols = col_tile(i)
            slope = GP[:, :, rows_of(k), cols].reshape(4 * half_n, TILE)
            v = (dot(half_rows(DF4, k), rows, 1, 1) * slope).astype(BF16)
            DH4[:, :, rows_of(k), cols] = v.reshape(2, 2, half_n, TILE)
            total = jnp.sum(v.astype(F32), axis=0, keepdims=True)
            UB[1:2, cols] = total if k == 0 else UB[1:2, cols] + total

        loop(hidden // TILE, body)

    class Scatter:
        def __init__(self, bufs, product):
            self.sa, self.ra, self.sb, self.rb, self.sc, self.rc, self.keep = bufs
            self.product = product
            self.shape = self.sa.shape[1:]
            self.parts = []
            for k, (one, two) in enumerate((("x", "y"), ("y", "x"))):
                of = range(k * tiles // 2, (k + 1) * tiles // 2)
                self.parts.append((
                    one, two, of,
                    Tiles(self.sa, self.ra, one, of), Tiles(self.sb, self.rb, two, of), Tiles(self.sc, self.rc, "h", of),
                ))

        def first(self):
            for one, two, of, a, b, c in self.parts:
                def body(i, one=one, of=of, a=a):
                    i = of[0] + i
                    self.sa[i] = self.product(one, 1 - here[one], i).reshape(self.shape).astype(BF16)
                    a.send(i)

                loop(len(of), body)

        def second(self):
            for one, two, of, a, b, c in self.parts:
                def body(i, one=one, two=two, of=of, a=a, b=b):
                    i = of[0] + i
                    v = self.product(one, here[one], i).reshape(self.shape)
                    a.wait(i)
                    self.keep[i] = v + self.ra[i].astype(F32)
                    self.sb[i] = self.keep[i, :, 1 - here[two]].astype(BF16)
                    b.send(i)

                loop(len(of), body)

        def third(self):
            for one, two, of, a, b, c in self.parts:
                def body(i, two=two, of=of, b=b, c=c):
                    i = of[0] + i
                    b.wait(i)
                    self.keep[i, :, 0] = self.keep[i, :, here[two]] + self.rb[i].astype(F32)
                    self.sc[i] = self.keep[i, 1 - h, 0].astype(BF16)
                    c.send(i)

                loop(len(of), body)

        def last(self, out):
            for one, two, of, a, b, c in self.parts:
                def body(i, of=of, c=c):
                    i = of[0] + i
                    c.wait(i)
                    out[:, col_tile(i)] = self.keep[i, h, 0] + self.rc[i].astype(F32)

                loop(len(of), body)

    def up_product(dim, v, i):
        rows = N4T[:, :, v] if dim == "x" else N4T[:, v]
        return dot(rows.reshape(group, group), DH4[:, :, :, col_tile(i)].reshape(group, TILE))

    def down_product(dim, v, i):
        rows = C4T[:, :, v] if dim == "x" else C4T[:, v]
        return dot(rows.reshape(group, group), DF4[:, :, :, col_tile(i)].reshape(group, TILE))

    def out_product(dim, v, i):
        rows = AT[:, :, pl.ds(pl.multiple_of(v * 32, 32), 32), :] if dim == "x" else AT[:, v]
        return dot(rows.reshape(128, group), DB4[:, :, :, col_tile(i)].reshape(group, TILE))

    down_s = Scatter((DSA, DRA, DSB, DRB, DSC, DRC, DK), down_product)
    up_s = Scatter((USA, URA, USB, URB, USC, URC, UK), up_product)
    out_s = Scatter((OSA, ORA, OSB, ORB, OSC, ORC, OK), out_product)

    def up_rows(i):
        return UW[i // 2, i % 2].reshape(TILE, hidden)

    d_first = GroupSum((R1A, R1B, R1C, R1D), DH4, lambda left, i: dot(left, up_rows(i), 1, 1))
    d_branches = GroupGather(DB4)
    d_feeds.relay(0)
    d_feeds.pull(0)
    d_hidden(0)
    d_feeds.relay(1)
    d_first.start(0)
    d_feeds.pull(1)
    d_hidden(1)
    d_first.relay(0)
    d_first.start(1)
    d_first.relay(1)
    down_s.first()
    for k in range(2):
        r = rows_of(k)
        d_sum_one, gain_one_grad, shift_one_grad = norm_backward(
            DSEC[r, :] + d_first.finish(k), NORM1[r, :], recips[k], gain_one
        )
        DSUM[r, :] = d_sum_one
        d_branch = d_sum_one.astype(BF16)
        d_branches.push(k, d_branch)
        add_vectors(
            k, (0, 2, 3), jnp.sum(d_branch.astype(F32), axis=0, keepdims=True), gain_one_grad, shift_one_grad
        )
    up_s.first()
    for k in range(2):
        d_branches.relay(k)
    for k in range(2):
        d_branches.pull(k)

    d_att = dot(DB4[...].reshape(group, width), OW[...].reshape(4 * HEAD_DIM, width), 1, 1).astype(BF16)
    d_att = d_att.astype(F32).T.astype(BF16).reshape(2, 2, HEAD_DIM, group)
    DS[...] = d_att
    d_sem = {f: ids() for f in others}
    for flips in others:
        p = at(flips)
        send(DS.at[p["h"], p["y"]], DR.at[h, y], d_sem[flips], flips)
    DR[h, y] = DS[h, y]

    out_s.first()
    down_s.second()

    for flips in others:
        p = at(flips)
        wait(DR.at[p["h"], p["y"]], d_sem[flips], flips)
    for sp in range(2):
        j = s if sp == 0 else 1 - s
        for hp, lp, yp in itertools.product(range(2), repeat=3):
            part = DR[hp, yp, :, (sp * 2 + lp) * tokens : (sp * 2 + lp + 1) * tokens]
            at_tok = (hp * 4 + lp * 2 + yp) * tokens
            DAT[j, :, at_tok : at_tok + tokens] = part
            DA[j, at_tok : at_tok + tokens, :] = part.astype(F32).T.astype(BF16)

    def attend_back(j):
        DKV[...] = jnp.zeros_like(DKV)

        def body(i):
            cols = col_tile(i)
            q = QKVT[j, 0:64, cols] * jnp.asarray(scale, BF16)
            p = jnp.exp(dot(KN[j], q) - LSE[j, 0:1, cols])
            da = DAT[j, :, cols]
            delta = jnp.sum(da.astype(F32) * OT[j, :, cols], axis=0, keepdims=True)
            dp = dot(VN[j], da)
            ds = (p * (dp - delta) * scale).astype(BF16)
            DQT[j, :, cols] = dot(QKVT[j, 64:128, :], ds)
            DKV[0] += dot(ds, QN[j, cols, :])
            DKV[1] += dot(p.astype(BF16), DA[j, cols, :])

        loop(qtiles, body)
        dqt = DQT[j].astype(BF16).astype(F32)
        dq = dqt.T
        dk, dv = DKV[0].astype(BF16).astype(F32), DKV[1].astype(BF16).astype(F32)
        DQKV[j] = jnp.concatenate([dq, dk, dv], axis=1).astype(BF16)
        DQKVT[j, 0:64, :] = dqt.astype(BF16)
        DQKVT[j, 64:128, :] = dk.T.astype(BF16)
        DQKVT[j, 128:192, :] = dv.T.astype(BF16)
        return jnp.sum(dq, axis=0, keepdims=True), jnp.sum(dv, axis=0, keepdims=True)

    def input_tile(j, i):
        w = WH[pl.ds(pl.multiple_of(i * 4, 4), 4)].reshape(TILE, WH.shape[-1])[:, 0 : 3 * HEAD_DIM]
        return dot(DQKV[j], w, 1, 1).reshape(2, 2, 2, tokens, TILE)

    ia, ib, ic, id_ = ([ids() for _ in range(tiles)][0] for _ in range(4))

    def in_sent(i):
        return (C4T if i < tiles // 2 else N4T).at[:, :, :, :, pl.ds(i % 2 * TILE, TILE)]

    q1, v1 = attend_back(1)
    down_s.third()
    up_s.second()
    for i in range(tiles):
        in_sent(i)[...] = input_tile(1, i).astype(BF16)
        send(in_sent(i), IRA.at[i], ia + i, ("s",))
    q0, v0 = attend_back(0)
    to_x = Tiles(QSA, QRA, "x", range(tiles))

    def q_first(i):
        cols = col_tile(i)
        v = dot(DQKVT[0], X16[s, :, :, :, :, cols].reshape(length, TILE))
        v += dot(DQKVT[1], X16[1 - s, :, :, :, :, cols].reshape(length, TILE))
        v = v.T.reshape(2, 2, 2, 32, 3 * HEAD_DIM)
        for xp in range(2):
            QK[i, xp] = v[:, :, xp]
        QSA[i, :, :, :, 0 : 3 * HEAD_DIM] = QK[i, 1 - x].astype(BF16)
        to_x.send(i)

    in_order = (0, 2, 1, 3)
    for i in in_order:
        dims = ("l", "y") if i < tiles // 2 else ("y", "l")
        wait(IRA.at[i], ia + i, ("s",))
        IK[i] = input_tile(0, i) + IRA[i].astype(F32)
        ISB[i] = (IK[i, :, 1 - l] if dims[0] == "l" else IK[i, :, :, 1 - y]).astype(BF16)
        send(ISB.at[i], IRB.at[i], ib + i, (dims[0],))
    up_s.third()
    out_s.second()
    loop(tiles, q_first)
    bq, bv = q0 + q1, v0 + v1
    VG[6:8, :] = jnp.zeros((2, width), F32)
    picked = [spread_matrix(width, 32, j) for j in range(4)]

    def exact_pick(row, j):
        a = jnp.where(mine, VG[row : row + 1, :], 0.0)
        hi = a.astype(BF16)
        rest = a - hi.astype(F32)
        mid = rest.astype(BF16)
        low = (rest - mid.astype(F32)).astype(BF16)
        r = picked[j].astype(BF16)
        return dot(hi, r, 1, 1) + dot(mid, r, 1, 1) + dot(low, r, 1, 1)

    SG[...] = jnp.zeros_like(SG)
    SG[:, 0, :] = exact_pick(0, 2) + exact_pick(1, 3)
    SG[:, 1, :] = exact_pick(2, 0) + exact_pick(3, 1) + exact_pick(4, 2) + exact_pick(5, 3)
    for k in range(2):
        b = head * 2 + k
        lanes = slice(k * 32, k * 32 + 32)
        SG[b, 0:1, :] += jnp.concatenate([bq[:, lanes], bv[:, lanes], jnp.zeros((1, 64), F32)], axis=1)
    for hp, yp, xp in itertools.product(range(2), repeat=3):
        r = hp * 4 + yp * 2 + xp
        SG[(s * 8 + hp * 4 + l * 2 + yp) * 2 + xp, 2:3, :] = UB[1:2, r * 128 : (r + 1) * 128]

    def grad_copy(j):
        return peer_copy(SG.at[pl.ds((head + j) % 16 * 2, 2)], RG.at[j], (hss, hrs), j)

    loop(15, lambda j: grad_copy(j + 1).start())
    RG[0] = SG[pl.ds(head * 2, 2)]

    for i in in_order:
        dims = ("l", "y") if i < tiles // 2 else ("y", "l")
        wait(IRB.at[i], ib + i, (dims[0],))
        if dims[0] == "l":
            u = IK[i, :, l] + IRB[i].astype(F32)
            IK[i, :, 0] = u
            ISC[i] = IK[i, :, 0, 1 - y].astype(BF16)
        else:
            u = IK[i, :, :, y] + IRB[i].astype(F32)
            IK[i, :, 0] = u
            ISC[i] = IK[i, :, 0, 1 - l].astype(BF16)
        send(ISC.at[i], IRC.at[i], ic + i, (dims[1],))

    out_s.third()

    def q_second(i):
        to_x.wait(i)
        v = QK[i, x] + QRA[i, :, :, :, 0 : 3 * HEAD_DIM].astype(F32)
        QSB[i // 2, i % 2, :, :, :, 0 : 3 * HEAD_DIM] = v.astype(BF16)

    loop(tiles, q_second)

    def piece_copy(j):
        to = (head + j) % 16
        return peer_copy(
            QSB.at[to // 8, (to // 4) % 2, (to // 2) % 2, to % 2], QG.at[head], (hss, hrs), 16 + j
        )

    loop(15, lambda j: piece_copy(j + 1).start())
    QG[head] = QSB[s, h, l, y]

    for i in in_order:
        dims = ("l", "y") if i < tiles // 2 else ("y", "l")
        wait(IRC.at[i], ic + i, (dims[1],))
        mine_at = y if dims[0] == "l" else l
        IK[i, :, 1, 0] = IK[i, :, 0, mine_at] + IRC[i].astype(F32)
        ISD[i] = IK[i, 1 - h, 1, 0].astype(BF16)
        send(ISD.at[i], IRD.at[i], id_ + i, ("h",))
    down_s.last(downg_o)
    loop(15, lambda j: grad_copy(j + 1).wait_recv())
    small_sum = jnp.sum(RG[...], axis=0)
    SX[0:2] = small_sum
    x_sem = ids()
    send(SX.at[1 - x], RX, x_sem, ("x",))
    up_s.last(UF)
    uf_sem = {}
    for flips in (("s",), ("l",), ("s", "l")):
        p = at(flips)
        for hp in range(2):
            uf_sem[flips, hp] = ids()
            send(
                UF.at[pl.ds(pl.multiple_of((p["s"] * 2 + p["l"]) * 32, 32), 32), pl.ds(hp * 512, 512)],
                upg_o.at[:, quarter(s, hp, l)], uf_sem[flips, hp], flips,
            )
    for hp in range(2):
        upg_o[:, quarter(s, hp, l)] = UF[pl.ds(pl.multiple_of((s * 2 + l) * 32, 32), 32), hp * 512 : (hp + 1) * 512]

    out_s.last(outg_o)

    wait(RX, x_sem, ("x",))
    small_o[...] = SX[x] + RX[...]

    loop(15, lambda j: piece_copy(j + 1).wait_recv())
    for k in range(HEADS // 2):
        a, b = QG[2 * k].astype(F32), QG[2 * k + 1].astype(F32)
        for part in range(3):
            lanes = slice(part * 64, part * 64 + 64)
            to = part * width + k * 128
            qkvg_o[:, to : to + 128] = jnp.concatenate([a[:, lanes], b[:, lanes]], axis=1)

    for i in range(tiles):
        wait(IRD.at[i], id_ + i, ("h",))
        cols = slice(i * TILE, (i + 1) * TILE)
        ig_o[:, cols] = IK[i, h, 1, 0] + IRD[i].astype(F32) + DSUM[:, cols]

    for flips in (("s",), ("l",), ("s", "l")):
        p = at(flips)
        for hp in range(2):
            wait(upg_o.at[:, quarter(p["s"], hp, p["l"])], uf_sem[flips, hp], flips)

    for d in sends:
        d.wait_send()

    def small_sent(j):
        for d in small_copy(j + 1, head):
            d.wait_send()
        grad_copy(j + 1).wait_send()

    loop(15, small_sent)
    loop(15, lambda j: piece_copy(j + 1).wait_send())


def hand_over(*refs):
    large, small, outs, sems = refs[:6], refs[6], refs[7:22], refs[22]
    copies = [pltpu.make_async_copy(a, b, sems.at[k]) for k, (a, b) in enumerate(zip(large, outs))]
    for c in copies:
        c.start()
    places = ((0, 0, 32), (0, 32, 32), (0, 64, 32), (2, 0, 128), (0, 96, 32), (1, 0, 32), (1, 32, 32), (1, 64, 32), (1, 96, 32))
    for ref, (row, lane, count) in zip(outs[6:], places):
        ref[...] = small[row : row + 1, lane : lane + count]
    for c in copies:
        c.wait()


def on_block(
    tokens, qkv_weight, out_weight, up_weight, down_weight,
    query_bias, value_bias, out_bias, up_bias, down_bias,
    norm1_gain, norm1_bias, norm2_gain, norm2_bias, cotangent,
):
    n, width = tokens.shape[1], tokens.shape[2]
    hidden = up_weight.shape[1] // 4
    group = 4 * n
    length = 8 * n
    tiles = width // TILE
    vectors = [
        v.reshape(1, -1)
        for v in (query_bias, value_bias, out_bias, up_bias, down_bias, norm1_gain, norm1_bias, norm2_gain, norm2_bias)
    ]

    def b(*shape):
        return pltpu.VMEM(shape, BF16)

    def f(*shape):
        return pltpu.VMEM(shape, F32)

    group_bufs = [b(2, tiles, 2, n // 2, TILE), b(2, tiles, 2, n // 2, TILE), b(2, tiles, n // 2, TILE), b(2, tiles, n // 2, TILE)]

    def scatter_bufs(rows):
        return [
            b(tiles, 2, 2, rows, TILE), b(tiles, 2, 2, rows, TILE),
            b(tiles, 2, rows, TILE), b(tiles, 2, rows, TILE),
            b(tiles, rows, TILE), b(tiles, rows, TILE),
            f(tiles, 2, 2, rows, TILE),
        ]

    sem = pltpu.SemaphoreType.DMA
    scratch = [
        f(8, 128), b(2, 2, 2, 2, n, width), b(HEADS, 32, 256), b(HEADS, 2, 32, 256), f(HEADS, 2, 8, 128),
        b(2, 2, 2, 32, width), b(2, 2, 2, 2, 2, 32, hidden), b(2, 2, 2, 128, width),
        b(2, length, 64), b(2, length, 64), b(2, length, 64), b(2, 192, length), f(2, 64, length), b(2, 64, length),
        f(2, 8, length), b(4, 2, 64, group // 2), b(2, 2, 64, group), b(2, 2, n, 256),
        *group_bufs, *group_bufs, f(2, tiles, 2, n // 2, TILE),
        b(2, 2, n, width), b(2, 2, 2, 128, group), b(2, 2, n, hidden), b(2, 2, 2, 128, group), f(2, 2, n, hidden),
        b(2, 2, n, width),
        f(n, width), f(n, width), f(n, width),
        b(2, 2, 64, group), b(2, 2, 64, group), b(2, length, 64), b(2, 64, length), f(2, length, 64), f(2, 64, length),
        b(2, length, 192), b(2, 192, length),
        *scatter_bufs(128), f(128, width),
        *scatter_bufs(128),
        *scatter_bufs(32),
        b(tiles, 2, 2, 2, n, TILE), b(tiles, 2, 2, n, TILE), b(tiles, 2, 2, n, TILE),
        b(tiles, 2, n, TILE), b(tiles, 2, n, TILE), b(tiles, n, TILE), b(tiles, n, TILE), f(tiles, 2, 2, 2, n, TILE),
        b(tiles, 2, 2, 32, 256), b(tiles, 2, 2, 32, 256), f(tiles, 2, 2, 2, 32, 192), b(2, 2, 2, 2, 32, 256), b(HEADS, 32, 256),
        f(8, width), f(8, hidden), f(8, width), f(32, 8, 128), f(HEADS, 2, 8, 128), f(2, 8, 128), f(8, 128),
        sem((300,)), sem((300,)), sem((16,)), sem((16,)), sem((16,)), sem((16,)), sem((32,)), sem((32,)),
    ]
    vmem = pl.BlockSpec(memory_space=pltpu.VMEM)
    shapes = [
        jax.ShapeDtypeStruct((n, width), BF16),
        jax.ShapeDtypeStruct((n, width), F32),
        jax.ShapeDtypeStruct((32, 3 * width), F32),
        jax.ShapeDtypeStruct((32, width), F32),
        jax.ShapeDtypeStruct((32, 4 * hidden), F32),
        jax.ShapeDtypeStruct((128, width), F32),
        jax.ShapeDtypeStruct((8, 128), F32),
    ]
    results = pl.pallas_call(
        layer_kernel,
        out_shape=shapes,
        in_specs=[vmem] * 15,
        out_specs=[vmem] * 7,
        scratch_shapes=scratch,
        compiler_params=pltpu.CompilerParams(
            collective_id=0, has_side_effects=True, vmem_limit_bytes=63 * 2**20
        ),
        name="layer",
    )(tokens[0], qkv_weight, out_weight, up_weight, down_weight, *vectors, cotangent[0])
    lengths = [v.shape[1] for v in vectors]
    everywhere = pl.BlockSpec(memory_space=pl.ANY)
    done = pl.pallas_call(
        hand_over,
        out_shape=shapes[:6] + [jax.ShapeDtypeStruct((1, k), F32) for k in lengths],
        in_specs=[vmem] * 7,
        out_specs=[everywhere] * 6 + [vmem] * 9,
        scratch_shapes=[sem((6,))],
        name="results",
    )(*results)
    return (
        done[0][None], done[1][None], *done[2:6], *(v.reshape(-1) for v in done[6:]),
    )


def solution(mesh):
    placed = (
        P(("seq", "fsdp"), "ctx", None),
        P(("seq", "ctx", "fsdp"), None),
        P(("seq", "ctx", "fsdp"), None),
        P(("seq", "ctx", "fsdp"), None),
        P(("seq", "ctx", "fsdp"), None),
        P(("seq", "ctx", "fsdp")),
        P(("seq", "ctx", "fsdp")),
        P(("seq", "ctx", "fsdp")),
        P(("seq", "ctx", "fsdp")),
        P(("seq", "ctx", "fsdp")),
        P(("seq", "ctx", "fsdp")),
        P(("seq", "ctx", "fsdp")),
        P(("seq", "ctx", "fsdp")),
        P(("seq", "ctx", "fsdp")),
        P(("seq", "fsdp"), "ctx", None),
    )
    fast = dict(mesh.shape) == {"seq": 2, "ctx": 8, "fsdp": 2}
    return jax.shard_map(
        on_block if fast else on_device,
        mesh=mesh,
        in_specs=placed,
        out_specs=(
            P(("seq", "fsdp"), "ctx", None),
            P(("seq", "fsdp"), "ctx", None),
            P(("seq", "ctx", "fsdp"), None),
            P(("seq", "ctx", "fsdp"), None),
            P(("seq", "ctx", "fsdp"), None),
            P(("seq", "ctx", "fsdp"), None),
            P(("seq", "ctx", "fsdp")),
            P(("seq", "ctx", "fsdp")),
            P(("seq", "ctx", "fsdp")),
            P(("seq", "ctx", "fsdp")),
            P(("seq", "ctx", "fsdp")),
            P(("seq", "ctx", "fsdp")),
            P(("seq", "ctx", "fsdp")),
            P(("seq", "ctx", "fsdp")),
            P(("seq", "ctx", "fsdp")),
        ),
        check_vma=False,
    )
```

```python
import functools
import itertools
import math

import jax
import jax.numpy as jnp
from jax import lax
from jax.experimental import pallas as pl
from jax.experimental.pallas import tpu as pltpu
from jax.sharding import PartitionSpec as P

HEADS = 16
HEAD_DIM = 64


epsilon = 1e-05
MESH = pl.DeviceIdType.MESH
F32 = jnp.float32
BF16 = jnp.bfloat16
TILE = 256


def split_blocks(piece):
    rows = piece.shape[0]
    block = math.gcd(rows, 512)
    return (piece.reshape(rows // block, block, HEADS, HEAD_DIM), block)


def norm_forward(values, gain, shift):
    centered = values - jnp.mean(values, axis=-1, keepdims=True)
    recip = lax.rsqrt(jnp.mean(centered * centered, axis=-1, keepdims=True) + epsilon)
    normal = centered * recip
    return (normal * gain + shift, normal, recip)


def norm_backward(upstream, normal, recip, gain):
    gain_grad = jnp.sum(upstream * normal, axis=0)
    shift_grad = jnp.sum(upstream, axis=0)
    scaled = upstream * gain
    inner = (
        scaled
        - jnp.mean(scaled, axis=-1, keepdims=True)
        - normal * jnp.mean(scaled * normal, axis=-1, keepdims=True)
    )
    return (recip * inner, gain_grad, shift_grad)


def matmul(left_neighbor, right_neighbor):
    return jnp.dot(left_neighbor, right_neighbor, preferred_element_type=jnp.float32)


def on_device(
    tokens,
    qkv_weight,
    out_weight,
    up_weight,
    down_weight,
    query_bias,
    value_bias,
    out_bias,
    up_bias,
    down_bias,
    norm1_gain,
    norm1_bias,
    norm2_gain,
    norm2_bias,
    cotangent,
):
    gathered = (
        lax.all_gather(qkv_weight, ("seq", "ctx", "fsdp"), axis=0, tiled=True),
        lax.all_gather(out_weight, ("seq", "ctx", "fsdp"), axis=0, tiled=True),
        lax.all_gather(up_weight, ("seq", "ctx", "fsdp"), axis=0, tiled=True),
        lax.all_gather(down_weight, ("seq", "ctx", "fsdp"), axis=0, tiled=True),
        lax.all_gather(query_bias, ("seq", "ctx", "fsdp"), axis=0, tiled=True),
        lax.all_gather(value_bias, ("seq", "ctx", "fsdp"), axis=0, tiled=True),
        lax.all_gather(out_bias, ("seq", "ctx", "fsdp"), axis=0, tiled=True),
        lax.all_gather(up_bias, ("seq", "ctx", "fsdp"), axis=0, tiled=True),
        lax.all_gather(down_bias, ("seq", "ctx", "fsdp"), axis=0, tiled=True),
        lax.all_gather(norm1_gain, ("seq", "ctx", "fsdp"), axis=0, tiled=True),
        lax.all_gather(norm1_bias, ("seq", "ctx", "fsdp"), axis=0, tiled=True),
        lax.all_gather(norm2_gain, ("seq", "ctx", "fsdp"), axis=0, tiled=True),
        lax.all_gather(norm2_bias, ("seq", "ctx", "fsdp"), axis=0, tiled=True),
    )
    qkv_full, out_full, up_full, down_full = (gathered[0], gathered[1], gathered[2], gathered[3])
    small = tuple((item.astype(jnp.float32) for item in gathered[4:]))
    q_shift, v_shift, o_shift, u_shift, d_shift, gain_one, shift_one, gain_two, shift_two = small
    scale = HEAD_DIM ** (-0.5)
    inputs = tokens[0]
    rows = inputs.shape[0]
    width = inputs.shape[1]
    joined_bias = jnp.concatenate([q_shift, jnp.zeros_like(q_shift), v_shift])
    qkv_low = (matmul(inputs, qkv_full) + joined_bias).astype(jnp.bfloat16)
    queries = qkv_low[:, :width].reshape(rows, HEADS, HEAD_DIM)
    keys_own = qkv_low[:, width : 2 * width]
    values_own = qkv_low[:, 2 * width :]
    start_state = (
        jnp.full((HEADS, rows), -1e30, jnp.float32),
        jnp.zeros((HEADS, rows), jnp.float32),
        jnp.zeros((rows, HEADS, HEAD_DIM), jnp.float32),
    )
    piece = (
        lax.all_gather(keys_own, "ctx", axis=0, tiled=True),
        lax.all_gather(values_own, "ctx", axis=0, tiled=True),
    )
    key_blocks, block = split_blocks(piece[0])
    value_blocks, block = split_blocks(piece[1])

    def inner(state, pair):
        run_max, run_sum, accum = state
        key_tile_rows, value_block = pair
        scores = (
            jnp.einsum("qhe,khe->hqk", queries, key_tile_rows, preferred_element_type=jnp.float32)
            * scale
        )
        new_max = jnp.maximum(run_max, jnp.max(scores, axis=-1))
        factor = jnp.exp(run_max - new_max)
        weights = jnp.exp(scores - new_max[..., None])
        run_sum = run_sum * factor + jnp.sum(weights, axis=-1)
        accum = accum * factor.T[..., None] + jnp.einsum(
            "hqk,khe->qhe",
            weights.astype(jnp.bfloat16),
            value_block,
            preferred_element_type=jnp.float32,
        )
        return ((new_max, run_sum, accum), None)

    result, unused = lax.scan(inner, start_state, (key_blocks, value_blocks))
    run_max, run_sum, accum = result
    attended = accum / run_sum.T[..., None]
    log_total = run_max + jnp.log(run_sum)
    attended_low = attended.reshape(rows, width).astype(jnp.bfloat16)
    first_sum = inputs.astype(jnp.float32) + matmul(attended_low, out_full) + o_shift
    first_norm, normal_one, recip_one = norm_forward(first_sum, gain_one, shift_one)
    normed_low = first_norm.astype(jnp.bfloat16)
    hidden_pre = matmul(normed_low, up_full) + u_shift
    activated_full, gelu_pull = jax.vjp(lambda pre: jax.nn.gelu(pre, approximate=False), hidden_pre)
    activated = activated_full.astype(jnp.bfloat16)
    second_sum = first_norm + matmul(activated, down_full) + d_shift
    final, normal_two, recip_two = norm_forward(second_sum, gain_two, shift_two)
    upstream = cotangent[0].astype(jnp.float32)
    d_second, gain_two_grad, shift_two_grad = norm_backward(
        upstream, normal_two, recip_two, gain_two
    )
    d_feed = d_second.astype(jnp.bfloat16)
    down_grad = matmul(activated.T, d_feed)
    down_bias_grad = jnp.sum(d_feed.astype(jnp.float32), axis=0)
    d_hidden = gelu_pull(matmul(d_feed, down_full.T))[0].astype(jnp.bfloat16)
    up_grad = matmul(normed_low.T, d_hidden)
    up_bias_grad = jnp.sum(d_hidden.astype(jnp.float32), axis=0)
    first_input_gradient = d_second + matmul(d_hidden, up_full.T)
    d_sum_one, gain_one_grad, first_shift_gradient = norm_backward(
        first_input_gradient, normal_one, recip_one, gain_one
    )
    d_branch = d_sum_one.astype(jnp.bfloat16)
    out_grad = matmul(attended_low.T, d_branch)
    out_bias_grad = jnp.sum(d_branch.astype(jnp.float32), axis=0)
    d_attended = matmul(d_branch, out_full.T).astype(jnp.bfloat16).reshape(rows, HEADS, HEAD_DIM)
    delta = jnp.sum(d_attended.astype(jnp.float32) * attended, axis=-1).T
    total_rows = rows * lax.axis_size("ctx")
    zero_query = jnp.zeros((rows, HEADS, HEAD_DIM), jnp.float32)
    start_back = (zero_query, jnp.zeros((total_rows, 2 * width), jnp.float32))
    piece = (
        lax.all_gather(keys_own, "ctx", axis=0, tiled=True),
        lax.all_gather(values_own, "ctx", axis=0, tiled=True),
    )
    key_blocks, block = split_blocks(piece[0])
    value_blocks, block = split_blocks(piece[1])
    counter = jnp.arange(key_blocks.shape[0], dtype=jnp.int32)

    def inner(state, triple):
        key_tile_rows, value_block, number = triple
        scores = (
            jnp.einsum("qhe,khe->hqk", queries, key_tile_rows, preferred_element_type=jnp.float32)
            * scale
        )
        weights = jnp.exp(scores - log_total[..., None])
        d_probs = jnp.einsum(
            "qhe,khe->hqk", d_attended, value_block, preferred_element_type=jnp.float32
        )
        d_scores = (weights * (d_probs - delta[..., None]) * scale).astype(jnp.bfloat16)
        d_query = state[0] + jnp.einsum(
            "hqk,khe->qhe", d_scores, key_tile_rows, preferred_element_type=jnp.float32
        )
        d_key = jnp.einsum(
            "hqk,qhe->khe", d_scores, queries, preferred_element_type=jnp.float32
        ).reshape(block, width)
        d_value = jnp.einsum(
            "hqk,qhe->khe",
            weights.astype(jnp.bfloat16),
            d_attended,
            preferred_element_type=jnp.float32,
        ).reshape(block, width)
        offset = number * block
        current = lax.dynamic_slice_in_dim(state[1], offset, block, 0)
        updated = lax.dynamic_update_slice_in_dim(
            state[1], current + jnp.concatenate([d_key, d_value], axis=1), offset, 0
        )
        return ((d_query, updated), None)

    result, unused = lax.scan(inner, start_back, (key_blocks, value_blocks, counter))
    d_query = result[0].reshape(rows, width)
    summed = lax.psum_scatter(result[1], "ctx", scatter_dimension=0, tiled=True)
    d_key = summed[:, :width]
    d_value = summed[:, width:]
    d_qkv = jnp.concatenate([d_query, d_key, d_value], axis=1).astype(jnp.bfloat16)
    qkv_grad = matmul(inputs.T, d_qkv)
    d_qkv_wide = d_qkv.astype(jnp.float32)
    query_bias_gradient = jnp.sum(d_qkv_wide[:, :width], axis=0)
    value_bias_grad = jnp.sum(d_qkv_wide[:, 2 * width :], axis=0)
    input_grad = matmul(d_qkv, qkv_full.T) + d_sum_one
    sharded = (
        lax.psum_scatter(qkv_grad, ("seq", "ctx", "fsdp"), scatter_dimension=0, tiled=True),
        lax.psum_scatter(out_grad, ("seq", "ctx", "fsdp"), scatter_dimension=0, tiled=True),
        lax.psum_scatter(up_grad, ("seq", "ctx", "fsdp"), scatter_dimension=0, tiled=True),
        lax.psum_scatter(down_grad, ("seq", "ctx", "fsdp"), scatter_dimension=0, tiled=True),
        lax.psum_scatter(
            query_bias_gradient, ("seq", "ctx", "fsdp"), scatter_dimension=0, tiled=True
        ),
        lax.psum_scatter(value_bias_grad, ("seq", "ctx", "fsdp"), scatter_dimension=0, tiled=True),
        lax.psum_scatter(out_bias_grad, ("seq", "ctx", "fsdp"), scatter_dimension=0, tiled=True),
        lax.psum_scatter(up_bias_grad, ("seq", "ctx", "fsdp"), scatter_dimension=0, tiled=True),
        lax.psum_scatter(down_bias_grad, ("seq", "ctx", "fsdp"), scatter_dimension=0, tiled=True),
        lax.psum_scatter(gain_one_grad, ("seq", "ctx", "fsdp"), scatter_dimension=0, tiled=True),
        lax.psum_scatter(
            first_shift_gradient, ("seq", "ctx", "fsdp"), scatter_dimension=0, tiled=True
        ),
        lax.psum_scatter(gain_two_grad, ("seq", "ctx", "fsdp"), scatter_dimension=0, tiled=True),
        lax.psum_scatter(shift_two_grad, ("seq", "ctx", "fsdp"), scatter_dimension=0, tiled=True),
    )
    return (
        final.astype(jnp.bfloat16)[None],
        input_grad[None],
        sharded[0],
        sharded[1],
        sharded[2],
        sharded[3],
        sharded[4],
        sharded[5],
        sharded[6],
        sharded[7],
        sharded[8],
        sharded[9],
        sharded[10],
        sharded[11],
        sharded[12],
    )


def dot(left, right, left_dim=1, right_dim=0):
    return lax.dot_general(
        left, right, (((left_dim,), (right_dim,)), ((), ())), preferred_element_type=F32
    )


def loop(count, body):
    def step(i, carry):
        body(i)
        return carry

    lax.fori_loop(0, count, step, 0)


def spread_matrix(width, piece, at):
    lane = lax.broadcasted_iota(jnp.int32, (128, width), 0)
    column = lax.broadcasted_iota(jnp.int32, (128, width), 1)
    return jnp.where(lane == at * piece + column % piece, 1.0, 0.0)


def own_columns(blocks, width):
    row = lax.broadcasted_iota(jnp.int32, (blocks, width), 0)
    column = lax.broadcasted_iota(jnp.int32, (blocks, width), 1)
    return column // (width // blocks), row


def layer_kernel(
    tok, qkvw, outw, upw, downw, qb, vb, ob, ub, db, g1, b1, g2, b2, cot,
    out_o, ig_o, qkvg_o, outg_o, upg_o, downg_o, small_o,
    PK, X16, WP, WH, G, OW, UW, DW,
    QN, KN, VN, QKVT, OT, OTB, LSE, AS, AT, A4,
    R1A, R1B, R1C, R1D, R2A, R2B, R2C, R2D, KR,
    N4, N4T, C4, C4T, GP, DF4,
    FN, NORM1, DSEC,
    DS, DR, DA, DAT, DKV, DQT, DQKV, DQKVT,
    USA, URA, USB, URB, USC, URC, UK, UF,
    DSA, DRA, DSB, DRB, DSC, DRC, DK,
    OSA, ORA, OSB, ORB, OSC, ORC, OK,
    IRA, ISB, IRB, ISC, IRC, ISD, IRD, IK,
    QSA, QRA, QK, QSB, QG,
    VEC, UB, VG, SG, RG, SX, RX,
    ssem, rsem, wss, wrs, gss, grs, hss, hrs,
):
    s = lax.axis_index("seq")
    c = lax.axis_index("ctx")
    x = lax.axis_index("fsdp")
    h, l, y = c // 4, (c // 2) % 2, c % 2
    here = {"s": s, "h": h, "l": l, "y": y, "x": x}
    me = s * 16 + c * 2 + x
    head = s * 8 + c
    width = tok.shape[1]
    tiles = width // TILE
    counter = itertools.count()
    sends = []

    def at(flips):
        return {k: (1 - v if k in flips else v) for k, v in here.items()}

    def device(flips):
        p = at(flips)
        return {"seq": p["s"], "ctx": p["h"] * 4 + p["l"] * 2 + p["y"], "fsdp": p["x"]}

    def ids(n=1):
        return [next(counter) for _ in range(n)][0]

    def copy(src, dst, sem, flips):
        return pltpu.make_async_remote_copy(
            src_ref=src, dst_ref=dst, send_sem=ssem.at[sem], recv_sem=rsem.at[sem],
            device_id=device(flips), device_id_type=MESH,
        )

    def settle(since):
        for d in sends[since:]:
            d.wait_send()
        del sends[since:]

    def send(src, dst, sem, flips):
        d = copy(src, dst, sem, flips)
        d.start()
        sends.append(d)

    def wait(ref, sem, flips):
        copy(ref, ref, sem, flips).wait_recv()

    class Tiles:
        def __init__(self, src, dst, dim, of):
            self.src, self.dst, self.dim, self.of = src, dst, dim, of
            self.base = [ids() for _ in of][0] - of[0]
            self.listed = False

        def each(self, i):
            return copy(self.src.at[i], self.dst.at[i], self.base + i, (self.dim,))

        def send(self, i):
            self.each(i).start()
            if not self.listed:
                sends.append(self)
                self.listed = True

        def wait(self, i):
            self.each(i).wait_recv()

        def wait_send(self):
            for i in self.of:
                self.each(i).wait_send()

    class Gather:
        def __init__(self, order, block):
            self.order, self.block, self.sem = order, block, {}
            for n in range(1, len(order) + 1):
                for k in itertools.combinations(order, n):
                    self.sem[frozenset(k)] = ids()

        def push(self, *have, along=None):
            have = frozenset(have)
            last = max([self.order.index(d) for d in have], default=-1)
            for d in self.order[last + 1 :]:
                if along and d not in along:
                    continue
                ref = self.block(at(have))
                send(ref, ref, self.sem[have | {d}], (d,))

        def pull(self, *have):
            have = frozenset(have)
            last = max(have, key=self.order.index)
            wait(self.block(at(have)), self.sem[have], (last,))

        def pass_on(self, *have):
            self.pull(*have)
            self.push(*have)

    barrier = pltpu.get_barrier_semaphore()

    def peer(j):
        to = (head + j) % 16
        return {"seq": to // 8, "ctx": to % 8, "fsdp": x}

    def peer_copy(src, dst, sems, j):
        return pltpu.make_async_remote_copy(
            src_ref=src, dst_ref=dst, send_sem=sems[0].at[j], recv_sem=sems[1].at[j],
            device_id=peer(j % 16), device_id_type=MESH)

    loop(15, lambda j: pl.semaphore_signal(barrier, inc=1, device_id=peer(j + 1), device_id_type=MESH))
    pl.semaphore_signal(barrier, inc=1, device_id=device("x"), device_id_type=MESH)

    X16[s, h, l, y] = tok[...]
    PK[...] = jnp.zeros_like(PK)
    for k, vector in enumerate((qb, vb, ob, db, g1, b1, g2, b2)):
        PK[k // 4, k % 4 * 32 : k % 4 * 32 + 32] = vector[0, :].astype(F32)
    PK[2, :] = ub[0, :].astype(F32)
    for k in range(HEADS):
        parts = [qkvw[:, j * width + k * HEAD_DIM : j * width + (k + 1) * HEAD_DIM] for j in range(3)]
        WP[k, :, 0 : 3 * HEAD_DIM] = jnp.concatenate(parts, axis=1)
    WH[head, x] = WP[head]
    G[head, x] = PK[...]
    OW[h, y, x] = outw[...]
    DW[h, y, x] = downw[...]

    def quarter(sp, hp, lp):
        return pl.ds(pl.multiple_of(sp * 2048 + hp * 1024 + lp * 512, 512), 512)

    for hp in range(2):
        UW[s, h, l, y, x, :, hp * 512 : (hp + 1) * 512] = upw[:, quarter(s, hp, l)]

    pl.semaphore_wait(barrier, 16)

    half = width // 2

    def token_block(k):
        return lambda p: X16.at[p["s"], p["h"], p["l"], p["y"], :, pl.ds(k * half, half)]

    xg = [Gather("hlys", token_block(0)), Gather("hyls", token_block(1))]
    for g in xg:
        g.push()

    def small_copy(j, dst):
        return [
            peer_copy(WP.at[(head + j) % 16], WH.at[dst, x], (wss, wrs), j),
            peer_copy(PK, G.at[dst, x], (gss, grs), j),
        ]

    loop(15, lambda j: [d.start() for d in small_copy(j + 1, head)])

    up_sem = {}
    for flips in (("s",), ("l",), ("s", "l")):
        p = at(flips)
        for hp in range(2):
            up_sem[flips, hp] = ids()
            send(
                upw.at[:, quarter(p["s"], hp, p["l"])],
                UW.at[s, h, l, y, x, :, pl.ds(hp * 512, 512)],
                up_sem[flips, hp], flips,
            )

    def up_block(k):
        cols = (pl.ds(0, UW.shape[-1] // 2), pl.ds(UW.shape[-1] // 2, UW.shape[-1] // 2))[k]
        return lambda p: UW.at[:, p["h"], :, p["y"], p["x"], :, cols]

    def down_block(k):
        rows = (pl.ds(0, DW.shape[-2] // 2), pl.ds(DW.shape[-2] // 2, DW.shape[-2] // 2))[k]
        return lambda p: DW.at[p["h"], p["y"], p["x"], rows]

    og = Gather("hyx", lambda p: OW.at[p["h"], p["y"], p["x"]])
    ug = [Gather("hyx", up_block(0)), Gather("hxy", up_block(1))]
    dg = [Gather("hyx", down_block(0)), Gather("hxy", down_block(1))]
    for g in dg:
        g.push(along="x")
    og.push()

    for g in xg:
        g.pass_on("h")
    for flips in (("s",), ("l",), ("s", "l")):
        p = at(flips)
        for hp in range(2):
            wait(UW.at[p["s"], h, p["l"], y, x, :, pl.ds(hp * 512, 512)], up_sem[flips, hp], flips)
    for g in ug:
        g.push()
    xg[0].pass_on("l")
    xg[1].pass_on("y")

    def wait_small(j):
        for d in small_copy(j + 1, (head + 15 - j) % 16):
            d.wait_recv()

    loop(15, wait_small)
    small_sem = [ids(), ids()]
    send(WH.at[:, x], WH.at[:, x], small_sem[0], ("x",))
    send(G.at[:, x], G.at[:, x], small_sem[1], ("x",))
    xg[0].pass_on("h", "l")
    xg[1].pass_on("h", "y")
    og.pass_on("h")
    og.pass_on("y")
    og.pass_on("h", "y")
    for a, b in (("y", "l"), ("l", "y")):
        g = xg[0] if a == "y" else xg[1]
        for have in ((a,), ("h", a), (b, a), ("h", b, a)):
            g.pass_on(*have)

    for g in dg:
        g.push(along="hy")
    wait(WH.at[:, 1 - x], small_sem[0], ("x",))
    wait(G.at[:, 1 - x], small_sem[1], ("x",))

    spread = [spread_matrix(width, 32, j).astype(BF16) for j in range(4)]
    block_of, row_at = own_columns(32, width)
    mine = block_of == row_at
    arrived = block_of == row_at % 16 * 2 + row_at // 16
    for row, j, to in ((0, 2, 0), (0, 3, 1), (1, 0, 2), (1, 1, 3), (1, 2, 4), (1, 3, 5)):
        rows = jnp.concatenate([G[:, 0, row, :], G[:, 1, row, :]], axis=0).astype(BF16)
        VEC[to : to + 1, :] = jnp.sum(jnp.where(arrived, dot(rows, spread[j]), 0.0), axis=0, keepdims=True)
    for hp, yp, xp in itertools.product(range(2), repeat=3):
        r = hp * 4 + yp * 2 + xp
        UB[0:1, r * 128 : (r + 1) * 128] = G[s * 8 + hp * 4 + l * 2 + yp, xp, 2:3, :]
    out_bias, down_bias = VEC[0:1, :], VEC[1:2, :]
    gain_one, shift_one, gain_two, shift_two = (VEC[k : k + 1, :] for k in range(2, 6))
    first, second = G[head, 0, 0:1, :], G[head, 1, 0:1, :]
    head_bias = jnp.concatenate(
        [first[:, 0:32], second[:, 0:32], jnp.zeros((1, 64), F32), first[:, 32:64], second[:, 32:64]], axis=1
    )
    head_weight = WH[...].reshape(width, WH.shape[-1])[:, 0 : 3 * HEAD_DIM]

    length = 8 * tok.shape[0]
    qtiles = length // TILE
    scale = HEAD_DIM ** (-0.5)
    DH4, DB4, DSUM = C4, N4, FN

    def project(j):
        sp = s if j == 0 else 1 - s

        def body(i):
            hl = X16[sp, i // 2, i % 2].reshape(TILE, width)
            res = (dot(hl, head_weight) + head_bias).astype(BF16).astype(F32)
            rows = pl.ds(pl.multiple_of(i * TILE, TILE), TILE)
            QN[j, rows, :] = res[:, 0:64].astype(BF16)
            KN[j, rows, :] = res[:, 64:128].astype(BF16)
            VN[j, rows, :] = res[:, 128:192].astype(BF16)
            QKVT[j, :, rows] = res.T.astype(BF16)

        loop(qtiles, body)

    def attend(j):
        def body(i):
            cols = pl.ds(pl.multiple_of(i * TILE, TILE), TILE)
            q = QKVT[j, 0:64, cols] * jnp.asarray(scale, BF16)
            st = dot(KN[j], q)
            top = jnp.max(st, axis=0, keepdims=True)
            e = jnp.exp(st - top)
            total = jnp.sum(e, axis=0, keepdims=True)
            o = dot(QKVT[j, 128:192, :], e.astype(BF16)) / total
            OT[j, :, cols] = o
            OTB[j, :, cols] = o.astype(BF16)
            LSE[j, 0:1, cols] = top + jnp.log(total)

        loop(qtiles, body)

    tokens = tok.shape[0]

    def tok_cols(hp, lp, yp):
        return pl.ds(pl.multiple_of((hp * 4 + lp * 2 + yp) * tokens, tokens), tokens)

    others = (("h",), ("y",), ("h", "y"))
    a_sem = {(f, j): ids() for f in others for j in range(2)}

    def seq_cols(j):
        sp = s if j == 0 else 1 - s
        return pl.ds(pl.multiple_of(sp * 2 * tokens, 2 * tokens), 2 * tokens)

    def hand_out(j):
        for k, flips in enumerate(((),) + others):
            p = at(flips)
            piece = jnp.concatenate([OTB[j, :, tok_cols(p["h"], lp, p["y"])] for lp in range(2)], axis=1)
            if flips:
                AS[k, j] = piece
                send(AS.at[k, j], AT.at[h, y, :, seq_cols(j)], a_sem[flips, j], flips)
            else:
                AT[h, y, :, seq_cols(j)] = piece

    project(0)
    attend(0)
    hand_out(0)
    for g in ug:
        g.pass_on("h")
    ug[0].pass_on("y")
    ug[1].pass_on("x")
    for have in (("s",), ("h", "s"), ("l", "s"), ("h", "l", "s"), ("y", "s"), ("h", "y", "s"), ("l", "y", "s"), ("h", "l", "y", "s")):
        for g in xg:
            g.pull(*have)
    project(1)
    attend(1)
    hand_out(1)
    ug[0].pass_on("h", "y")
    ug[1].pass_on("h", "x")
    for g in dg:
        g.pass_on("h")
    for have in (("x",), ("h", "x"), ("y", "x"), ("h", "y", "x")):
        og.pull(*have)
    for flips in others:
        p = at(flips)
        for j in range(2):
            wait(AT.at[p["h"], p["y"], :, seq_cols(j)], a_sem[flips, j], flips)

    group = 4 * tokens
    half_n = tokens // 2
    A4[...] = AT[...].reshape(4 * HEAD_DIM, group).astype(F32).T.astype(BF16).reshape(A4.shape)

    def rows_of(k):
        return slice(k * half_n, (k + 1) * half_n)

    def half_rows(ref, k):
        return ref[:, :, rows_of(k), :].reshape(4 * half_n, ref.shape[-1])

    def core_rows(ref, k, sp):
        return ref[sp, :, rows_of(k), :].reshape(2 * half_n, ref.shape[-1])

    class GroupSum:
        def __init__(self, bufs, ref, product):
            self.sa, self.ra, self.sb, self.rb = bufs
            self.ref, self.product = ref, product
            self.to_core = [Tiles(self.sa.at[k], self.ra.at[k], "s", range(tiles)) for k in range(2)]
            self.to_pair = [Tiles(self.sb.at[k], self.rb.at[k], "l", range(tiles)) for k in range(2)]

        def start(self, k):
            def body(i):
                left = jnp.concatenate([core_rows(self.ref, k, 1 - s), core_rows(self.ref, k, s)], axis=0)
                v = self.product(left, i).reshape(2, 2, half_n, TILE)
                self.sa[k, i] = v[0].astype(BF16)
                self.to_core[k].send(i)
                KR[k, i] = v[1]

            loop(tiles, body)

        def relay(self, k):
            def body(i):
                self.to_core[k].wait(i)
                KR[k, i] += self.ra[k, i].astype(F32)
                self.sb[k, i] = KR[k, i, 1 - l].astype(BF16)
                self.to_pair[k].send(i)

            loop(tiles, body)

        def finish(self, k):
            for i in range(tiles):
                self.to_pair[k].wait(i)
            return jnp.concatenate([KR[k, i, l] + self.rb[k, i].astype(F32) for i in range(tiles)], axis=1)

    class GroupGather:
        def __init__(self, ref):
            self.ref = ref
            self.half = [
                Gather("ls", lambda p, k=k: ref.at[p["s"], p["l"], pl.ds(k * half_n, half_n)]) for k in range(2)
            ]

        def push(self, k, value):
            self.ref[s, l, rows_of(k)] = value
            self.half[k].push()

        def relay(self, k):
            self.half[k].pass_on("l")

        def pull(self, k):
            self.half[k].pull("s")
            self.half[k].pull("l", "s")

    def col_tile(i):
        return pl.ds(pl.multiple_of(i * TILE, TILE), TILE)

    def norm_forward(values, gain, shift):
        centered = values - jnp.mean(values, axis=-1, keepdims=True)
        recip = lax.rsqrt(jnp.mean(centered * centered, axis=-1, keepdims=True) + epsilon)
        normal = centered * recip
        return normal * gain + shift, normal, recip

    def norm_backward(upstream, normal, recip, gain):
        gain_grad = jnp.sum(upstream * normal, axis=0, keepdims=True)
        shift_grad = jnp.sum(upstream, axis=0, keepdims=True)
        scaled = upstream * gain
        inner = (
            scaled
            - jnp.mean(scaled, axis=-1, keepdims=True)
            - normal * jnp.mean(scaled * normal, axis=-1, keepdims=True)
        )
        return recip * inner, gain_grad, shift_grad

    def add_vectors(k, first_row, *rows):
        for at_row, row in zip(first_row, rows):
            VG[at_row : at_row + 1, :] = row if k == 0 else VG[at_row : at_row + 1, :] + row

    mark = len(sends)
    branch = GroupSum(
        (R1A, R1B, R1C, R1D), A4,
        lambda left, i: dot(left, OW[:, :, :, :, col_tile(i)].reshape(4 * HEAD_DIM, TILE)),
    )
    branch.start(0)
    branch.start(1)
    branch.relay(0)
    branch.relay(1)
    dg[0].pass_on("y")
    dg[1].pass_on("x")
    dg[0].pass_on("h", "y")
    dg[1].pass_on("h", "x")

    normed = GroupGather(N4)
    recips = []
    for k in range(2):
        r = rows_of(k)
        first_norm, normal_one, recip_one = norm_forward(
            tok[r, :].astype(F32) + branch.finish(k) + out_bias, gain_one, shift_one
        )
        FN[r, :] = first_norm
        NORM1[r, :] = normal_one
        recips.append(recip_one)
        normed.push(k, first_norm.astype(BF16))

    def pull_rest(pair):
        for have in (("x",), ("h", "x"), ("y", "x"), ("h", "y", "x")):
            pair[0].pull(*have)
        for have in (("y",), ("h", "y"), ("x", "y"), ("h", "x", "y")):
            pair[1].pull(*have)

    hidden = UB.shape[1]

    def up(k):
        def body(i):
            cols = col_tile(i)
            w = UW[:, :, :, :, :, :, cols].reshape(width, TILE)
            pre = dot(half_rows(N4, k), w) + UB[0:1, cols]
            phi = 0.5 * (1.0 + lax.erf(pre * (2.0 ** -0.5)))
            slope = phi + pre * (jnp.exp(-0.5 * pre * pre) * ((2.0 * math.pi) ** -0.5))
            GP[:, :, rows_of(k), cols] = slope.reshape(2, 2, half_n, TILE)
            C4[:, :, rows_of(k), cols] = (pre * phi).astype(BF16).reshape(2, 2, half_n, TILE)

        loop(hidden // TILE, body)

    feed = GroupSum(
        (R2A, R2B, R2C, R2D), C4,
        lambda left, i: dot(left, DW[:, :, :, :, col_tile(i)].reshape(hidden, TILE)),
    )
    normed.relay(0)
    pull_rest(ug)
    normed.pull(0)
    up(0)
    normed.relay(1)
    pull_rest(dg)
    feed.start(0)
    normed.pull(1)
    up(1)
    feed.relay(0)
    feed.start(1)
    feed.relay(1)
    settle(mark)

    d_feeds = GroupGather(DF4)
    for k in range(2):
        r = rows_of(k)
        final, normal_two, recip_two = norm_forward(
            FN[r, :] + feed.finish(k) + down_bias, gain_two, shift_two
        )
        out_o[r, :] = final.astype(BF16)
        d_second, gain_two_grad, shift_two_grad = norm_backward(
            cot[r, :].astype(F32), normal_two, recip_two, gain_two
        )
        DSEC[r, :] = d_second
        d_feed = d_second.astype(BF16)
        d_feeds.push(k, d_feed)
        add_vectors(
            k, (1, 4, 5), jnp.sum(d_feed.astype(F32), axis=0, keepdims=True), gain_two_grad, shift_two_grad
        )

    def transpose_rows(i):
        cols = pl.ds(pl.multiple_of(i * 128, 128), 128)
        t = N4[:, :, :, cols].reshape(group, 128)
        t = t.astype(F32).T.astype(BF16).reshape(2, 2, 32, group)
        for yp, xp in itertools.product(range(2), repeat=2):
            to = pl.ds(pl.multiple_of((i // 4 * 2 + i % 2) * 32, 32), 32)
            N4T[(i // 2) % 2, yp, xp, to, :] = t[yp, xp]
        C4T[i // 4, (i // 2) % 2, i % 2] = C4[:, :, :, cols].reshape(group, 128).astype(F32).T.astype(BF16)

    loop(8, transpose_rows)

    def d_hidden(k):
        def body(i):
            rows = DW[i // 2, i % 2].reshape(TILE, width)
            cols = col_tile(i)
            slope = GP[:, :, rows_of(k), cols].reshape(4 * half_n, TILE)
            v = (dot(half_rows(DF4, k), rows, 1, 1) * slope).astype(BF16)
            DH4[:, :, rows_of(k), cols] = v.reshape(2, 2, half_n, TILE)
            total = jnp.sum(v.astype(F32), axis=0, keepdims=True)
            UB[1:2, cols] = total if k == 0 else UB[1:2, cols] + total

        loop(hidden // TILE, body)

    class Scatter:
        def __init__(self, bufs, product):
            self.sa, self.ra, self.sb, self.rb, self.sc, self.rc, self.keep = bufs
            self.product = product
            self.shape = self.sa.shape[1:]
            self.parts = []
            for k, (one, two) in enumerate((("x", "y"), ("y", "x"))):
                of = range(k * tiles // 2, (k + 1) * tiles // 2)
                self.parts.append((
                    one, two, of,
                    Tiles(self.sa, self.ra, one, of), Tiles(self.sb, self.rb, two, of), Tiles(self.sc, self.rc, "h", of),
                ))

        def first(self):
            for one, two, of, a, b, c in self.parts:
                def body(i, one=one, of=of, a=a):
                    i = of[0] + i
                    self.sa[i] = self.product(one, 1 - here[one], i).reshape(self.shape).astype(BF16)
                    a.send(i)

                loop(len(of), body)

        def second(self):
            for one, two, of, a, b, c in self.parts:
                def body(i, one=one, two=two, of=of, a=a, b=b):
                    i = of[0] + i
                    v = self.product(one, here[one], i).reshape(self.shape)
                    a.wait(i)
                    self.keep[i] = v + self.ra[i].astype(F32)
                    self.sb[i] = self.keep[i, :, 1 - here[two]].astype(BF16)
                    b.send(i)

                loop(len(of), body)

        def third(self):
            for one, two, of, a, b, c in self.parts:
                def body(i, two=two, of=of, b=b, c=c):
                    i = of[0] + i
                    b.wait(i)
                    self.keep[i, :, 0] = self.keep[i, :, here[two]] + self.rb[i].astype(F32)
                    self.sc[i] = self.keep[i, 1 - h, 0].astype(BF16)
                    c.send(i)

                loop(len(of), body)

        def last(self, out):
            for one, two, of, a, b, c in self.parts:
                def body(i, of=of, c=c):
                    i = of[0] + i
                    c.wait(i)
                    out[:, col_tile(i)] = self.keep[i, h, 0] + self.rc[i].astype(F32)

                loop(len(of), body)

    def up_product(dim, v, i):
        rows = N4T[:, :, v] if dim == "x" else N4T[:, v]
        return dot(rows.reshape(group, group), DH4[:, :, :, col_tile(i)].reshape(group, TILE))

    def down_product(dim, v, i):
        rows = C4T[:, :, v] if dim == "x" else C4T[:, v]
        return dot(rows.reshape(group, group), DF4[:, :, :, col_tile(i)].reshape(group, TILE))

    def out_product(dim, v, i):
        rows = AT[:, :, pl.ds(pl.multiple_of(v * 32, 32), 32), :] if dim == "x" else AT[:, v]
        return dot(rows.reshape(128, group), DB4[:, :, :, col_tile(i)].reshape(group, TILE))

    down_s = Scatter((DSA, DRA, DSB, DRB, DSC, DRC, DK), down_product)
    up_s = Scatter((USA, URA, USB, URB, USC, URC, UK), up_product)
    out_s = Scatter((OSA, ORA, OSB, ORB, OSC, ORC, OK), out_product)

    def up_rows(i):
        return UW[i // 2, i % 2].reshape(TILE, hidden)

    d_first = GroupSum((R1A, R1B, R1C, R1D), DH4, lambda left, i: dot(left, up_rows(i), 1, 1))
    d_branches = GroupGather(DB4)
    d_feeds.relay(0)
    d_feeds.pull(0)
    d_hidden(0)
    d_feeds.relay(1)
    d_first.start(0)
    d_feeds.pull(1)
    d_hidden(1)
    down_s.first()
    d_first.relay(0)
    d_first.start(1)
    d_first.relay(1)
    for k in range(2):
        r = rows_of(k)
        d_sum_one, gain_one_grad, shift_one_grad = norm_backward(
            DSEC[r, :] + d_first.finish(k), NORM1[r, :], recips[k], gain_one
        )
        DSUM[r, :] = d_sum_one
        d_branch = d_sum_one.astype(BF16)
        d_branches.push(k, d_branch)
        add_vectors(
            k, (0, 2, 3), jnp.sum(d_branch.astype(F32), axis=0, keepdims=True), gain_one_grad, shift_one_grad
        )
    up_s.first()
    for k in range(2):
        d_branches.relay(k)
    for k in range(2):
        d_branches.pull(k)

    d_att = dot(DB4[...].reshape(group, width), OW[...].reshape(4 * HEAD_DIM, width), 1, 1).astype(BF16)
    d_att = d_att.astype(F32).T.astype(BF16).reshape(2, 2, HEAD_DIM, group)
    DS[...] = d_att
    d_sem = {f: ids() for f in others}
    for flips in others:
        p = at(flips)
        send(DS.at[p["h"], p["y"]], DR.at[h, y], d_sem[flips], flips)
    DR[h, y] = DS[h, y]

    out_s.first()
    down_s.second()
    up_s.second()

    VG[6:8, :] = jnp.zeros((2, width), F32)
    picked = [spread_matrix(width, 32, j) for j in range(4)]

    def exact_pick(row, j):
        a = jnp.where(mine, VG[row : row + 1, :], 0.0)
        hi = a.astype(BF16)
        rest = a - hi.astype(F32)
        mid = rest.astype(BF16)
        low = (rest - mid.astype(F32)).astype(BF16)
        r = picked[j].astype(BF16)
        return dot(hi, r, 1, 1) + dot(mid, r, 1, 1) + dot(low, r, 1, 1)

    SG[...] = jnp.zeros_like(SG)
    SG[:, 0, :] = exact_pick(0, 2) + exact_pick(1, 3)
    SG[:, 1, :] = exact_pick(2, 0) + exact_pick(3, 1) + exact_pick(4, 2) + exact_pick(5, 3)
    for hp, yp, xp in itertools.product(range(2), repeat=3):
        r = hp * 4 + yp * 2 + xp
        SG[(s * 8 + hp * 4 + l * 2 + yp) * 2 + xp, 2:3, :] = UB[1:2, r * 128 : (r + 1) * 128]

    for flips in others:
        p = at(flips)
        wait(DR.at[p["h"], p["y"]], d_sem[flips], flips)
    for sp in range(2):
        j = s if sp == 0 else 1 - s
        for hp, lp, yp in itertools.product(range(2), repeat=3):
            part = DR[hp, yp, :, (sp * 2 + lp) * tokens : (sp * 2 + lp + 1) * tokens]
            at_tok = (hp * 4 + lp * 2 + yp) * tokens
            DAT[j, :, at_tok : at_tok + tokens] = part
            DA[j, at_tok : at_tok + tokens, :] = part.astype(F32).T.astype(BF16)

    def attend_back(j):
        DKV[...] = jnp.zeros_like(DKV)

        def body(i):
            cols = col_tile(i)
            q = QKVT[j, 0:64, cols] * jnp.asarray(scale, BF16)
            p = jnp.exp(dot(KN[j], q) - LSE[j, 0:1, cols])
            da = DAT[j, :, cols]
            delta = jnp.sum(da.astype(F32) * OT[j, :, cols], axis=0, keepdims=True)
            dp = dot(VN[j], da)
            ds = (p * (dp - delta) * scale).astype(BF16)
            DQT[j, :, cols] = dot(QKVT[j, 64:128, :], ds)
            DKV[0] += dot(ds, QN[j, cols, :])
            DKV[1] += dot(p.astype(BF16), DA[j, cols, :])

        loop(qtiles, body)
        dqt = DQT[j].astype(BF16).astype(F32)
        dq = dqt.T
        dk, dv = DKV[0].astype(BF16).astype(F32), DKV[1].astype(BF16).astype(F32)
        DQKV[j] = jnp.concatenate([dq, dk, dv], axis=1).astype(BF16)
        DQKVT[j, 0:64, :] = dqt.astype(BF16)
        DQKVT[j, 64:128, :] = dk.T.astype(BF16)
        DQKVT[j, 128:192, :] = dv.T.astype(BF16)
        return jnp.sum(dq, axis=0, keepdims=True), jnp.sum(dv, axis=0, keepdims=True)

    def input_tile(j, part, i):
        w = WH[pl.ds(pl.multiple_of(i * 4, 4), 4)].reshape(TILE, WH.shape[-1])[:, 0 : 3 * HEAD_DIM]
        rows = pl.ds(pl.multiple_of(part * (length // 2), length // 2), length // 2)
        return dot(DQKV[j, rows, :], w, 1, 1).reshape(2, 2, tokens, TILE)

    in_order = (0, 2, 1, 3)
    far, near = 1 - h, h
    ia, ib, ic, id_ = ({(p, i): ids() for p in range(2) for i in range(tiles)} for _ in range(4))

    def in_sent(i):
        return (C4T if i < tiles // 2 else N4T).at[:, :, :, :, pl.ds(i % 2 * TILE, TILE)]

    q1, v1 = attend_back(1)
    down_s.third()
    for p, part in enumerate((far, near)):
        for i in in_order:
            piece = in_sent(i).at[part]
            piece[...] = input_tile(1, part, i).astype(BF16)
            send(piece, IRA.at[i, part], ia[p, i], ("s",))
    q0, v0 = attend_back(0)
    to_x = Tiles(QSA, QRA, "x", range(tiles))

    def q_first(i):
        cols = col_tile(i)
        v = dot(DQKVT[0], X16[s, :, :, :, :, cols].reshape(length, TILE))
        v += dot(DQKVT[1], X16[1 - s, :, :, :, :, cols].reshape(length, TILE))
        v = v.T.reshape(2, 2, 2, 32, 3 * HEAD_DIM)
        for xp in range(2):
            QK[i, xp] = v[:, :, xp]
        QSA[i, :, :, :, 0 : 3 * HEAD_DIM] = QK[i, 1 - x].astype(BF16)
        to_x.send(i)

    def in_second(p):
        part = (far, near)[p]
        for i in in_order:
            wait(IRA.at[i, part], ia[p, i], ("s",))
            IK[i, part] = input_tile(0, part, i) + IRA[i, part].astype(F32)
            dim = "l" if i < tiles // 2 else "y"
            ISB[i, part] = (IK[i, part, 1 - l] if dim == "l" else IK[i, part, :, 1 - y]).astype(BF16)
            send(ISB.at[i, part], IRB.at[i, part], ib[p, i], (dim,))

    def in_third(p):
        part = (far, near)[p]
        for i in in_order:
            one, two = ("l", "y") if i < tiles // 2 else ("y", "l")
            wait(IRB.at[i, part], ib[p, i], (one,))
            IK[i, part, 0] = (IK[i, part, l] if one == "l" else IK[i, part, :, y]) + IRB[i, part].astype(F32)
            ISC[i, part] = IK[i, part, 0, 1 - here[two]].astype(BF16)
            send(ISC.at[i, part], IRC.at[i, part], ic[p, i], (two,))

    def in_summed(p, i):
        part = (far, near)[p]
        two = "y" if i < tiles // 2 else "l"
        wait(IRC.at[i, part], ic[p, i], (two,))
        return IK[i, part, 0, here[two]] + IRC[i, part].astype(F32)

    def q_second(i):
        to_x.wait(i)
        v = QK[i, x] + QRA[i, :, :, :, 0 : 3 * HEAD_DIM].astype(F32)
        QSB[i // 2, i % 2, :, :, :, 0 : 3 * HEAD_DIM] = v.astype(BF16)

    def piece_copy(j):
        to = (head + j) % 16
        return peer_copy(
            QSB.at[to // 8, (to // 4) % 2, (to // 2) % 2, to % 2], QG.at[head], (hss, hrs), 16 + j
        )

    in_second(0)
    in_second(1)
    up_s.third()
    out_s.second()
    loop(tiles, q_first)
    bq, bv = q0 + q1, v0 + v1
    for k in range(2):
        b = head * 2 + k
        lanes = slice(k * 32, k * 32 + 32)
        SG[b, 0:1, :] += jnp.concatenate([bq[:, lanes], bv[:, lanes], jnp.zeros((1, 64), F32)], axis=1)

    def grad_copy(j):
        return peer_copy(SG.at[pl.ds((head + j) % 16 * 2, 2)], RG.at[j], (hss, hrs), j)

    loop(15, lambda j: grad_copy(j + 1).start())
    RG[0] = SG[pl.ds(head * 2, 2)]
    in_third(0)
    out_s.third()
    loop(tiles, q_second)
    loop(15, lambda j: piece_copy(j + 1).start())
    QG[head] = QSB[s, h, l, y]
    for i in in_order:
        ISD[i] = in_summed(0, i).astype(BF16)
        send(ISD.at[i], IRD.at[i], id_[0, i], ("h",))
    in_third(1)
    down_s.last(downg_o)
    loop(15, lambda j: grad_copy(j + 1).wait_recv())
    small_sum = jnp.sum(RG[...], axis=0)
    SX[0:2] = small_sum
    x_sem = ids()
    send(SX.at[1 - x], RX, x_sem, ("x",))
    up_s.last(UF)
    uf_sem = {}
    for flips in (("s",), ("l",), ("s", "l")):
        p = at(flips)
        for hp in range(2):
            uf_sem[flips, hp] = ids()
            send(
                UF.at[pl.ds(pl.multiple_of((p["s"] * 2 + p["l"]) * 32, 32), 32), pl.ds(hp * 512, 512)],
                upg_o.at[:, quarter(s, hp, l)], uf_sem[flips, hp], flips,
            )
    for hp in range(2):
        upg_o[:, quarter(s, hp, l)] = UF[pl.ds(pl.multiple_of((s * 2 + l) * 32, 32), 32), hp * 512 : (hp + 1) * 512]
    out_s.last(outg_o)
    wait(RX, x_sem, ("x",))
    small_o[...] = SX[x] + RX[...]
    loop(15, lambda j: piece_copy(j + 1).wait_recv())
    for k in range(HEADS // 2):
        a, b = QG[2 * k].astype(F32), QG[2 * k + 1].astype(F32)
        for part in range(3):
            lanes = slice(part * 64, part * 64 + 64)
            to = part * width + k * 128
            qkvg_o[:, to : to + 128] = jnp.concatenate([a[:, lanes], b[:, lanes]], axis=1)
    for i in range(tiles):
        total = in_summed(1, i) + DSUM[:, i * TILE : (i + 1) * TILE]
        wait(IRD.at[i], id_[0, i], ("h",))
        ig_o[:, i * TILE : (i + 1) * TILE] = total + IRD[i].astype(F32)

    for flips in (("s",), ("l",), ("s", "l")):
        p = at(flips)
        for hp in range(2):
            wait(upg_o.at[:, quarter(p["s"], hp, p["l"])], uf_sem[flips, hp], flips)

    for d in sends:
        d.wait_send()

    def small_sent(j):
        for d in small_copy(j + 1, head):
            d.wait_send()
        grad_copy(j + 1).wait_send()

    loop(15, small_sent)
    loop(15, lambda j: piece_copy(j + 1).wait_send())


def hand_over(*refs):
    large, small, outs, sems = refs[:6], refs[6], refs[7:22], refs[22]
    copies = [pltpu.make_async_copy(a, b, sems.at[k]) for k, (a, b) in enumerate(zip(large, outs))]
    for c in copies:
        c.start()
    places = ((0, 0, 32), (0, 32, 32), (0, 64, 32), (2, 0, 128), (0, 96, 32), (1, 0, 32), (1, 32, 32), (1, 64, 32), (1, 96, 32))
    for ref, (row, lane, count) in zip(outs[6:], places):
        ref[...] = small[row : row + 1, lane : lane + count]
    for c in copies:
        c.wait()


def on_block(
    tokens, qkv_weight, out_weight, up_weight, down_weight,
    query_bias, value_bias, out_bias, up_bias, down_bias,
    norm1_gain, norm1_bias, norm2_gain, norm2_bias, cotangent,
):
    n, width = tokens.shape[1], tokens.shape[2]
    hidden = up_weight.shape[1] // 4
    group = 4 * n
    length = 8 * n
    tiles = width // TILE
    vectors = [
        v.reshape(1, -1)
        for v in (query_bias, value_bias, out_bias, up_bias, down_bias, norm1_gain, norm1_bias, norm2_gain, norm2_bias)
    ]

    def b(*shape):
        return pltpu.VMEM(shape, BF16)

    def f(*shape):
        return pltpu.VMEM(shape, F32)

    group_bufs = [b(2, tiles, 2, n // 2, TILE), b(2, tiles, 2, n // 2, TILE), b(2, tiles, n // 2, TILE), b(2, tiles, n // 2, TILE)]

    def scatter_bufs(rows):
        return [
            b(tiles, 2, 2, rows, TILE), b(tiles, 2, 2, rows, TILE),
            b(tiles, 2, rows, TILE), b(tiles, 2, rows, TILE),
            b(tiles, rows, TILE), b(tiles, rows, TILE),
            f(tiles, 2, 2, rows, TILE),
        ]

    sem = pltpu.SemaphoreType.DMA
    scratch = [
        f(8, 128), b(2, 2, 2, 2, n, width), b(HEADS, 32, 256), b(HEADS, 2, 32, 256), f(HEADS, 2, 8, 128),
        b(2, 2, 2, 32, width), b(2, 2, 2, 2, 2, 32, hidden), b(2, 2, 2, 128, width),
        b(2, length, 64), b(2, length, 64), b(2, length, 64), b(2, 192, length), f(2, 64, length), b(2, 64, length),
        f(2, 8, length), b(4, 2, 64, group // 2), b(2, 2, 64, group), b(2, 2, n, 256),
        *group_bufs, *group_bufs, f(2, tiles, 2, n // 2, TILE),
        b(2, 2, n, width), b(2, 2, 2, 128, group), b(2, 2, n, hidden), b(2, 2, 2, 128, group), f(2, 2, n, hidden),
        b(2, 2, n, width),
        f(n, width), f(n, width), f(n, width),
        b(2, 2, 64, group), b(2, 2, 64, group), b(2, length, 64), b(2, 64, length), f(2, length, 64), f(2, 64, length),
        b(2, length, 192), b(2, 192, length),
        *scatter_bufs(128), f(128, width),
        *scatter_bufs(128),
        *scatter_bufs(32),
        b(tiles, 2, 2, 2, n, TILE), b(tiles, 2, 2, n, TILE), b(tiles, 2, 2, n, TILE),
        b(tiles, 2, n, TILE), b(tiles, 2, n, TILE), b(tiles, n, TILE), b(tiles, n, TILE), f(tiles, 2, 2, 2, n, TILE),
        b(tiles, 2, 2, 32, 256), b(tiles, 2, 2, 32, 256), f(tiles, 2, 2, 2, 32, 192), b(2, 2, 2, 2, 32, 256), b(HEADS, 32, 256),
        f(8, width), f(8, hidden), f(8, width), f(32, 8, 128), f(HEADS, 2, 8, 128), f(2, 8, 128), f(8, 128),
        sem((300,)), sem((300,)), sem((16,)), sem((16,)), sem((16,)), sem((16,)), sem((32,)), sem((32,)),
    ]
    vmem = pl.BlockSpec(memory_space=pltpu.VMEM)
    shapes = [
        jax.ShapeDtypeStruct((n, width), BF16),
        jax.ShapeDtypeStruct((n, width), F32),
        jax.ShapeDtypeStruct((32, 3 * width), F32),
        jax.ShapeDtypeStruct((32, width), F32),
        jax.ShapeDtypeStruct((32, 4 * hidden), F32),
        jax.ShapeDtypeStruct((128, width), F32),
        jax.ShapeDtypeStruct((8, 128), F32),
    ]
    results = pl.pallas_call(
        layer_kernel,
        out_shape=shapes,
        in_specs=[vmem] * 15,
        out_specs=[vmem] * 7,
        scratch_shapes=scratch,
        compiler_params=pltpu.CompilerParams(
            collective_id=0, has_side_effects=True, vmem_limit_bytes=63 * 2**20
        ),
        name="layer",
    )(tokens[0], qkv_weight, out_weight, up_weight, down_weight, *vectors, cotangent[0])
    lengths = [v.shape[1] for v in vectors]
    everywhere = pl.BlockSpec(memory_space=pl.ANY)
    done = pl.pallas_call(
        hand_over,
        out_shape=shapes[:6] + [jax.ShapeDtypeStruct((1, k), F32) for k in lengths],
        in_specs=[vmem] * 7,
        out_specs=[everywhere] * 6 + [vmem] * 9,
        scratch_shapes=[sem((6,))],
        name="results",
    )(*results)
    return (
        done[0][None], done[1][None], *done[2:6], *(v.reshape(-1) for v in done[6:]),
    )


def solution(mesh):
    placed = (
        P(("seq", "fsdp"), "ctx", None),
        P(("seq", "ctx", "fsdp"), None),
        P(("seq", "ctx", "fsdp"), None),
        P(("seq", "ctx", "fsdp"), None),
        P(("seq", "ctx", "fsdp"), None),
        P(("seq", "ctx", "fsdp")),
        P(("seq", "ctx", "fsdp")),
        P(("seq", "ctx", "fsdp")),
        P(("seq", "ctx", "fsdp")),
        P(("seq", "ctx", "fsdp")),
        P(("seq", "ctx", "fsdp")),
        P(("seq", "ctx", "fsdp")),
        P(("seq", "ctx", "fsdp")),
        P(("seq", "ctx", "fsdp")),
        P(("seq", "fsdp"), "ctx", None),
    )
    fast = dict(mesh.shape) == {"seq": 2, "ctx": 8, "fsdp": 2}
    return jax.shard_map(
        on_block if fast else on_device,
        mesh=mesh,
        in_specs=placed,
        out_specs=(
            P(("seq", "fsdp"), "ctx", None),
            P(("seq", "fsdp"), "ctx", None),
            P(("seq", "ctx", "fsdp"), None),
            P(("seq", "ctx", "fsdp"), None),
            P(("seq", "ctx", "fsdp"), None),
            P(("seq", "ctx", "fsdp"), None),
            P(("seq", "ctx", "fsdp")),
            P(("seq", "ctx", "fsdp")),
            P(("seq", "ctx", "fsdp")),
            P(("seq", "ctx", "fsdp")),
            P(("seq", "ctx", "fsdp")),
            P(("seq", "ctx", "fsdp")),
            P(("seq", "ctx", "fsdp")),
            P(("seq", "ctx", "fsdp")),
            P(("seq", "ctx", "fsdp")),
        ),
        check_vma=False,
    )
```

```python
import functools
import itertools
import math

import jax
import jax.numpy as jnp
from jax import lax
from jax.experimental import pallas as pl
from jax.experimental.pallas import tpu as pltpu
from jax.sharding import PartitionSpec as P

HEADS = 16
HEAD_DIM = 64


epsilon = 1e-05
MESH = pl.DeviceIdType.MESH
F32 = jnp.float32
BF16 = jnp.bfloat16
TILE = 256


def split_blocks(piece):
    rows = piece.shape[0]
    block = math.gcd(rows, 512)
    return (piece.reshape(rows // block, block, HEADS, HEAD_DIM), block)


def norm_forward(values, gain, shift):
    centered = values - jnp.mean(values, axis=-1, keepdims=True)
    recip = lax.rsqrt(jnp.mean(centered * centered, axis=-1, keepdims=True) + epsilon)
    normal = centered * recip
    return (normal * gain + shift, normal, recip)


def norm_backward(upstream, normal, recip, gain):
    gain_grad = jnp.sum(upstream * normal, axis=0)
    shift_grad = jnp.sum(upstream, axis=0)
    scaled = upstream * gain
    inner = (
        scaled
        - jnp.mean(scaled, axis=-1, keepdims=True)
        - normal * jnp.mean(scaled * normal, axis=-1, keepdims=True)
    )
    return (recip * inner, gain_grad, shift_grad)


def matmul(left_neighbor, right_neighbor):
    return jnp.dot(left_neighbor, right_neighbor, preferred_element_type=jnp.float32)


def on_device(
    tokens,
    qkv_weight,
    out_weight,
    up_weight,
    down_weight,
    query_bias,
    value_bias,
    out_bias,
    up_bias,
    down_bias,
    norm1_gain,
    norm1_bias,
    norm2_gain,
    norm2_bias,
    cotangent,
):
    gathered = (
        lax.all_gather(qkv_weight, ("seq", "ctx", "fsdp"), axis=0, tiled=True),
        lax.all_gather(out_weight, ("seq", "ctx", "fsdp"), axis=0, tiled=True),
        lax.all_gather(up_weight, ("seq", "ctx", "fsdp"), axis=0, tiled=True),
        lax.all_gather(down_weight, ("seq", "ctx", "fsdp"), axis=0, tiled=True),
        lax.all_gather(query_bias, ("seq", "ctx", "fsdp"), axis=0, tiled=True),
        lax.all_gather(value_bias, ("seq", "ctx", "fsdp"), axis=0, tiled=True),
        lax.all_gather(out_bias, ("seq", "ctx", "fsdp"), axis=0, tiled=True),
        lax.all_gather(up_bias, ("seq", "ctx", "fsdp"), axis=0, tiled=True),
        lax.all_gather(down_bias, ("seq", "ctx", "fsdp"), axis=0, tiled=True),
        lax.all_gather(norm1_gain, ("seq", "ctx", "fsdp"), axis=0, tiled=True),
        lax.all_gather(norm1_bias, ("seq", "ctx", "fsdp"), axis=0, tiled=True),
        lax.all_gather(norm2_gain, ("seq", "ctx", "fsdp"), axis=0, tiled=True),
        lax.all_gather(norm2_bias, ("seq", "ctx", "fsdp"), axis=0, tiled=True),
    )
    qkv_full, out_full, up_full, down_full = (gathered[0], gathered[1], gathered[2], gathered[3])
    small = tuple((item.astype(jnp.float32) for item in gathered[4:]))
    q_shift, v_shift, o_shift, u_shift, d_shift, gain_one, shift_one, gain_two, shift_two = small
    scale = HEAD_DIM ** (-0.5)
    inputs = tokens[0]
    rows = inputs.shape[0]
    width = inputs.shape[1]
    joined_bias = jnp.concatenate([q_shift, jnp.zeros_like(q_shift), v_shift])
    qkv_low = (matmul(inputs, qkv_full) + joined_bias).astype(jnp.bfloat16)
    queries = qkv_low[:, :width].reshape(rows, HEADS, HEAD_DIM)
    keys_own = qkv_low[:, width : 2 * width]
    values_own = qkv_low[:, 2 * width :]
    start_state = (
        jnp.full((HEADS, rows), -1e30, jnp.float32),
        jnp.zeros((HEADS, rows), jnp.float32),
        jnp.zeros((rows, HEADS, HEAD_DIM), jnp.float32),
    )
    piece = (
        lax.all_gather(keys_own, "ctx", axis=0, tiled=True),
        lax.all_gather(values_own, "ctx", axis=0, tiled=True),
    )
    key_blocks, block = split_blocks(piece[0])
    value_blocks, block = split_blocks(piece[1])

    def inner(state, pair):
        run_max, run_sum, accum = state
        key_tile_rows, value_block = pair
        scores = (
            jnp.einsum("qhe,khe->hqk", queries, key_tile_rows, preferred_element_type=jnp.float32)
            * scale
        )
        new_max = jnp.maximum(run_max, jnp.max(scores, axis=-1))
        factor = jnp.exp(run_max - new_max)
        weights = jnp.exp(scores - new_max[..., None])
        run_sum = run_sum * factor + jnp.sum(weights, axis=-1)
        accum = accum * factor.T[..., None] + jnp.einsum(
            "hqk,khe->qhe",
            weights.astype(jnp.bfloat16),
            value_block,
            preferred_element_type=jnp.float32,
        )
        return ((new_max, run_sum, accum), None)

    result, unused = lax.scan(inner, start_state, (key_blocks, value_blocks))
    run_max, run_sum, accum = result
    attended = accum / run_sum.T[..., None]
    log_total = run_max + jnp.log(run_sum)
    attended_low = attended.reshape(rows, width).astype(jnp.bfloat16)
    first_sum = inputs.astype(jnp.float32) + matmul(attended_low, out_full) + o_shift
    first_norm, normal_one, recip_one = norm_forward(first_sum, gain_one, shift_one)
    normed_low = first_norm.astype(jnp.bfloat16)
    hidden_pre = matmul(normed_low, up_full) + u_shift
    activated_full, gelu_pull = jax.vjp(lambda pre: jax.nn.gelu(pre, approximate=False), hidden_pre)
    activated = activated_full.astype(jnp.bfloat16)
    second_sum = first_norm + matmul(activated, down_full) + d_shift
    final, normal_two, recip_two = norm_forward(second_sum, gain_two, shift_two)
    upstream = cotangent[0].astype(jnp.float32)
    d_second, gain_two_grad, shift_two_grad = norm_backward(
        upstream, normal_two, recip_two, gain_two
    )
    d_feed = d_second.astype(jnp.bfloat16)
    down_grad = matmul(activated.T, d_feed)
    down_bias_grad = jnp.sum(d_feed.astype(jnp.float32), axis=0)
    d_hidden = gelu_pull(matmul(d_feed, down_full.T))[0].astype(jnp.bfloat16)
    up_grad = matmul(normed_low.T, d_hidden)
    up_bias_grad = jnp.sum(d_hidden.astype(jnp.float32), axis=0)
    first_input_gradient = d_second + matmul(d_hidden, up_full.T)
    d_sum_one, gain_one_grad, first_shift_gradient = norm_backward(
        first_input_gradient, normal_one, recip_one, gain_one
    )
    d_branch = d_sum_one.astype(jnp.bfloat16)
    out_grad = matmul(attended_low.T, d_branch)
    out_bias_grad = jnp.sum(d_branch.astype(jnp.float32), axis=0)
    d_attended = matmul(d_branch, out_full.T).astype(jnp.bfloat16).reshape(rows, HEADS, HEAD_DIM)
    delta = jnp.sum(d_attended.astype(jnp.float32) * attended, axis=-1).T
    total_rows = rows * lax.axis_size("ctx")
    zero_query = jnp.zeros((rows, HEADS, HEAD_DIM), jnp.float32)
    start_back = (zero_query, jnp.zeros((total_rows, 2 * width), jnp.float32))
    piece = (
        lax.all_gather(keys_own, "ctx", axis=0, tiled=True),
        lax.all_gather(values_own, "ctx", axis=0, tiled=True),
    )
    key_blocks, block = split_blocks(piece[0])
    value_blocks, block = split_blocks(piece[1])
    counter = jnp.arange(key_blocks.shape[0], dtype=jnp.int32)

    def inner(state, triple):
        key_tile_rows, value_block, number = triple
        scores = (
            jnp.einsum("qhe,khe->hqk", queries, key_tile_rows, preferred_element_type=jnp.float32)
            * scale
        )
        weights = jnp.exp(scores - log_total[..., None])
        d_probs = jnp.einsum(
            "qhe,khe->hqk", d_attended, value_block, preferred_element_type=jnp.float32
        )
        d_scores = (weights * (d_probs - delta[..., None]) * scale).astype(jnp.bfloat16)
        d_query = state[0] + jnp.einsum(
            "hqk,khe->qhe", d_scores, key_tile_rows, preferred_element_type=jnp.float32
        )
        d_key = jnp.einsum(
            "hqk,qhe->khe", d_scores, queries, preferred_element_type=jnp.float32
        ).reshape(block, width)
        d_value = jnp.einsum(
            "hqk,qhe->khe",
            weights.astype(jnp.bfloat16),
            d_attended,
            preferred_element_type=jnp.float32,
        ).reshape(block, width)
        offset = number * block
        current = lax.dynamic_slice_in_dim(state[1], offset, block, 0)
        updated = lax.dynamic_update_slice_in_dim(
            state[1], current + jnp.concatenate([d_key, d_value], axis=1), offset, 0
        )
        return ((d_query, updated), None)

    result, unused = lax.scan(inner, start_back, (key_blocks, value_blocks, counter))
    d_query = result[0].reshape(rows, width)
    summed = lax.psum_scatter(result[1], "ctx", scatter_dimension=0, tiled=True)
    d_key = summed[:, :width]
    d_value = summed[:, width:]
    d_qkv = jnp.concatenate([d_query, d_key, d_value], axis=1).astype(jnp.bfloat16)
    qkv_grad = matmul(inputs.T, d_qkv)
    d_qkv_wide = d_qkv.astype(jnp.float32)
    query_bias_gradient = jnp.sum(d_qkv_wide[:, :width], axis=0)
    value_bias_grad = jnp.sum(d_qkv_wide[:, 2 * width :], axis=0)
    input_grad = matmul(d_qkv, qkv_full.T) + d_sum_one
    sharded = (
        lax.psum_scatter(qkv_grad, ("seq", "ctx", "fsdp"), scatter_dimension=0, tiled=True),
        lax.psum_scatter(out_grad, ("seq", "ctx", "fsdp"), scatter_dimension=0, tiled=True),
        lax.psum_scatter(up_grad, ("seq", "ctx", "fsdp"), scatter_dimension=0, tiled=True),
        lax.psum_scatter(down_grad, ("seq", "ctx", "fsdp"), scatter_dimension=0, tiled=True),
        lax.psum_scatter(
            query_bias_gradient, ("seq", "ctx", "fsdp"), scatter_dimension=0, tiled=True
        ),
        lax.psum_scatter(value_bias_grad, ("seq", "ctx", "fsdp"), scatter_dimension=0, tiled=True),
        lax.psum_scatter(out_bias_grad, ("seq", "ctx", "fsdp"), scatter_dimension=0, tiled=True),
        lax.psum_scatter(up_bias_grad, ("seq", "ctx", "fsdp"), scatter_dimension=0, tiled=True),
        lax.psum_scatter(down_bias_grad, ("seq", "ctx", "fsdp"), scatter_dimension=0, tiled=True),
        lax.psum_scatter(gain_one_grad, ("seq", "ctx", "fsdp"), scatter_dimension=0, tiled=True),
        lax.psum_scatter(
            first_shift_gradient, ("seq", "ctx", "fsdp"), scatter_dimension=0, tiled=True
        ),
        lax.psum_scatter(gain_two_grad, ("seq", "ctx", "fsdp"), scatter_dimension=0, tiled=True),
        lax.psum_scatter(shift_two_grad, ("seq", "ctx", "fsdp"), scatter_dimension=0, tiled=True),
    )
    return (
        final.astype(jnp.bfloat16)[None],
        input_grad[None],
        sharded[0],
        sharded[1],
        sharded[2],
        sharded[3],
        sharded[4],
        sharded[5],
        sharded[6],
        sharded[7],
        sharded[8],
        sharded[9],
        sharded[10],
        sharded[11],
        sharded[12],
    )


def dot(left, right, left_dim=1, right_dim=0):
    return lax.dot_general(
        left, right, (((left_dim,), (right_dim,)), ((), ())), preferred_element_type=F32
    )


def loop(count, body):
    def step(i, carry):
        body(i)
        return carry

    lax.fori_loop(0, count, step, 0)


def spread_matrix(width, piece, at):
    lane = lax.broadcasted_iota(jnp.int32, (128, width), 0)
    column = lax.broadcasted_iota(jnp.int32, (128, width), 1)
    return jnp.where(lane == at * piece + column % piece, 1.0, 0.0)


def own_columns(blocks, width):
    row = lax.broadcasted_iota(jnp.int32, (blocks, width), 0)
    column = lax.broadcasted_iota(jnp.int32, (blocks, width), 1)
    return column // (width // blocks), row


def layer_kernel(
    tok, qkvw, outw, upw, downw, qb, vb, ob, ub, db, g1, b1, g2, b2, cot,
    out_o, ig_o, qkvg_o, outg_o, upg_o, downg_o, small_o,
    PK, X16, WP, WH, G, OW, UW, DW,
    QN, KN, VN, QKVT, OT, OTB, LSE, AS, AT, A4,
    R1A, R1B, R1C, R1D, R2A, R2B, R2C, R2D, KR,
    N4, N4T, C4, C4T, GP, DF4,
    FN, NORM1, DSEC,
    DS, DR, DA, DAT, DKV, DQT, DQKV, DQKVT,
    USA, URA, USB, URB, USC, URC, UK, UF,
    DSA, DRA, DSB, DRB, DSC, DRC, DK,
    OSA, ORA, OSB, ORB, OSC, ORC, OK,
    IRA, ISB, IRB, ISC, IRC, ISD, IRD, IK,
    QSA, QRA, QK, QSB, QG,
    VEC, UB, VG, SG, RG, SX, RX,
    ssem, rsem, wss, wrs, gss, grs, hss, hrs,
):
    s = lax.axis_index("seq")
    c = lax.axis_index("ctx")
    x = lax.axis_index("fsdp")
    h, l, y = c // 4, (c // 2) % 2, c % 2
    here = {"s": s, "h": h, "l": l, "y": y, "x": x}
    me = s * 16 + c * 2 + x
    head = s * 8 + c
    width = tok.shape[1]
    tiles = width // TILE
    counter = itertools.count()
    sends = []

    def at(flips):
        return {k: (1 - v if k in flips else v) for k, v in here.items()}

    def device(flips):
        p = at(flips)
        return {"seq": p["s"], "ctx": p["h"] * 4 + p["l"] * 2 + p["y"], "fsdp": p["x"]}

    def ids(n=1):
        return [next(counter) for _ in range(n)][0]

    def copy(src, dst, sem, flips):
        return pltpu.make_async_remote_copy(
            src_ref=src, dst_ref=dst, send_sem=ssem.at[sem], recv_sem=rsem.at[sem],
            device_id=device(flips), device_id_type=MESH,
        )

    def settle(since):
        for d in sends[since:]:
            d.wait_send()
        del sends[since:]

    def send(src, dst, sem, flips):
        d = copy(src, dst, sem, flips)
        d.start()
        sends.append(d)

    def wait(ref, sem, flips):
        copy(ref, ref, sem, flips).wait_recv()

    class Tiles:
        def __init__(self, src, dst, dim, of):
            self.src, self.dst, self.dim, self.of = src, dst, dim, of
            self.base = [ids() for _ in of][0] - of[0]
            self.listed = False

        def each(self, i):
            return copy(self.src.at[i], self.dst.at[i], self.base + i, (self.dim,))

        def send(self, i):
            self.each(i).start()
            if not self.listed:
                sends.append(self)
                self.listed = True

        def wait(self, i):
            self.each(i).wait_recv()

        def wait_send(self):
            for i in self.of:
                self.each(i).wait_send()

    class Gather:
        def __init__(self, order, block):
            self.order, self.block, self.sem = order, block, {}
            for n in range(1, len(order) + 1):
                for k in itertools.combinations(order, n):
                    self.sem[frozenset(k)] = ids()

        def push(self, *have, along=None):
            have = frozenset(have)
            last = max([self.order.index(d) for d in have], default=-1)
            for d in self.order[last + 1 :]:
                if along and d not in along:
                    continue
                ref = self.block(at(have))
                send(ref, ref, self.sem[have | {d}], (d,))

        def pull(self, *have):
            have = frozenset(have)
            last = max(have, key=self.order.index)
            wait(self.block(at(have)), self.sem[have], (last,))

        def pass_on(self, *have):
            self.pull(*have)
            self.push(*have)

    barrier = pltpu.get_barrier_semaphore()

    def peer(j):
        to = (head + j) % 16
        return {"seq": to // 8, "ctx": to % 8, "fsdp": x}

    def peer_copy(src, dst, sems, j):
        return pltpu.make_async_remote_copy(
            src_ref=src, dst_ref=dst, send_sem=sems[0].at[j], recv_sem=sems[1].at[j],
            device_id=peer(j % 16), device_id_type=MESH)

    loop(15, lambda j: pl.semaphore_signal(barrier, inc=1, device_id=peer(j + 1), device_id_type=MESH))
    pl.semaphore_signal(barrier, inc=1, device_id=device("x"), device_id_type=MESH)

    X16[s, h, l, y] = tok[...]
    PK[...] = jnp.zeros_like(PK)
    for k, vector in enumerate((qb, vb, ob, db, g1, b1, g2, b2)):
        PK[k // 4, k % 4 * 32 : k % 4 * 32 + 32] = vector[0, :].astype(F32)
    PK[2, :] = ub[0, :].astype(F32)
    for k in range(HEADS):
        parts = [qkvw[:, j * width + k * HEAD_DIM : j * width + (k + 1) * HEAD_DIM] for j in range(3)]
        WP[k, :, 0 : 3 * HEAD_DIM] = jnp.concatenate(parts, axis=1)
    WH[head, x] = WP[head]
    G[head, x] = PK[...]
    OW[h, y, x] = outw[...]
    DW[h, y, x] = downw[...]

    def quarter(sp, hp, lp):
        return pl.ds(pl.multiple_of(sp * 2048 + hp * 1024 + lp * 512, 512), 512)

    for hp in range(2):
        UW[s, h, l, y, x, :, hp * 512 : (hp + 1) * 512] = upw[:, quarter(s, hp, l)]

    pl.semaphore_wait(barrier, 16)

    half = width // 2

    def token_block(k):
        return lambda p: X16.at[p["s"], p["h"], p["l"], p["y"], :, pl.ds(k * half, half)]

    xg = [Gather("hlys", token_block(0)), Gather("hyls", token_block(1))]
    for g in xg:
        g.push()

    def small_copy(j, dst):
        return [
            peer_copy(WP.at[(head + j) % 16], WH.at[dst, x], (wss, wrs), j),
            peer_copy(PK, G.at[dst, x], (gss, grs), j),
        ]

    loop(15, lambda j: [d.start() for d in small_copy(j + 1, head)])

    up_sem = {}
    for flips in (("s",), ("l",), ("s", "l")):
        p = at(flips)
        for hp in range(2):
            up_sem[flips, hp] = ids()
            send(
                upw.at[:, quarter(p["s"], hp, p["l"])],
                UW.at[s, h, l, y, x, :, pl.ds(hp * 512, 512)],
                up_sem[flips, hp], flips,
            )

    def up_block(k):
        cols = (pl.ds(0, UW.shape[-1] // 2), pl.ds(UW.shape[-1] // 2, UW.shape[-1] // 2))[k]
        return lambda p: UW.at[:, p["h"], :, p["y"], p["x"], :, cols]

    def down_block(k):
        rows = (pl.ds(0, DW.shape[-2] // 2), pl.ds(DW.shape[-2] // 2, DW.shape[-2] // 2))[k]
        return lambda p: DW.at[p["h"], p["y"], p["x"], rows]

    og = Gather("hyx", lambda p: OW.at[p["h"], p["y"], p["x"]])
    ug = [Gather("hyx", up_block(0)), Gather("hxy", up_block(1))]
    dg = [Gather("hyx", down_block(0)), Gather("hxy", down_block(1))]
    for g in dg:
        g.push(along="x")
    og.push()

    for g in xg:
        g.pass_on("h")
    for flips in (("s",), ("l",), ("s", "l")):
        p = at(flips)
        for hp in range(2):
            wait(UW.at[p["s"], h, p["l"], y, x, :, pl.ds(hp * 512, 512)], up_sem[flips, hp], flips)
    for g in ug:
        g.push()
    xg[0].pass_on("l")
    xg[1].pass_on("y")

    def wait_small(j):
        for d in small_copy(j + 1, (head + 15 - j) % 16):
            d.wait_recv()

    loop(15, wait_small)
    small_sem = [ids(), ids()]
    send(WH.at[:, x], WH.at[:, x], small_sem[0], ("x",))
    send(G.at[:, x], G.at[:, x], small_sem[1], ("x",))
    xg[0].pass_on("h", "l")
    xg[1].pass_on("h", "y")
    og.pass_on("h")
    og.pass_on("y")
    og.pass_on("h", "y")
    for a, b in (("y", "l"), ("l", "y")):
        g = xg[0] if a == "y" else xg[1]
        for have in ((a,), ("h", a), (b, a), ("h", b, a)):
            g.pass_on(*have)

    for g in dg:
        g.push(along="hy")
    wait(WH.at[:, 1 - x], small_sem[0], ("x",))
    wait(G.at[:, 1 - x], small_sem[1], ("x",))

    spread = [spread_matrix(width, 32, j).astype(BF16) for j in range(4)]
    block_of, row_at = own_columns(32, width)
    mine = block_of == row_at
    arrived = block_of == row_at % 16 * 2 + row_at // 16
    for row, j, to in ((0, 2, 0), (0, 3, 1), (1, 0, 2), (1, 1, 3), (1, 2, 4), (1, 3, 5)):
        rows = jnp.concatenate([G[:, 0, row, :], G[:, 1, row, :]], axis=0).astype(BF16)
        VEC[to : to + 1, :] = jnp.sum(jnp.where(arrived, dot(rows, spread[j]), 0.0), axis=0, keepdims=True)
    for hp, yp, xp in itertools.product(range(2), repeat=3):
        r = hp * 4 + yp * 2 + xp
        UB[0:1, r * 128 : (r + 1) * 128] = G[s * 8 + hp * 4 + l * 2 + yp, xp, 2:3, :]
    out_bias, down_bias = VEC[0:1, :], VEC[1:2, :]
    gain_one, shift_one, gain_two, shift_two = (VEC[k : k + 1, :] for k in range(2, 6))
    first, second = G[head, 0, 0:1, :], G[head, 1, 0:1, :]
    head_bias = jnp.concatenate(
        [first[:, 0:32], second[:, 0:32], jnp.zeros((1, 64), F32), first[:, 32:64], second[:, 32:64]], axis=1
    )
    head_weight = WH[...].reshape(width, WH.shape[-1])[:, 0 : 3 * HEAD_DIM]

    length = 8 * tok.shape[0]
    qtiles = length // TILE
    scale = HEAD_DIM ** (-0.5)
    DH4, DB4, DSUM = C4, N4, FN

    def project(j):
        sp = s if j == 0 else 1 - s

        def body(i):
            hl = X16[sp, i // 2, i % 2].reshape(TILE, width)
            res = (dot(hl, head_weight) + head_bias).astype(BF16).astype(F32)
            rows = pl.ds(pl.multiple_of(i * TILE, TILE), TILE)
            QN[j, rows, :] = res[:, 0:64].astype(BF16)
            KN[j, rows, :] = res[:, 64:128].astype(BF16)
            VN[j, rows, :] = res[:, 128:192].astype(BF16)
            QKVT[j, :, rows] = res.T.astype(BF16)

        loop(qtiles, body)

    def attend(j):
        def body(i):
            cols = pl.ds(pl.multiple_of(i * TILE, TILE), TILE)
            q = QKVT[j, 0:64, cols] * jnp.asarray(scale, BF16)
            st = dot(KN[j], q)
            top = jnp.max(st, axis=0, keepdims=True)
            e = jnp.exp(st - top)
            total = jnp.sum(e, axis=0, keepdims=True)
            o = dot(QKVT[j, 128:192, :], e.astype(BF16)) / total
            OT[j, :, cols] = o
            OTB[j, :, cols] = o.astype(BF16)
            LSE[j, 0:1, cols] = top + jnp.log(total)

        loop(qtiles, body)

    tokens = tok.shape[0]

    def tok_cols(hp, lp, yp):
        return pl.ds(pl.multiple_of((hp * 4 + lp * 2 + yp) * tokens, tokens), tokens)

    others = (("h",), ("y",), ("h", "y"))
    a_sem = {(f, j): ids() for f in others for j in range(2)}

    def seq_cols(j):
        sp = s if j == 0 else 1 - s
        return pl.ds(pl.multiple_of(sp * 2 * tokens, 2 * tokens), 2 * tokens)

    def hand_out(j):
        for k, flips in enumerate(((),) + others):
            p = at(flips)
            piece = jnp.concatenate([OTB[j, :, tok_cols(p["h"], lp, p["y"])] for lp in range(2)], axis=1)
            if flips:
                AS[k, j] = piece
                send(AS.at[k, j], AT.at[h, y, :, seq_cols(j)], a_sem[flips, j], flips)
            else:
                AT[h, y, :, seq_cols(j)] = piece

    project(0)
    attend(0)
    hand_out(0)
    for g in ug:
        g.pass_on("h")
    ug[0].pass_on("y")
    ug[1].pass_on("x")
    for have in (("s",), ("h", "s"), ("l", "s"), ("h", "l", "s"), ("y", "s"), ("h", "y", "s"), ("l", "y", "s"), ("h", "l", "y", "s")):
        for g in xg:
            g.pull(*have)
    project(1)
    attend(1)
    hand_out(1)
    ug[0].pass_on("h", "y")
    ug[1].pass_on("h", "x")
    for g in dg:
        g.pass_on("h")
    for have in (("x",), ("h", "x"), ("y", "x"), ("h", "y", "x")):
        og.pull(*have)
    for flips in others:
        p = at(flips)
        for j in range(2):
            wait(AT.at[p["h"], p["y"], :, seq_cols(j)], a_sem[flips, j], flips)

    group = 4 * tokens
    half_n = tokens // 2
    A4[...] = AT[...].reshape(4 * HEAD_DIM, group).astype(F32).T.astype(BF16).reshape(A4.shape)

    def rows_of(k):
        return slice(k * half_n, (k + 1) * half_n)

    def half_rows(ref, k):
        return ref[:, :, rows_of(k), :].reshape(4 * half_n, ref.shape[-1])

    def core_rows(ref, k, sp):
        return ref[sp, :, rows_of(k), :].reshape(2 * half_n, ref.shape[-1])

    class GroupSum:
        def __init__(self, bufs, ref, product):
            self.sa, self.ra, self.sb, self.rb = bufs
            self.ref, self.product = ref, product
            self.to_core = [Tiles(self.sa.at[k], self.ra.at[k], "s", range(tiles)) for k in range(2)]
            self.to_pair = [Tiles(self.sb.at[k], self.rb.at[k], "l", range(tiles)) for k in range(2)]

        def start(self, k):
            def body(i):
                left = jnp.concatenate([core_rows(self.ref, k, 1 - s), core_rows(self.ref, k, s)], axis=0)
                v = self.product(left, i).reshape(2, 2, half_n, TILE)
                self.sa[k, i] = v[0].astype(BF16)
                self.to_core[k].send(i)
                KR[k, i] = v[1]

            loop(tiles, body)

        def relay(self, k):
            def body(i):
                self.to_core[k].wait(i)
                KR[k, i] += self.ra[k, i].astype(F32)
                self.sb[k, i] = KR[k, i, 1 - l].astype(BF16)
                self.to_pair[k].send(i)

            loop(tiles, body)

        def finish(self, k):
            for i in range(tiles):
                self.to_pair[k].wait(i)
            return jnp.concatenate([KR[k, i, l] + self.rb[k, i].astype(F32) for i in range(tiles)], axis=1)

    class GroupGather:
        def __init__(self, ref):
            self.ref = ref
            self.half = [
                Gather("ls", lambda p, k=k: ref.at[p["s"], p["l"], pl.ds(k * half_n, half_n)]) for k in range(2)
            ]

        def push(self, k, value):
            self.ref[s, l, rows_of(k)] = value
            self.half[k].push()

        def relay(self, k):
            self.half[k].pass_on("l")

        def pull(self, k):
            self.half[k].pull("s")
            self.half[k].pull("l", "s")

    def col_tile(i):
        return pl.ds(pl.multiple_of(i * TILE, TILE), TILE)

    def norm_forward(values, gain, shift):
        centered = values - jnp.mean(values, axis=-1, keepdims=True)
        recip = lax.rsqrt(jnp.mean(centered * centered, axis=-1, keepdims=True) + epsilon)
        normal = centered * recip
        return normal * gain + shift, normal, recip

    def norm_backward(upstream, normal, recip, gain):
        gain_grad = jnp.sum(upstream * normal, axis=0, keepdims=True)
        shift_grad = jnp.sum(upstream, axis=0, keepdims=True)
        scaled = upstream * gain
        inner = (
            scaled
            - jnp.mean(scaled, axis=-1, keepdims=True)
            - normal * jnp.mean(scaled * normal, axis=-1, keepdims=True)
        )
        return recip * inner, gain_grad, shift_grad

    def add_vectors(k, first_row, *rows):
        for at_row, row in zip(first_row, rows):
            VG[at_row : at_row + 1, :] = row if k == 0 else VG[at_row : at_row + 1, :] + row

    mark = len(sends)
    branch = GroupSum(
        (R1A, R1B, R1C, R1D), A4,
        lambda left, i: dot(left, OW[:, :, :, :, col_tile(i)].reshape(4 * HEAD_DIM, TILE)),
    )
    branch.start(0)
    branch.start(1)
    branch.relay(0)
    branch.relay(1)
    dg[0].pass_on("y")
    dg[1].pass_on("x")
    dg[0].pass_on("h", "y")
    dg[1].pass_on("h", "x")

    normed = GroupGather(N4)
    recips = []
    for k in range(2):
        r = rows_of(k)
        first_norm, normal_one, recip_one = norm_forward(
            tok[r, :].astype(F32) + branch.finish(k) + out_bias, gain_one, shift_one
        )
        FN[r, :] = first_norm
        NORM1[r, :] = normal_one
        recips.append(recip_one)
        normed.push(k, first_norm.astype(BF16))

    def pull_rest(pair):
        for have in (("x",), ("h", "x"), ("y", "x"), ("h", "y", "x")):
            pair[0].pull(*have)
        for have in (("y",), ("h", "y"), ("x", "y"), ("h", "x", "y")):
            pair[1].pull(*have)

    hidden = UB.shape[1]

    def up(k):
        def body(i):
            cols = col_tile(i)
            w = UW[:, :, :, :, :, :, cols].reshape(width, TILE)
            pre = dot(half_rows(N4, k), w) + UB[0:1, cols]
            phi = 0.5 * (1.0 + lax.erf(pre * (2.0 ** -0.5)))
            slope = phi + pre * (jnp.exp(-0.5 * pre * pre) * ((2.0 * math.pi) ** -0.5))
            GP[:, :, rows_of(k), cols] = slope.reshape(2, 2, half_n, TILE)
            C4[:, :, rows_of(k), cols] = (pre * phi).astype(BF16).reshape(2, 2, half_n, TILE)

        loop(hidden // TILE, body)

    feed = GroupSum(
        (R2A, R2B, R2C, R2D), C4,
        lambda left, i: dot(left, DW[:, :, :, :, col_tile(i)].reshape(hidden, TILE)),
    )
    normed.relay(0)
    pull_rest(ug)
    normed.pull(0)
    up(0)
    normed.relay(1)
    pull_rest(dg)
    feed.start(0)
    normed.pull(1)
    up(1)
    settle(mark)
    feed.relay(0)
    feed.start(1)
    feed.relay(1)

    d_feeds = GroupGather(DF4)
    for k in range(2):
        r = rows_of(k)
        final, normal_two, recip_two = norm_forward(
            FN[r, :] + feed.finish(k) + down_bias, gain_two, shift_two
        )
        out_o[r, :] = final.astype(BF16)
        d_second, gain_two_grad, shift_two_grad = norm_backward(
            cot[r, :].astype(F32), normal_two, recip_two, gain_two
        )
        DSEC[r, :] = d_second
        d_feed = d_second.astype(BF16)
        d_feeds.push(k, d_feed)
        add_vectors(
            k, (1, 4, 5), jnp.sum(d_feed.astype(F32), axis=0, keepdims=True), gain_two_grad, shift_two_grad
        )

    def transpose_rows(i):
        cols = pl.ds(pl.multiple_of(i * 128, 128), 128)
        t = N4[:, :, :, cols].reshape(group, 128)
        t = t.astype(F32).T.astype(BF16).reshape(2, 2, 32, group)
        for yp, xp in itertools.product(range(2), repeat=2):
            to = pl.ds(pl.multiple_of((i // 4 * 2 + i % 2) * 32, 32), 32)
            N4T[(i // 2) % 2, yp, xp, to, :] = t[yp, xp]
        C4T[i // 4, (i // 2) % 2, i % 2] = C4[:, :, :, cols].reshape(group, 128).astype(F32).T.astype(BF16)

    loop(8, transpose_rows)

    def d_hidden(k):
        def body(i):
            rows = DW[i // 2, i % 2].reshape(TILE, width)
            cols = col_tile(i)
            slope = GP[:, :, rows_of(k), cols].reshape(4 * half_n, TILE)
            v = (dot(half_rows(DF4, k), rows, 1, 1) * slope).astype(BF16)
            DH4[:, :, rows_of(k), cols] = v.reshape(2, 2, half_n, TILE)
            total = jnp.sum(v.astype(F32), axis=0, keepdims=True)
            UB[1:2, cols] = total if k == 0 else UB[1:2, cols] + total

        loop(hidden // TILE, body)

    class Scatter:
        def __init__(self, bufs, product):
            self.sa, self.ra, self.sb, self.rb, self.sc, self.rc, self.keep = bufs
            self.product = product
            self.shape = self.sa.shape[1:]
            self.parts = []
            for k, (one, two) in enumerate((("x", "y"), ("y", "x"))):
                of = range(k * tiles // 2, (k + 1) * tiles // 2)
                self.parts.append((
                    one, two, of,
                    Tiles(self.sa, self.ra, one, of), Tiles(self.sb, self.rb, two, of), Tiles(self.sc, self.rc, "h", of),
                ))

        def first(self):
            for one, two, of, a, b, c in self.parts:
                def body(i, one=one, of=of, a=a):
                    i = of[0] + i
                    self.sa[i] = self.product(one, 1 - here[one], i).reshape(self.shape).astype(BF16)
                    a.send(i)

                loop(len(of), body)

        def second(self):
            for one, two, of, a, b, c in self.parts:
                def body(i, one=one, two=two, of=of, a=a, b=b):
                    i = of[0] + i
                    v = self.product(one, here[one], i).reshape(self.shape)
                    a.wait(i)
                    self.keep[i] = v + self.ra[i].astype(F32)
                    self.sb[i] = self.keep[i, :, 1 - here[two]].astype(BF16)
                    b.send(i)

                loop(len(of), body)

        def third(self):
            for one, two, of, a, b, c in self.parts:
                def body(i, two=two, of=of, b=b, c=c):
                    i = of[0] + i
                    b.wait(i)
                    self.keep[i, :, 0] = self.keep[i, :, here[two]] + self.rb[i].astype(F32)
                    self.sc[i] = self.keep[i, 1 - h, 0].astype(BF16)
                    c.send(i)

                loop(len(of), body)

        def last(self, out):
            for one, two, of, a, b, c in self.parts:
                def body(i, of=of, c=c):
                    i = of[0] + i
                    c.wait(i)
                    out[:, col_tile(i)] = self.keep[i, h, 0] + self.rc[i].astype(F32)

                loop(len(of), body)

    def up_product(dim, v, i):
        rows = N4T[:, :, v] if dim == "x" else N4T[:, v]
        return dot(rows.reshape(group, group), DH4[:, :, :, col_tile(i)].reshape(group, TILE))

    def down_product(dim, v, i):
        rows = C4T[:, :, v] if dim == "x" else C4T[:, v]
        return dot(rows.reshape(group, group), DF4[:, :, :, col_tile(i)].reshape(group, TILE))

    def out_product(dim, v, i):
        rows = AT[:, :, pl.ds(pl.multiple_of(v * 32, 32), 32), :] if dim == "x" else AT[:, v]
        return dot(rows.reshape(128, group), DB4[:, :, :, col_tile(i)].reshape(group, TILE))

    down_s = Scatter((DSA, DRA, DSB, DRB, DSC, DRC, DK), down_product)
    up_s = Scatter((USA, URA, USB, URB, USC, URC, UK), up_product)
    out_s = Scatter((OSA, ORA, OSB, ORB, OSC, ORC, OK), out_product)

    def up_rows(i):
        return UW[i // 2, i % 2].reshape(TILE, hidden)

    d_first = GroupSum((R1A, R1B, R1C, R1D), DH4, lambda left, i: dot(left, up_rows(i), 1, 1))
    d_branches = GroupGather(DB4)
    d_feeds.relay(0)
    d_feeds.pull(0)
    d_hidden(0)
    d_feeds.relay(1)
    d_first.start(0)
    d_feeds.pull(1)
    d_hidden(1)
    down_s.first()
    d_first.relay(0)
    d_first.start(1)
    d_first.relay(1)
    for k in range(2):
        r = rows_of(k)
        d_sum_one, gain_one_grad, shift_one_grad = norm_backward(
            DSEC[r, :] + d_first.finish(k), NORM1[r, :], recips[k], gain_one
        )
        DSUM[r, :] = d_sum_one
        d_branch = d_sum_one.astype(BF16)
        d_branches.push(k, d_branch)
        add_vectors(
            k, (0, 2, 3), jnp.sum(d_branch.astype(F32), axis=0, keepdims=True), gain_one_grad, shift_one_grad
        )
    up_s.first()
    for k in range(2):
        d_branches.relay(k)
    for k in range(2):
        d_branches.pull(k)

    d_att = dot(DB4[...].reshape(group, width), OW[...].reshape(4 * HEAD_DIM, width), 1, 1).astype(BF16)
    d_att = d_att.astype(F32).T.astype(BF16).reshape(2, 2, HEAD_DIM, group)
    DS[...] = d_att
    d_sem = {f: ids() for f in others}
    for flips in others:
        p = at(flips)
        send(DS.at[p["h"], p["y"]], DR.at[h, y], d_sem[flips], flips)
    DR[h, y] = DS[h, y]

    out_s.first()
    down_s.second()
    up_s.second()

    VG[6:8, :] = jnp.zeros((2, width), F32)
    picked = [spread_matrix(width, 32, j) for j in range(4)]

    def exact_pick(row, j):
        a = jnp.where(mine, VG[row : row + 1, :], 0.0)
        hi = a.astype(BF16)
        rest = a - hi.astype(F32)
        mid = rest.astype(BF16)
        low = (rest - mid.astype(F32)).astype(BF16)
        r = picked[j].astype(BF16)
        return dot(hi, r, 1, 1) + dot(mid, r, 1, 1) + dot(low, r, 1, 1)

    SG[...] = jnp.zeros_like(SG)
    SG[:, 0, :] = exact_pick(0, 2) + exact_pick(1, 3)
    SG[:, 1, :] = exact_pick(2, 0) + exact_pick(3, 1) + exact_pick(4, 2) + exact_pick(5, 3)
    for hp, yp, xp in itertools.product(range(2), repeat=3):
        r = hp * 4 + yp * 2 + xp
        SG[(s * 8 + hp * 4 + l * 2 + yp) * 2 + xp, 2:3, :] = UB[1:2, r * 128 : (r + 1) * 128]

    for flips in others:
        p = at(flips)
        wait(DR.at[p["h"], p["y"]], d_sem[flips], flips)
    for sp in range(2):
        j = s if sp == 0 else 1 - s
        for hp, lp, yp in itertools.product(range(2), repeat=3):
            part = DR[hp, yp, :, (sp * 2 + lp) * tokens : (sp * 2 + lp + 1) * tokens]
            at_tok = (hp * 4 + lp * 2 + yp) * tokens
            DAT[j, :, at_tok : at_tok + tokens] = part
            DA[j, at_tok : at_tok + tokens, :] = part.astype(F32).T.astype(BF16)

    def attend_back(j):
        DKV[...] = jnp.zeros_like(DKV)

        def body(i):
            cols = col_tile(i)
            q = QKVT[j, 0:64, cols] * jnp.asarray(scale, BF16)
            p = jnp.exp(dot(KN[j], q) - LSE[j, 0:1, cols])
            da = DAT[j, :, cols]
            delta = jnp.sum(da.astype(F32) * OT[j, :, cols], axis=0, keepdims=True)
            dp = dot(VN[j], da)
            ds = (p * (dp - delta) * scale).astype(BF16)
            DQT[j, :, cols] = dot(QKVT[j, 64:128, :], ds)
            DKV[0] += dot(ds, QN[j, cols, :])
            DKV[1] += dot(p.astype(BF16), DA[j, cols, :])

        loop(qtiles, body)
        dqt = DQT[j].astype(BF16).astype(F32)
        dq = dqt.T
        dk, dv = DKV[0].astype(BF16).astype(F32), DKV[1].astype(BF16).astype(F32)
        DQKV[j] = jnp.concatenate([dq, dk, dv], axis=1).astype(BF16)
        DQKVT[j, 0:64, :] = dqt.astype(BF16)
        DQKVT[j, 64:128, :] = dk.T.astype(BF16)
        DQKVT[j, 128:192, :] = dv.T.astype(BF16)
        return jnp.sum(dq, axis=0, keepdims=True), jnp.sum(dv, axis=0, keepdims=True)

    def input_tile(j, part, i):
        w = WH[pl.ds(pl.multiple_of(i * 4, 4), 4)].reshape(TILE, WH.shape[-1])[:, 0 : 3 * HEAD_DIM]
        rows = pl.ds(pl.multiple_of(part * (length // 2), length // 2), length // 2)
        return dot(DQKV[j, rows, :], w, 1, 1).reshape(2, 2, tokens, TILE)

    in_order = (0, 1, 2, 3)
    far, near = 1 - h, h
    ia, ib, ic, id_ = ({(p, i): ids() for p in range(2) for i in range(tiles)} for _ in range(4))

    def in_sent(i):
        return (C4T if i < tiles // 2 else N4T).at[:, :, :, :, pl.ds(i % 2 * TILE, TILE)]

    q1, v1 = attend_back(1)
    down_s.third()
    for p, part in enumerate((far, near)):
        for i in in_order:
            piece = in_sent(i).at[part]
            piece[...] = input_tile(1, part, i).astype(BF16)
            send(piece, IRA.at[i, part], ia[p, i], ("s",))
    q0, v0 = attend_back(0)
    to_x = Tiles(QSA, QRA, "x", range(tiles))

    def q_first(i):
        cols = col_tile(i)
        v = dot(DQKVT[0], X16[s, :, :, :, :, cols].reshape(length, TILE))
        v += dot(DQKVT[1], X16[1 - s, :, :, :, :, cols].reshape(length, TILE))
        v = v.T.reshape(2, 2, 2, 32, 3 * HEAD_DIM)
        for xp in range(2):
            QK[i, xp] = v[:, :, xp]
        QSA[i, :, :, :, 0 : 3 * HEAD_DIM] = QK[i, 1 - x].astype(BF16)
        to_x.send(i)

    def in_second(p):
        part = (far, near)[p]
        for i in in_order:
            wait(IRA.at[i, part], ia[p, i], ("s",))
            IK[i, part] = input_tile(0, part, i) + IRA[i, part].astype(F32)
            dim = "l" if i < 1 else "y"
            ISB[i, part] = (IK[i, part, 1 - l] if dim == "l" else IK[i, part, :, 1 - y]).astype(BF16)
            send(ISB.at[i, part], IRB.at[i, part], ib[p, i], (dim,))

    def in_third(p):
        part = (far, near)[p]
        for i in in_order:
            one, two = ("l", "y") if i < 1 else ("y", "l")
            wait(IRB.at[i, part], ib[p, i], (one,))
            IK[i, part, 0] = (IK[i, part, l] if one == "l" else IK[i, part, :, y]) + IRB[i, part].astype(F32)
            ISC[i, part] = IK[i, part, 0, 1 - here[two]].astype(BF16)
            send(ISC.at[i, part], IRC.at[i, part], ic[p, i], (two,))

    def in_summed(p, i):
        part = (far, near)[p]
        two = "y" if i < 1 else "l"
        wait(IRC.at[i, part], ic[p, i], (two,))
        return IK[i, part, 0, here[two]] + IRC[i, part].astype(F32)

    def q_second(i):
        to_x.wait(i)
        v = QK[i, x] + QRA[i, :, :, :, 0 : 3 * HEAD_DIM].astype(F32)
        QSB[i // 2, i % 2, :, :, :, 0 : 3 * HEAD_DIM] = v.astype(BF16)

    def piece_copy(j):
        to = (head + j) % 16
        return peer_copy(
            QSB.at[to // 8, (to // 4) % 2, (to // 2) % 2, to % 2], QG.at[head], (hss, hrs), 16 + j
        )

    in_second(0)
    in_second(1)
    up_s.third()
    out_s.second()
    loop(tiles, q_first)
    bq, bv = q0 + q1, v0 + v1
    for k in range(2):
        b = head * 2 + k
        lanes = slice(k * 32, k * 32 + 32)
        SG[b, 0:1, :] += jnp.concatenate([bq[:, lanes], bv[:, lanes], jnp.zeros((1, 64), F32)], axis=1)

    def grad_copy(j):
        return peer_copy(SG.at[pl.ds((head + j) % 16 * 2, 2)], RG.at[j], (hss, hrs), j)

    loop(15, lambda j: grad_copy(j + 1).start())
    RG[0] = SG[pl.ds(head * 2, 2)]
    in_third(0)
    out_s.third()
    loop(tiles, q_second)
    loop(15, lambda j: piece_copy(j + 1).start())
    QG[head] = QSB[s, h, l, y]
    for i in in_order:
        ISD[i] = in_summed(0, i).astype(BF16)
        send(ISD.at[i], IRD.at[i], id_[0, i], ("h",))
    in_third(1)
    down_s.last(downg_o)
    loop(15, lambda j: grad_copy(j + 1).wait_recv())
    small_sum = jnp.sum(RG[...], axis=0)
    SX[0:2] = small_sum
    x_sem = ids()
    send(SX.at[1 - x], RX, x_sem, ("x",))
    up_s.last(UF)
    uf_sem = {}
    for flips in (("s",), ("l",), ("s", "l")):
        p = at(flips)
        for hp in range(2):
            uf_sem[flips, hp] = ids()
            send(
                UF.at[pl.ds(pl.multiple_of((p["s"] * 2 + p["l"]) * 32, 32), 32), pl.ds(hp * 512, 512)],
                upg_o.at[:, quarter(s, hp, l)], uf_sem[flips, hp], flips,
            )
    for hp in range(2):
        upg_o[:, quarter(s, hp, l)] = UF[pl.ds(pl.multiple_of((s * 2 + l) * 32, 32), 32), hp * 512 : (hp + 1) * 512]
    out_s.last(outg_o)
    wait(RX, x_sem, ("x",))
    small_o[...] = SX[x] + RX[...]
    loop(15, lambda j: piece_copy(j + 1).wait_recv())
    for k in range(HEADS // 2):
        a, b = QG[2 * k].astype(F32), QG[2 * k + 1].astype(F32)
        for part in range(3):
            lanes = slice(part * 64, part * 64 + 64)
            to = part * width + k * 128
            qkvg_o[:, to : to + 128] = jnp.concatenate([a[:, lanes], b[:, lanes]], axis=1)
    for i in range(tiles):
        total = in_summed(1, i) + DSUM[:, i * TILE : (i + 1) * TILE]
        wait(IRD.at[i], id_[0, i], ("h",))
        ig_o[:, i * TILE : (i + 1) * TILE] = total + IRD[i].astype(F32)

    for flips in (("s",), ("l",), ("s", "l")):
        p = at(flips)
        for hp in range(2):
            wait(upg_o.at[:, quarter(p["s"], hp, p["l"])], uf_sem[flips, hp], flips)

    for d in sends:
        d.wait_send()

    def small_sent(j):
        for d in small_copy(j + 1, head):
            d.wait_send()
        grad_copy(j + 1).wait_send()

    loop(15, small_sent)
    loop(15, lambda j: piece_copy(j + 1).wait_send())


def hand_over(*refs):
    large, small, outs, sems = refs[:6], refs[6], refs[7:22], refs[22]
    copies = [pltpu.make_async_copy(a, b, sems.at[k]) for k, (a, b) in enumerate(zip(large, outs))]
    for c in copies:
        c.start()
    places = ((0, 0, 32), (0, 32, 32), (0, 64, 32), (2, 0, 128), (0, 96, 32), (1, 0, 32), (1, 32, 32), (1, 64, 32), (1, 96, 32))
    for ref, (row, lane, count) in zip(outs[6:], places):
        ref[...] = small[row : row + 1, lane : lane + count]
    for c in copies:
        c.wait()


def on_block(
    tokens, qkv_weight, out_weight, up_weight, down_weight,
    query_bias, value_bias, out_bias, up_bias, down_bias,
    norm1_gain, norm1_bias, norm2_gain, norm2_bias, cotangent,
):
    n, width = tokens.shape[1], tokens.shape[2]
    hidden = up_weight.shape[1] // 4
    group = 4 * n
    length = 8 * n
    tiles = width // TILE
    vectors = [
        v.reshape(1, -1)
        for v in (query_bias, value_bias, out_bias, up_bias, down_bias, norm1_gain, norm1_bias, norm2_gain, norm2_bias)
    ]

    def b(*shape):
        return pltpu.VMEM(shape, BF16)

    def f(*shape):
        return pltpu.VMEM(shape, F32)

    group_bufs = [b(2, tiles, 2, n // 2, TILE), b(2, tiles, 2, n // 2, TILE), b(2, tiles, n // 2, TILE), b(2, tiles, n // 2, TILE)]

    def scatter_bufs(rows):
        return [
            b(tiles, 2, 2, rows, TILE), b(tiles, 2, 2, rows, TILE),
            b(tiles, 2, rows, TILE), b(tiles, 2, rows, TILE),
            b(tiles, rows, TILE), b(tiles, rows, TILE),
            f(tiles, 2, 2, rows, TILE),
        ]

    sem = pltpu.SemaphoreType.DMA
    scratch = [
        f(8, 128), b(2, 2, 2, 2, n, width), b(HEADS, 32, 256), b(HEADS, 2, 32, 256), f(HEADS, 2, 8, 128),
        b(2, 2, 2, 32, width), b(2, 2, 2, 2, 2, 32, hidden), b(2, 2, 2, 128, width),
        b(2, length, 64), b(2, length, 64), b(2, length, 64), b(2, 192, length), f(2, 64, length), b(2, 64, length),
        f(2, 8, length), b(4, 2, 64, group // 2), b(2, 2, 64, group), b(2, 2, n, 256),
        *group_bufs, *group_bufs, f(2, tiles, 2, n // 2, TILE),
        b(2, 2, n, width), b(2, 2, 2, 128, group), b(2, 2, n, hidden), b(2, 2, 2, 128, group), f(2, 2, n, hidden),
        b(2, 2, n, width),
        f(n, width), f(n, width), f(n, width),
        b(2, 2, 64, group), b(2, 2, 64, group), b(2, length, 64), b(2, 64, length), f(2, length, 64), f(2, 64, length),
        b(2, length, 192), b(2, 192, length),
        *scatter_bufs(128), f(128, width),
        *scatter_bufs(128),
        *scatter_bufs(32),
        b(tiles, 2, 2, 2, n, TILE), b(tiles, 2, 2, n, TILE), b(tiles, 2, 2, n, TILE),
        b(tiles, 2, n, TILE), b(tiles, 2, n, TILE), b(tiles, n, TILE), b(tiles, n, TILE), f(tiles, 2, 2, 2, n, TILE),
        b(tiles, 2, 2, 32, 256), b(tiles, 2, 2, 32, 256), f(tiles, 2, 2, 2, 32, 192), b(2, 2, 2, 2, 32, 256), b(HEADS, 32, 256),
        f(8, width), f(8, hidden), f(8, width), f(32, 8, 128), f(HEADS, 2, 8, 128), f(2, 8, 128), f(8, 128),
        sem((300,)), sem((300,)), sem((16,)), sem((16,)), sem((16,)), sem((16,)), sem((32,)), sem((32,)),
    ]
    vmem = pl.BlockSpec(memory_space=pltpu.VMEM)
    shapes = [
        jax.ShapeDtypeStruct((n, width), BF16),
        jax.ShapeDtypeStruct((n, width), F32),
        jax.ShapeDtypeStruct((32, 3 * width), F32),
        jax.ShapeDtypeStruct((32, width), F32),
        jax.ShapeDtypeStruct((32, 4 * hidden), F32),
        jax.ShapeDtypeStruct((128, width), F32),
        jax.ShapeDtypeStruct((8, 128), F32),
    ]
    results = pl.pallas_call(
        layer_kernel,
        out_shape=shapes,
        in_specs=[vmem] * 15,
        out_specs=[vmem] * 7,
        scratch_shapes=scratch,
        compiler_params=pltpu.CompilerParams(
            collective_id=0, has_side_effects=True, vmem_limit_bytes=63 * 2**20
        ),
        name="layer",
    )(tokens[0], qkv_weight, out_weight, up_weight, down_weight, *vectors, cotangent[0])
    lengths = [v.shape[1] for v in vectors]
    everywhere = pl.BlockSpec(memory_space=pl.ANY)
    done = pl.pallas_call(
        hand_over,
        out_shape=shapes[:6] + [jax.ShapeDtypeStruct((1, k), F32) for k in lengths],
        in_specs=[vmem] * 7,
        out_specs=[everywhere] * 6 + [vmem] * 9,
        scratch_shapes=[sem((6,))],
        name="results",
    )(*results)
    return (
        done[0][None], done[1][None], *done[2:6], *(v.reshape(-1) for v in done[6:]),
    )


def solution(mesh):
    placed = (
        P(("seq", "fsdp"), "ctx", None),
        P(("seq", "ctx", "fsdp"), None),
        P(("seq", "ctx", "fsdp"), None),
        P(("seq", "ctx", "fsdp"), None),
        P(("seq", "ctx", "fsdp"), None),
        P(("seq", "ctx", "fsdp")),
        P(("seq", "ctx", "fsdp")),
        P(("seq", "ctx", "fsdp")),
        P(("seq", "ctx", "fsdp")),
        P(("seq", "ctx", "fsdp")),
        P(("seq", "ctx", "fsdp")),
        P(("seq", "ctx", "fsdp")),
        P(("seq", "ctx", "fsdp")),
        P(("seq", "ctx", "fsdp")),
        P(("seq", "fsdp"), "ctx", None),
    )
    fast = dict(mesh.shape) == {"seq": 2, "ctx": 8, "fsdp": 2}
    return jax.shard_map(
        on_block if fast else on_device,
        mesh=mesh,
        in_specs=placed,
        out_specs=(
            P(("seq", "fsdp"), "ctx", None),
            P(("seq", "fsdp"), "ctx", None),
            P(("seq", "ctx", "fsdp"), None),
            P(("seq", "ctx", "fsdp"), None),
            P(("seq", "ctx", "fsdp"), None),
            P(("seq", "ctx", "fsdp"), None),
            P(("seq", "ctx", "fsdp")),
            P(("seq", "ctx", "fsdp")),
            P(("seq", "ctx", "fsdp")),
            P(("seq", "ctx", "fsdp")),
            P(("seq", "ctx", "fsdp")),
            P(("seq", "ctx", "fsdp")),
            P(("seq", "ctx", "fsdp")),
            P(("seq", "ctx", "fsdp")),
            P(("seq", "ctx", "fsdp")),
        ),
        check_vma=False,
    )
```

```python
import functools
import itertools
import math

import jax
import jax.numpy as jnp
from jax import lax
from jax.experimental import pallas as pl
from jax.experimental.pallas import tpu as pltpu
from jax.sharding import PartitionSpec as P

HEADS = 16
HEAD_DIM = 64


epsilon = 1e-05
MESH = pl.DeviceIdType.MESH
F32 = jnp.float32
BF16 = jnp.bfloat16
TILE = 256


def split_blocks(piece):
    rows = piece.shape[0]
    block = math.gcd(rows, 512)
    return (piece.reshape(rows // block, block, HEADS, HEAD_DIM), block)


def norm_forward(values, gain, shift):
    centered = values - jnp.mean(values, axis=-1, keepdims=True)
    recip = lax.rsqrt(jnp.mean(centered * centered, axis=-1, keepdims=True) + epsilon)
    normal = centered * recip
    return (normal * gain + shift, normal, recip)


def norm_backward(upstream, normal, recip, gain):
    gain_grad = jnp.sum(upstream * normal, axis=0)
    shift_grad = jnp.sum(upstream, axis=0)
    scaled = upstream * gain
    inner = (
        scaled
        - jnp.mean(scaled, axis=-1, keepdims=True)
        - normal * jnp.mean(scaled * normal, axis=-1, keepdims=True)
    )
    return (recip * inner, gain_grad, shift_grad)


def matmul(left_neighbor, right_neighbor):
    return jnp.dot(left_neighbor, right_neighbor, preferred_element_type=jnp.float32)


def on_device(
    tokens,
    qkv_weight,
    out_weight,
    up_weight,
    down_weight,
    query_bias,
    value_bias,
    out_bias,
    up_bias,
    down_bias,
    norm1_gain,
    norm1_bias,
    norm2_gain,
    norm2_bias,
    cotangent,
):
    gathered = (
        lax.all_gather(qkv_weight, ("seq", "ctx", "fsdp"), axis=0, tiled=True),
        lax.all_gather(out_weight, ("seq", "ctx", "fsdp"), axis=0, tiled=True),
        lax.all_gather(up_weight, ("seq", "ctx", "fsdp"), axis=0, tiled=True),
        lax.all_gather(down_weight, ("seq", "ctx", "fsdp"), axis=0, tiled=True),
        lax.all_gather(query_bias, ("seq", "ctx", "fsdp"), axis=0, tiled=True),
        lax.all_gather(value_bias, ("seq", "ctx", "fsdp"), axis=0, tiled=True),
        lax.all_gather(out_bias, ("seq", "ctx", "fsdp"), axis=0, tiled=True),
        lax.all_gather(up_bias, ("seq", "ctx", "fsdp"), axis=0, tiled=True),
        lax.all_gather(down_bias, ("seq", "ctx", "fsdp"), axis=0, tiled=True),
        lax.all_gather(norm1_gain, ("seq", "ctx", "fsdp"), axis=0, tiled=True),
        lax.all_gather(norm1_bias, ("seq", "ctx", "fsdp"), axis=0, tiled=True),
        lax.all_gather(norm2_gain, ("seq", "ctx", "fsdp"), axis=0, tiled=True),
        lax.all_gather(norm2_bias, ("seq", "ctx", "fsdp"), axis=0, tiled=True),
    )
    qkv_full, out_full, up_full, down_full = (gathered[0], gathered[1], gathered[2], gathered[3])
    small = tuple((item.astype(jnp.float32) for item in gathered[4:]))
    q_shift, v_shift, o_shift, u_shift, d_shift, gain_one, shift_one, gain_two, shift_two = small
    scale = HEAD_DIM ** (-0.5)
    inputs = tokens[0]
    rows = inputs.shape[0]
    width = inputs.shape[1]
    joined_bias = jnp.concatenate([q_shift, jnp.zeros_like(q_shift), v_shift])
    qkv_low = (matmul(inputs, qkv_full) + joined_bias).astype(jnp.bfloat16)
    queries = qkv_low[:, :width].reshape(rows, HEADS, HEAD_DIM)
    keys_own = qkv_low[:, width : 2 * width]
    values_own = qkv_low[:, 2 * width :]
    start_state = (
        jnp.full((HEADS, rows), -1e30, jnp.float32),
        jnp.zeros((HEADS, rows), jnp.float32),
        jnp.zeros((rows, HEADS, HEAD_DIM), jnp.float32),
    )
    piece = (
        lax.all_gather(keys_own, "ctx", axis=0, tiled=True),
        lax.all_gather(values_own, "ctx", axis=0, tiled=True),
    )
    key_blocks, block = split_blocks(piece[0])
    value_blocks, block = split_blocks(piece[1])

    def inner(state, pair):
        run_max, run_sum, accum = state
        key_tile_rows, value_block = pair
        scores = (
            jnp.einsum("qhe,khe->hqk", queries, key_tile_rows, preferred_element_type=jnp.float32)
            * scale
        )
        new_max = jnp.maximum(run_max, jnp.max(scores, axis=-1))
        factor = jnp.exp(run_max - new_max)
        weights = jnp.exp(scores - new_max[..., None])
        run_sum = run_sum * factor + jnp.sum(weights, axis=-1)
        accum = accum * factor.T[..., None] + jnp.einsum(
            "hqk,khe->qhe",
            weights.astype(jnp.bfloat16),
            value_block,
            preferred_element_type=jnp.float32,
        )
        return ((new_max, run_sum, accum), None)

    result, unused = lax.scan(inner, start_state, (key_blocks, value_blocks))
    run_max, run_sum, accum = result
    attended = accum / run_sum.T[..., None]
    log_total = run_max + jnp.log(run_sum)
    attended_low = attended.reshape(rows, width).astype(jnp.bfloat16)
    first_sum = inputs.astype(jnp.float32) + matmul(attended_low, out_full) + o_shift
    first_norm, normal_one, recip_one = norm_forward(first_sum, gain_one, shift_one)
    normed_low = first_norm.astype(jnp.bfloat16)
    hidden_pre = matmul(normed_low, up_full) + u_shift
    activated_full, gelu_pull = jax.vjp(lambda pre: jax.nn.gelu(pre, approximate=False), hidden_pre)
    activated = activated_full.astype(jnp.bfloat16)
    second_sum = first_norm + matmul(activated, down_full) + d_shift
    final, normal_two, recip_two = norm_forward(second_sum, gain_two, shift_two)
    upstream = cotangent[0].astype(jnp.float32)
    d_second, gain_two_grad, shift_two_grad = norm_backward(
        upstream, normal_two, recip_two, gain_two
    )
    d_feed = d_second.astype(jnp.bfloat16)
    down_grad = matmul(activated.T, d_feed)
    down_bias_grad = jnp.sum(d_feed.astype(jnp.float32), axis=0)
    d_hidden = gelu_pull(matmul(d_feed, down_full.T))[0].astype(jnp.bfloat16)
    up_grad = matmul(normed_low.T, d_hidden)
    up_bias_grad = jnp.sum(d_hidden.astype(jnp.float32), axis=0)
    first_input_gradient = d_second + matmul(d_hidden, up_full.T)
    d_sum_one, gain_one_grad, first_shift_gradient = norm_backward(
        first_input_gradient, normal_one, recip_one, gain_one
    )
    d_branch = d_sum_one.astype(jnp.bfloat16)
    out_grad = matmul(attended_low.T, d_branch)
    out_bias_grad = jnp.sum(d_branch.astype(jnp.float32), axis=0)
    d_attended = matmul(d_branch, out_full.T).astype(jnp.bfloat16).reshape(rows, HEADS, HEAD_DIM)
    delta = jnp.sum(d_attended.astype(jnp.float32) * attended, axis=-1).T
    total_rows = rows * lax.axis_size("ctx")
    zero_query = jnp.zeros((rows, HEADS, HEAD_DIM), jnp.float32)
    start_back = (zero_query, jnp.zeros((total_rows, 2 * width), jnp.float32))
    piece = (
        lax.all_gather(keys_own, "ctx", axis=0, tiled=True),
        lax.all_gather(values_own, "ctx", axis=0, tiled=True),
    )
    key_blocks, block = split_blocks(piece[0])
    value_blocks, block = split_blocks(piece[1])
    counter = jnp.arange(key_blocks.shape[0], dtype=jnp.int32)

    def inner(state, triple):
        key_tile_rows, value_block, number = triple
        scores = (
            jnp.einsum("qhe,khe->hqk", queries, key_tile_rows, preferred_element_type=jnp.float32)
            * scale
        )
        weights = jnp.exp(scores - log_total[..., None])
        d_probs = jnp.einsum(
            "qhe,khe->hqk", d_attended, value_block, preferred_element_type=jnp.float32
        )
        d_scores = (weights * (d_probs - delta[..., None]) * scale).astype(jnp.bfloat16)
        d_query = state[0] + jnp.einsum(
            "hqk,khe->qhe", d_scores, key_tile_rows, preferred_element_type=jnp.float32
        )
        d_key = jnp.einsum(
            "hqk,qhe->khe", d_scores, queries, preferred_element_type=jnp.float32
        ).reshape(block, width)
        d_value = jnp.einsum(
            "hqk,qhe->khe",
            weights.astype(jnp.bfloat16),
            d_attended,
            preferred_element_type=jnp.float32,
        ).reshape(block, width)
        offset = number * block
        current = lax.dynamic_slice_in_dim(state[1], offset, block, 0)
        updated = lax.dynamic_update_slice_in_dim(
            state[1], current + jnp.concatenate([d_key, d_value], axis=1), offset, 0
        )
        return ((d_query, updated), None)

    result, unused = lax.scan(inner, start_back, (key_blocks, value_blocks, counter))
    d_query = result[0].reshape(rows, width)
    summed = lax.psum_scatter(result[1], "ctx", scatter_dimension=0, tiled=True)
    d_key = summed[:, :width]
    d_value = summed[:, width:]
    d_qkv = jnp.concatenate([d_query, d_key, d_value], axis=1).astype(jnp.bfloat16)
    qkv_grad = matmul(inputs.T, d_qkv)
    d_qkv_wide = d_qkv.astype(jnp.float32)
    query_bias_gradient = jnp.sum(d_qkv_wide[:, :width], axis=0)
    value_bias_grad = jnp.sum(d_qkv_wide[:, 2 * width :], axis=0)
    input_grad = matmul(d_qkv, qkv_full.T) + d_sum_one
    sharded = (
        lax.psum_scatter(qkv_grad, ("seq", "ctx", "fsdp"), scatter_dimension=0, tiled=True),
        lax.psum_scatter(out_grad, ("seq", "ctx", "fsdp"), scatter_dimension=0, tiled=True),
        lax.psum_scatter(up_grad, ("seq", "ctx", "fsdp"), scatter_dimension=0, tiled=True),
        lax.psum_scatter(down_grad, ("seq", "ctx", "fsdp"), scatter_dimension=0, tiled=True),
        lax.psum_scatter(
            query_bias_gradient, ("seq", "ctx", "fsdp"), scatter_dimension=0, tiled=True
        ),
        lax.psum_scatter(value_bias_grad, ("seq", "ctx", "fsdp"), scatter_dimension=0, tiled=True),
        lax.psum_scatter(out_bias_grad, ("seq", "ctx", "fsdp"), scatter_dimension=0, tiled=True),
        lax.psum_scatter(up_bias_grad, ("seq", "ctx", "fsdp"), scatter_dimension=0, tiled=True),
        lax.psum_scatter(down_bias_grad, ("seq", "ctx", "fsdp"), scatter_dimension=0, tiled=True),
        lax.psum_scatter(gain_one_grad, ("seq", "ctx", "fsdp"), scatter_dimension=0, tiled=True),
        lax.psum_scatter(
            first_shift_gradient, ("seq", "ctx", "fsdp"), scatter_dimension=0, tiled=True
        ),
        lax.psum_scatter(gain_two_grad, ("seq", "ctx", "fsdp"), scatter_dimension=0, tiled=True),
        lax.psum_scatter(shift_two_grad, ("seq", "ctx", "fsdp"), scatter_dimension=0, tiled=True),
    )
    return (
        final.astype(jnp.bfloat16)[None],
        input_grad[None],
        sharded[0],
        sharded[1],
        sharded[2],
        sharded[3],
        sharded[4],
        sharded[5],
        sharded[6],
        sharded[7],
        sharded[8],
        sharded[9],
        sharded[10],
        sharded[11],
        sharded[12],
    )


def dot(left, right, left_dim=1, right_dim=0):
    return lax.dot_general(
        left, right, (((left_dim,), (right_dim,)), ((), ())), preferred_element_type=F32
    )


def loop(count, body):
    def step(i, carry):
        body(i)
        return carry

    lax.fori_loop(0, count, step, 0)


def spread_matrix(width, piece, at):
    lane = lax.broadcasted_iota(jnp.int32, (128, width), 0)
    column = lax.broadcasted_iota(jnp.int32, (128, width), 1)
    return jnp.where(lane == at * piece + column % piece, 1.0, 0.0)


def own_columns(blocks, width):
    row = lax.broadcasted_iota(jnp.int32, (blocks, width), 0)
    column = lax.broadcasted_iota(jnp.int32, (blocks, width), 1)
    return column // (width // blocks), row


def layer_kernel(
    tok, qkvw, outw, upw, downw, qb, vb, ob, ub, db, g1, b1, g2, b2, cot,
    out_o, ig_o, qkvg_o, outg_o, upg_o, downg_o, small_o,
    PK, X16, WP, WH, G, OW, UW, DW,
    QN, KN, VN, QKVT, OT, OTB, LSE, AS, AT, A4,
    R1A, R1B, R1C, R1D, R2A, R2B, R2C, R2D, KR,
    N4, N4T, C4, C4T, GP, DF4,
    FN, NORM1, DSEC,
    DS, DR, DA, DAT, DKV, DQT, DQKV, DQKVT,
    USA, URA, USB, URB, USC, URC, UK, UF,
    DSA, DRA, DSB, DRB, DSC, DRC, DK,
    OSA, ORA, OSB, ORB, OSC, ORC, OK,
    IRA, ISB, IRB, ISC, IRC, ISD, IRD, IK,
    QSA, QRA, QK, QSB, QG,
    VEC, UB, VG, SG, RG, SX, RX,
    ssem, rsem, wss, wrs, gss, grs, hss, hrs,
):
    s = lax.axis_index("seq")
    c = lax.axis_index("ctx")
    x = lax.axis_index("fsdp")
    h, l, y = c // 4, (c // 2) % 2, c % 2
    here = {"s": s, "h": h, "l": l, "y": y, "x": x}
    me = s * 16 + c * 2 + x
    head = s * 8 + c
    width = tok.shape[1]
    tiles = width // TILE
    counter = itertools.count()
    sends = []

    def at(flips):
        return {k: (1 - v if k in flips else v) for k, v in here.items()}

    def device(flips):
        p = at(flips)
        return {"seq": p["s"], "ctx": p["h"] * 4 + p["l"] * 2 + p["y"], "fsdp": p["x"]}

    def ids(n=1):
        return [next(counter) for _ in range(n)][0]

    def copy(src, dst, sem, flips):
        return pltpu.make_async_remote_copy(
            src_ref=src, dst_ref=dst, send_sem=ssem.at[sem], recv_sem=rsem.at[sem],
            device_id=device(flips), device_id_type=MESH,
        )

    def settle(since):
        for d in sends[since:]:
            d.wait_send()
        del sends[since:]

    def send(src, dst, sem, flips):
        d = copy(src, dst, sem, flips)
        d.start()
        sends.append(d)

    def wait(ref, sem, flips):
        copy(ref, ref, sem, flips).wait_recv()

    class Tiles:
        def __init__(self, src, dst, dim, of):
            self.src, self.dst, self.dim, self.of = src, dst, dim, of
            self.base = [ids() for _ in of][0] - of[0]
            self.listed = False

        def each(self, i):
            return copy(self.src.at[i], self.dst.at[i], self.base + i, (self.dim,))

        def send(self, i):
            self.each(i).start()
            if not self.listed:
                sends.append(self)
                self.listed = True

        def wait(self, i):
            self.each(i).wait_recv()

        def wait_send(self):
            for i in self.of:
                self.each(i).wait_send()

    class Gather:
        def __init__(self, order, block):
            self.order, self.block, self.sem = order, block, {}
            for n in range(1, len(order) + 1):
                for k in itertools.combinations(order, n):
                    self.sem[frozenset(k)] = ids()

        def push(self, *have, along=None):
            have = frozenset(have)
            last = max([self.order.index(d) for d in have], default=-1)
            for d in self.order[last + 1 :]:
                if along and d not in along:
                    continue
                ref = self.block(at(have))
                send(ref, ref, self.sem[have | {d}], (d,))

        def pull(self, *have):
            have = frozenset(have)
            last = max(have, key=self.order.index)
            wait(self.block(at(have)), self.sem[have], (last,))

        def pass_on(self, *have):
            self.pull(*have)
            self.push(*have)

    barrier = pltpu.get_barrier_semaphore()

    def peer(j):
        to = (head + j) % 16
        return {"seq": to // 8, "ctx": to % 8, "fsdp": x}

    def peer_copy(src, dst, sems, j):
        return pltpu.make_async_remote_copy(
            src_ref=src, dst_ref=dst, send_sem=sems[0].at[j], recv_sem=sems[1].at[j],
            device_id=peer(j % 16), device_id_type=MESH)

    loop(15, lambda j: pl.semaphore_signal(barrier, inc=1, device_id=peer(j + 1), device_id_type=MESH))
    pl.semaphore_signal(barrier, inc=1, device_id=device("x"), device_id_type=MESH)

    X16[s, h, l, y] = tok[...]
    PK[...] = jnp.zeros_like(PK)
    for k, vector in enumerate((qb, vb, ob, db, g1, b1, g2, b2)):
        PK[k // 4, k % 4 * 32 : k % 4 * 32 + 32] = vector[0, :].astype(F32)
    PK[2, :] = ub[0, :].astype(F32)
    for k in range(HEADS):
        parts = [qkvw[:, j * width + k * HEAD_DIM : j * width + (k + 1) * HEAD_DIM] for j in range(3)]
        WP[k, :, 0 : 3 * HEAD_DIM] = jnp.concatenate(parts, axis=1)
    WH[head, x] = WP[head]
    G[head, x] = PK[...]
    OW[h, y, x] = outw[...]
    DW[h, y, x] = downw[...]

    def quarter(sp, hp, lp):
        return pl.ds(pl.multiple_of(sp * 2048 + hp * 1024 + lp * 512, 512), 512)

    for hp in range(2):
        UW[s, h, l, y, x, :, hp * 512 : (hp + 1) * 512] = upw[:, quarter(s, hp, l)]

    pl.semaphore_wait(barrier, 16)

    half = width // 2

    def token_block(k):
        return lambda p: X16.at[p["s"], p["h"], p["l"], p["y"], :, pl.ds(k * half, half)]

    xg = [Gather("hlys", token_block(0)), Gather("hyls", token_block(1))]
    for g in xg:
        g.push()

    def small_copy(j, dst):
        return [
            peer_copy(WP.at[(head + j) % 16], WH.at[dst, x], (wss, wrs), j),
            peer_copy(PK, G.at[dst, x], (gss, grs), j),
        ]

    loop(15, lambda j: [d.start() for d in small_copy(j + 1, head)])

    up_sem = {}
    for flips in (("s",), ("l",), ("s", "l")):
        p = at(flips)
        for hp in range(2):
            up_sem[flips, hp] = ids()
            send(
                upw.at[:, quarter(p["s"], hp, p["l"])],
                UW.at[s, h, l, y, x, :, pl.ds(hp * 512, 512)],
                up_sem[flips, hp], flips,
            )

    def up_block(k):
        cols = (pl.ds(0, UW.shape[-1] // 8 * 5), pl.ds(UW.shape[-1] // 8 * 5, UW.shape[-1] // 8 * 3))[k]
        return lambda p: UW.at[:, p["h"], :, p["y"], p["x"], :, cols]

    def down_block(k):
        rows = (pl.ds(0, DW.shape[-2] // 8 * 5), pl.ds(DW.shape[-2] // 8 * 5, DW.shape[-2] // 8 * 3))[k]
        return lambda p: DW.at[p["h"], p["y"], p["x"], rows]

    og = Gather("hyx", lambda p: OW.at[p["h"], p["y"], p["x"]])
    ug = [Gather("hyx", up_block(0)), Gather("hxy", up_block(1))]
    dg = [Gather("hyx", down_block(0)), Gather("hxy", down_block(1))]
    for g in dg:
        g.push(along="x")
    og.push()

    for g in xg:
        g.pass_on("h")
    for flips in (("s",), ("l",), ("s", "l")):
        p = at(flips)
        for hp in range(2):
            wait(UW.at[p["s"], h, p["l"], y, x, :, pl.ds(hp * 512, 512)], up_sem[flips, hp], flips)
    for g in ug:
        g.push()
    xg[0].pass_on("l")
    xg[1].pass_on("y")

    def wait_small(j):
        for d in small_copy(j + 1, (head + 15 - j) % 16):
            d.wait_recv()

    loop(15, wait_small)
    small_sem = [ids(), ids()]
    send(WH.at[:, x], WH.at[:, x], small_sem[0], ("x",))
    send(G.at[:, x], G.at[:, x], small_sem[1], ("x",))
    xg[0].pass_on("h", "l")
    xg[1].pass_on("h", "y")
    og.pass_on("h")
    og.pass_on("y")
    og.pass_on("h", "y")
    for a, b in (("y", "l"), ("l", "y")):
        g = xg[0] if a == "y" else xg[1]
        for have in ((a,), ("h", a), (b, a), ("h", b, a)):
            g.pass_on(*have)

    for g in dg:
        g.push(along="hy")
    wait(WH.at[:, 1 - x], small_sem[0], ("x",))
    wait(G.at[:, 1 - x], small_sem[1], ("x",))

    spread = [spread_matrix(width, 32, j).astype(BF16) for j in range(4)]
    block_of, row_at = own_columns(32, width)
    mine = block_of == row_at
    arrived = block_of == row_at % 16 * 2 + row_at // 16
    for row, j, to in ((0, 2, 0), (0, 3, 1), (1, 0, 2), (1, 1, 3), (1, 2, 4), (1, 3, 5)):
        rows = jnp.concatenate([G[:, 0, row, :], G[:, 1, row, :]], axis=0).astype(BF16)
        VEC[to : to + 1, :] = jnp.sum(jnp.where(arrived, dot(rows, spread[j]), 0.0), axis=0, keepdims=True)
    for hp, yp, xp in itertools.product(range(2), repeat=3):
        r = hp * 4 + yp * 2 + xp
        UB[0:1, r * 128 : (r + 1) * 128] = G[s * 8 + hp * 4 + l * 2 + yp, xp, 2:3, :]
    out_bias, down_bias = VEC[0:1, :], VEC[1:2, :]
    gain_one, shift_one, gain_two, shift_two = (VEC[k : k + 1, :] for k in range(2, 6))
    first, second = G[head, 0, 0:1, :], G[head, 1, 0:1, :]
    head_bias = jnp.concatenate(
        [first[:, 0:32], second[:, 0:32], jnp.zeros((1, 64), F32), first[:, 32:64], second[:, 32:64]], axis=1
    )
    head_weight = WH[...].reshape(width, WH.shape[-1])[:, 0 : 3 * HEAD_DIM]

    length = 8 * tok.shape[0]
    qtiles = length // TILE
    scale = HEAD_DIM ** (-0.5)
    DH4, DB4, DSUM = C4, N4, FN

    def project(j):
        sp = s if j == 0 else 1 - s

        def body(i):
            hl = X16[sp, i // 2, i % 2].reshape(TILE, width)
            res = (dot(hl, head_weight) + head_bias).astype(BF16).astype(F32)
            rows = pl.ds(pl.multiple_of(i * TILE, TILE), TILE)
            QN[j, rows, :] = res[:, 0:64].astype(BF16)
            KN[j, rows, :] = res[:, 64:128].astype(BF16)
            VN[j, rows, :] = res[:, 128:192].astype(BF16)
            QKVT[j, :, rows] = res.T.astype(BF16)

        loop(qtiles, body)

    def attend(j):
        def body(i):
            cols = pl.ds(pl.multiple_of(i * TILE, TILE), TILE)
            q = QKVT[j, 0:64, cols] * jnp.asarray(scale, BF16)
            st = dot(KN[j], q)
            top = jnp.max(st, axis=0, keepdims=True)
            e = jnp.exp(st - top)
            total = jnp.sum(e, axis=0, keepdims=True)
            o = dot(QKVT[j, 128:192, :], e.astype(BF16)) / total
            OT[j, :, cols] = o
            OTB[j, :, cols] = o.astype(BF16)
            LSE[j, 0:1, cols] = top + jnp.log(total)

        loop(qtiles, body)

    tokens = tok.shape[0]

    def tok_cols(hp, lp, yp):
        return pl.ds(pl.multiple_of((hp * 4 + lp * 2 + yp) * tokens, tokens), tokens)

    others = (("h",), ("y",), ("h", "y"))
    a_sem = {(f, j): ids() for f in others for j in range(2)}

    def seq_cols(j):
        sp = s if j == 0 else 1 - s
        return pl.ds(pl.multiple_of(sp * 2 * tokens, 2 * tokens), 2 * tokens)

    def hand_out(j):
        for k, flips in enumerate(((),) + others):
            p = at(flips)
            piece = jnp.concatenate([OTB[j, :, tok_cols(p["h"], lp, p["y"])] for lp in range(2)], axis=1)
            if flips:
                AS[k, j] = piece
                send(AS.at[k, j], AT.at[h, y, :, seq_cols(j)], a_sem[flips, j], flips)
            else:
                AT[h, y, :, seq_cols(j)] = piece

    project(0)
    attend(0)
    hand_out(0)
    for g in ug:
        g.pass_on("h")
    ug[0].pass_on("y")
    ug[1].pass_on("x")
    for have in (("s",), ("h", "s"), ("l", "s"), ("h", "l", "s"), ("y", "s"), ("h", "y", "s"), ("l", "y", "s"), ("h", "l", "y", "s")):
        for g in xg:
            g.pull(*have)
    project(1)
    attend(1)
    hand_out(1)
    ug[0].pass_on("h", "y")
    ug[1].pass_on("h", "x")
    for g in dg:
        g.pass_on("h")
    for have in (("x",), ("h", "x"), ("y", "x"), ("h", "y", "x")):
        og.pull(*have)
    for flips in others:
        p = at(flips)
        for j in range(2):
            wait(AT.at[p["h"], p["y"], :, seq_cols(j)], a_sem[flips, j], flips)

    group = 4 * tokens
    half_n = tokens // 2
    A4[...] = AT[...].reshape(4 * HEAD_DIM, group).astype(F32).T.astype(BF16).reshape(A4.shape)

    def rows_of(k):
        return slice(k * half_n, (k + 1) * half_n)

    def half_rows(ref, k):
        return ref[:, :, rows_of(k), :].reshape(4 * half_n, ref.shape[-1])

    def core_rows(ref, k, sp):
        return ref[sp, :, rows_of(k), :].reshape(2 * half_n, ref.shape[-1])

    class GroupSum:
        def __init__(self, bufs, ref, product):
            self.sa, self.ra, self.sb, self.rb = bufs
            self.ref, self.product = ref, product
            self.to_core = [Tiles(self.sa.at[k], self.ra.at[k], "s", range(tiles)) for k in range(2)]
            self.to_pair = [Tiles(self.sb.at[k], self.rb.at[k], "l", range(tiles)) for k in range(2)]

        def start(self, k):
            def body(i):
                left = jnp.concatenate([core_rows(self.ref, k, 1 - s), core_rows(self.ref, k, s)], axis=0)
                v = self.product(left, i).reshape(2, 2, half_n, TILE)
                self.sa[k, i] = v[0].astype(BF16)
                self.to_core[k].send(i)
                KR[k, i] = v[1]

            loop(tiles, body)

        def relay(self, k):
            def body(i):
                self.to_core[k].wait(i)
                KR[k, i] += self.ra[k, i].astype(F32)
                self.sb[k, i] = KR[k, i, 1 - l].astype(BF16)
                self.to_pair[k].send(i)

            loop(tiles, body)

        def finish(self, k):
            for i in range(tiles):
                self.to_pair[k].wait(i)
            return jnp.concatenate([KR[k, i, l] + self.rb[k, i].astype(F32) for i in range(tiles)], axis=1)

    class GroupGather:
        def __init__(self, ref):
            self.ref = ref
            self.half = [
                Gather("ls", lambda p, k=k: ref.at[p["s"], p["l"], pl.ds(k * half_n, half_n)]) for k in range(2)
            ]

        def push(self, k, value):
            self.ref[s, l, rows_of(k)] = value
            self.half[k].push()

        def relay(self, k):
            self.half[k].pass_on("l")

        def pull(self, k):
            self.half[k].pull("s")
            self.half[k].pull("l", "s")

    def col_tile(i):
        return pl.ds(pl.multiple_of(i * TILE, TILE), TILE)

    def norm_forward(values, gain, shift):
        centered = values - jnp.mean(values, axis=-1, keepdims=True)
        recip = lax.rsqrt(jnp.mean(centered * centered, axis=-1, keepdims=True) + epsilon)
        normal = centered * recip
        return normal * gain + shift, normal, recip

    def norm_backward(upstream, normal, recip, gain):
        gain_grad = jnp.sum(upstream * normal, axis=0, keepdims=True)
        shift_grad = jnp.sum(upstream, axis=0, keepdims=True)
        scaled = upstream * gain
        inner = (
            scaled
            - jnp.mean(scaled, axis=-1, keepdims=True)
            - normal * jnp.mean(scaled * normal, axis=-1, keepdims=True)
        )
        return recip * inner, gain_grad, shift_grad

    def add_vectors(k, first_row, *rows):
        for at_row, row in zip(first_row, rows):
            VG[at_row : at_row + 1, :] = row if k == 0 else VG[at_row : at_row + 1, :] + row

    mark = len(sends)
    branch = GroupSum(
        (R1A, R1B, R1C, R1D), A4,
        lambda left, i: dot(left, OW[:, :, :, :, col_tile(i)].reshape(4 * HEAD_DIM, TILE)),
    )
    branch.start(0)
    branch.start(1)
    branch.relay(0)
    branch.relay(1)
    dg[0].pass_on("y")
    dg[1].pass_on("x")
    dg[0].pass_on("h", "y")
    dg[1].pass_on("h", "x")

    normed = GroupGather(N4)
    recips = []
    for k in range(2):
        r = rows_of(k)
        first_norm, normal_one, recip_one = norm_forward(
            tok[r, :].astype(F32) + branch.finish(k) + out_bias, gain_one, shift_one
        )
        FN[r, :] = first_norm
        NORM1[r, :] = normal_one
        recips.append(recip_one)
        normed.push(k, first_norm.astype(BF16))

    def pull_rest(pair):
        for have in (("x",), ("h", "x"), ("y", "x"), ("h", "y", "x")):
            pair[0].pull(*have)
        for have in (("y",), ("h", "y"), ("x", "y"), ("h", "x", "y")):
            pair[1].pull(*have)

    hidden = UB.shape[1]

    def up(k):
        def body(i):
            cols = col_tile(i)
            w = UW[:, :, :, :, :, :, cols].reshape(width, TILE)
            pre = dot(half_rows(N4, k), w) + UB[0:1, cols]
            phi = 0.5 * (1.0 + lax.erf(pre * (2.0 ** -0.5)))
            slope = phi + pre * (jnp.exp(-0.5 * pre * pre) * ((2.0 * math.pi) ** -0.5))
            GP[:, :, rows_of(k), cols] = slope.reshape(2, 2, half_n, TILE)
            C4[:, :, rows_of(k), cols] = (pre * phi).astype(BF16).reshape(2, 2, half_n, TILE)

        loop(hidden // TILE, body)

    feed = GroupSum(
        (R2A, R2B, R2C, R2D), C4,
        lambda left, i: dot(left, DW[:, :, :, :, col_tile(i)].reshape(hidden, TILE)),
    )
    normed.relay(0)
    pull_rest(ug)
    normed.pull(0)
    up(0)
    normed.relay(1)
    pull_rest(dg)
    feed.start(0)
    normed.pull(1)
    up(1)
    settle(mark)
    feed.relay(0)
    feed.start(1)
    feed.relay(1)

    d_feeds = GroupGather(DF4)
    for k in range(2):
        r = rows_of(k)
        final, normal_two, recip_two = norm_forward(
            FN[r, :] + feed.finish(k) + down_bias, gain_two, shift_two
        )
        out_o[r, :] = final.astype(BF16)
        d_second, gain_two_grad, shift_two_grad = norm_backward(
            cot[r, :].astype(F32), normal_two, recip_two, gain_two
        )
        DSEC[r, :] = d_second
        d_feed = d_second.astype(BF16)
        d_feeds.push(k, d_feed)
        add_vectors(
            k, (1, 4, 5), jnp.sum(d_feed.astype(F32), axis=0, keepdims=True), gain_two_grad, shift_two_grad
        )

    def transpose_rows(i):
        cols = pl.ds(pl.multiple_of(i * 128, 128), 128)
        t = N4[:, :, :, cols].reshape(group, 128)
        t = t.astype(F32).T.astype(BF16).reshape(2, 2, 32, group)
        for yp, xp in itertools.product(range(2), repeat=2):
            to = pl.ds(pl.multiple_of((i // 4 * 2 + i % 2) * 32, 32), 32)
            N4T[(i // 2) % 2, yp, xp, to, :] = t[yp, xp]
        C4T[i // 4, (i // 2) % 2, i % 2] = C4[:, :, :, cols].reshape(group, 128).astype(F32).T.astype(BF16)

    loop(8, transpose_rows)

    def d_hidden(k):
        def body(i):
            rows = DW[i // 2, i % 2].reshape(TILE, width)
            cols = col_tile(i)
            slope = GP[:, :, rows_of(k), cols].reshape(4 * half_n, TILE)
            v = (dot(half_rows(DF4, k), rows, 1, 1) * slope).astype(BF16)
            DH4[:, :, rows_of(k), cols] = v.reshape(2, 2, half_n, TILE)
            total = jnp.sum(v.astype(F32), axis=0, keepdims=True)
            UB[1:2, cols] = total if k == 0 else UB[1:2, cols] + total

        loop(hidden // TILE, body)

    class Scatter:
        def __init__(self, bufs, product, cut=tiles // 2):
            self.sa, self.ra, self.sb, self.rb, self.sc, self.rc, self.keep = bufs
            self.product = product
            self.shape = self.sa.shape[1:]
            self.parts = []
            for k, (one, two) in enumerate((("x", "y"), ("y", "x"))):
                of = (range(cut), range(cut, tiles))[k]
                self.parts.append((
                    one, two, of,
                    Tiles(self.sa, self.ra, one, of), Tiles(self.sb, self.rb, two, of), Tiles(self.sc, self.rc, "h", of),
                ))

        def first(self):
            for one, two, of, a, b, c in self.parts:
                def body(i, one=one, of=of, a=a):
                    i = of[0] + i
                    self.sa[i] = self.product(one, 1 - here[one], i).reshape(self.shape).astype(BF16)
                    a.send(i)

                loop(len(of), body)

        def second(self):
            for one, two, of, a, b, c in self.parts:
                def body(i, one=one, two=two, of=of, a=a, b=b):
                    i = of[0] + i
                    v = self.product(one, here[one], i).reshape(self.shape)
                    a.wait(i)
                    self.keep[i] = v + self.ra[i].astype(F32)
                    self.sb[i] = self.keep[i, :, 1 - here[two]].astype(BF16)
                    b.send(i)

                loop(len(of), body)

        def third(self):
            for one, two, of, a, b, c in self.parts:
                def body(i, two=two, of=of, b=b, c=c):
                    i = of[0] + i
                    b.wait(i)
                    self.keep[i, :, 0] = self.keep[i, :, here[two]] + self.rb[i].astype(F32)
                    self.sc[i] = self.keep[i, 1 - h, 0].astype(BF16)
                    c.send(i)

                loop(len(of), body)

        def last(self, out):
            for one, two, of, a, b, c in self.parts:
                def body(i, of=of, c=c):
                    i = of[0] + i
                    c.wait(i)
                    out[:, col_tile(i)] = self.keep[i, h, 0] + self.rc[i].astype(F32)

                loop(len(of), body)

    def up_product(dim, v, i):
        rows = N4T[:, :, v] if dim == "x" else N4T[:, v]
        return dot(rows.reshape(group, group), DH4[:, :, :, col_tile(i)].reshape(group, TILE))

    def down_product(dim, v, i):
        rows = C4T[:, :, v] if dim == "x" else C4T[:, v]
        return dot(rows.reshape(group, group), DF4[:, :, :, col_tile(i)].reshape(group, TILE))

    def out_product(dim, v, i):
        rows = AT[:, :, pl.ds(pl.multiple_of(v * 32, 32), 32), :] if dim == "x" else AT[:, v]
        return dot(rows.reshape(128, group), DB4[:, :, :, col_tile(i)].reshape(group, TILE))

    down_s = Scatter((DSA, DRA, DSB, DRB, DSC, DRC, DK), down_product)
    up_s = Scatter((USA, URA, USB, URB, USC, URC, UK), up_product)
    out_s = Scatter((OSA, ORA, OSB, ORB, OSC, ORC, OK), out_product, 3)

    def up_rows(i):
        return UW[i // 2, i % 2].reshape(TILE, hidden)

    d_first = GroupSum((R1A, R1B, R1C, R1D), DH4, lambda left, i: dot(left, up_rows(i), 1, 1))
    d_branches = GroupGather(DB4)
    d_feeds.relay(0)
    d_feeds.pull(0)
    d_hidden(0)
    d_feeds.relay(1)
    d_first.start(0)
    d_feeds.pull(1)
    d_hidden(1)
    down_s.first()
    d_first.relay(0)
    d_first.start(1)
    d_first.relay(1)
    for k in range(2):
        r = rows_of(k)
        d_sum_one, gain_one_grad, shift_one_grad = norm_backward(
            DSEC[r, :] + d_first.finish(k), NORM1[r, :], recips[k], gain_one
        )
        DSUM[r, :] = d_sum_one
        d_branch = d_sum_one.astype(BF16)
        d_branches.push(k, d_branch)
        add_vectors(
            k, (0, 2, 3), jnp.sum(d_branch.astype(F32), axis=0, keepdims=True), gain_one_grad, shift_one_grad
        )
    up_s.first()
    for k in range(2):
        d_branches.relay(k)
    for k in range(2):
        d_branches.pull(k)

    d_att = dot(DB4[...].reshape(group, width), OW[...].reshape(4 * HEAD_DIM, width), 1, 1).astype(BF16)
    d_att = d_att.astype(F32).T.astype(BF16).reshape(2, 2, HEAD_DIM, group)
    DS[...] = d_att
    d_sem = {f: ids() for f in others}
    for flips in others:
        p = at(flips)
        send(DS.at[p["h"], p["y"]], DR.at[h, y], d_sem[flips], flips)
    DR[h, y] = DS[h, y]

    out_s.first()
    down_s.second()
    up_s.second()

    VG[6:8, :] = jnp.zeros((2, width), F32)
    picked = [spread_matrix(width, 32, j) for j in range(4)]

    def exact_pick(row, j):
        a = jnp.where(mine, VG[row : row + 1, :], 0.0)
        hi = a.astype(BF16)
        rest = a - hi.astype(F32)
        mid = rest.astype(BF16)
        low = (rest - mid.astype(F32)).astype(BF16)
        r = picked[j].astype(BF16)
        return dot(hi, r, 1, 1) + dot(mid, r, 1, 1) + dot(low, r, 1, 1)

    SG[...] = jnp.zeros_like(SG)
    SG[:, 0, :] = exact_pick(0, 2) + exact_pick(1, 3)
    SG[:, 1, :] = exact_pick(2, 0) + exact_pick(3, 1) + exact_pick(4, 2) + exact_pick(5, 3)
    for hp, yp, xp in itertools.product(range(2), repeat=3):
        r = hp * 4 + yp * 2 + xp
        SG[(s * 8 + hp * 4 + l * 2 + yp) * 2 + xp, 2:3, :] = UB[1:2, r * 128 : (r + 1) * 128]

    for flips in others:
        p = at(flips)
        wait(DR.at[p["h"], p["y"]], d_sem[flips], flips)
    for sp in range(2):
        j = s if sp == 0 else 1 - s
        for hp, lp, yp in itertools.product(range(2), repeat=3):
            part = DR[hp, yp, :, (sp * 2 + lp) * tokens : (sp * 2 + lp + 1) * tokens]
            at_tok = (hp * 4 + lp * 2 + yp) * tokens
            DAT[j, :, at_tok : at_tok + tokens] = part
            DA[j, at_tok : at_tok + tokens, :] = part.astype(F32).T.astype(BF16)

    def attend_back(j):
        DKV[...] = jnp.zeros_like(DKV)

        def body(i):
            cols = col_tile(i)
            q = QKVT[j, 0:64, cols] * jnp.asarray(scale, BF16)
            p = jnp.exp(dot(KN[j], q) - LSE[j, 0:1, cols])
            da = DAT[j, :, cols]
            delta = jnp.sum(da.astype(F32) * OT[j, :, cols], axis=0, keepdims=True)
            dp = dot(VN[j], da)
            ds = (p * (dp - delta) * scale).astype(BF16)
            DQT[j, :, cols] = dot(QKVT[j, 64:128, :], ds)
            DKV[0] += dot(ds, QN[j, cols, :])
            DKV[1] += dot(p.astype(BF16), DA[j, cols, :])

        loop(qtiles, body)
        dqt = DQT[j].astype(BF16).astype(F32)
        dq = dqt.T
        dk, dv = DKV[0].astype(BF16).astype(F32), DKV[1].astype(BF16).astype(F32)
        DQKV[j] = jnp.concatenate([dq, dk, dv], axis=1).astype(BF16)
        DQKVT[j, 0:64, :] = dqt.astype(BF16)
        DQKVT[j, 64:128, :] = dk.T.astype(BF16)
        DQKVT[j, 128:192, :] = dv.T.astype(BF16)
        return jnp.sum(dq, axis=0, keepdims=True), jnp.sum(dv, axis=0, keepdims=True)

    def input_tile(j, part, i):
        w = WH[pl.ds(pl.multiple_of(i * 4, 4), 4)].reshape(TILE, WH.shape[-1])[:, 0 : 3 * HEAD_DIM]
        rows = pl.ds(pl.multiple_of(part * (length // 2), length // 2), length // 2)
        return dot(DQKV[j, rows, :], w, 1, 1).reshape(2, 2, tokens, TILE)

    in_order = (0, 1, 2, 3)
    far, near = 1 - h, h
    ia, ib, ic, id_ = ({(p, i): ids() for p in range(2) for i in range(tiles)} for _ in range(4))

    def in_sent(i):
        return (C4T if i < tiles // 2 else N4T).at[:, :, :, :, pl.ds(i % 2 * TILE, TILE)]

    q1, v1 = attend_back(1)
    down_s.third()
    for p, part in enumerate((far, near)):
        for i in in_order:
            piece = in_sent(i).at[part]
            piece[...] = input_tile(1, part, i).astype(BF16)
            send(piece, IRA.at[i, part], ia[p, i], ("s",))
    q0, v0 = attend_back(0)
    to_x = Tiles(QSA, QRA, "x", range(tiles))

    def q_first(i):
        cols = col_tile(i)
        v = dot(DQKVT[0], X16[s, :, :, :, :, cols].reshape(length, TILE))
        v += dot(DQKVT[1], X16[1 - s, :, :, :, :, cols].reshape(length, TILE))
        v = v.T.reshape(2, 2, 2, 32, 3 * HEAD_DIM)
        for xp in range(2):
            QK[i, xp] = v[:, :, xp]
        QSA[i, :, :, :, 0 : 3 * HEAD_DIM] = QK[i, 1 - x].astype(BF16)
        to_x.send(i)

    def in_second(p):
        part = (far, near)[p]
        for i in in_order:
            wait(IRA.at[i, part], ia[p, i], ("s",))
            IK[i, part] = input_tile(0, part, i) + IRA[i, part].astype(F32)
            dim = "l" if i < 1 else "y"
            ISB[i, part] = (IK[i, part, 1 - l] if dim == "l" else IK[i, part, :, 1 - y]).astype(BF16)
            send(ISB.at[i, part], IRB.at[i, part], ib[p, i], (dim,))

    def in_third(p):
        part = (far, near)[p]
        for i in in_order:
            one, two = ("l", "y") if i < 1 else ("y", "l")
            wait(IRB.at[i, part], ib[p, i], (one,))
            IK[i, part, 0] = (IK[i, part, l] if one == "l" else IK[i, part, :, y]) + IRB[i, part].astype(F32)
            ISC[i, part] = IK[i, part, 0, 1 - here[two]].astype(BF16)
            send(ISC.at[i, part], IRC.at[i, part], ic[p, i], (two,))

    def in_summed(p, i):
        part = (far, near)[p]
        two = "y" if i < 1 else "l"
        wait(IRC.at[i, part], ic[p, i], (two,))
        return IK[i, part, 0, here[two]] + IRC[i, part].astype(F32)

    def q_second(i):
        to_x.wait(i)
        v = QK[i, x] + QRA[i, :, :, :, 0 : 3 * HEAD_DIM].astype(F32)
        QSB[i // 2, i % 2, :, :, :, 0 : 3 * HEAD_DIM] = v.astype(BF16)

    def piece_copy(j):
        to = (head + j) % 16
        return peer_copy(
            QSB.at[to // 8, (to // 4) % 2, (to // 2) % 2, to % 2], QG.at[head], (hss, hrs), 16 + j
        )

    in_second(0)
    in_second(1)
    up_s.third()
    out_s.second()
    loop(tiles, q_first)
    bq, bv = q0 + q1, v0 + v1
    for k in range(2):
        b = head * 2 + k
        lanes = slice(k * 32, k * 32 + 32)
        SG[b, 0:1, :] += jnp.concatenate([bq[:, lanes], bv[:, lanes], jnp.zeros((1, 64), F32)], axis=1)

    def grad_copy(j):
        return peer_copy(SG.at[pl.ds((head + j) % 16 * 2, 2)], RG.at[j], (hss, hrs), j)

    loop(15, lambda j: grad_copy(j + 1).start())
    RG[0] = SG[pl.ds(head * 2, 2)]
    in_third(0)
    out_s.third()
    loop(tiles, q_second)
    loop(15, lambda j: piece_copy(j + 1).start())
    QG[head] = QSB[s, h, l, y]
    for i in in_order:
        ISD[i] = in_summed(0, i).astype(BF16)
        send(ISD.at[i], IRD.at[i], id_[0, i], ("h",))
    in_third(1)
    down_s.last(downg_o)
    loop(15, lambda j: grad_copy(j + 1).wait_recv())
    small_sum = jnp.sum(RG[...], axis=0)
    SX[0:2] = small_sum
    x_sem = ids()
    send(SX.at[1 - x], RX, x_sem, ("x",))
    up_s.last(UF)
    uf_sem = {}
    for flips in (("s",), ("l",), ("s", "l")):
        p = at(flips)
        for hp in range(2):
            uf_sem[flips, hp] = ids()
            send(
                UF.at[pl.ds(pl.multiple_of((p["s"] * 2 + p["l"]) * 32, 32), 32), pl.ds(hp * 512, 512)],
                upg_o.at[:, quarter(s, hp, l)], uf_sem[flips, hp], flips,
            )
    for hp in range(2):
        upg_o[:, quarter(s, hp, l)] = UF[pl.ds(pl.multiple_of((s * 2 + l) * 32, 32), 32), hp * 512 : (hp + 1) * 512]
    out_s.last(outg_o)
    wait(RX, x_sem, ("x",))
    small_o[...] = SX[x] + RX[...]
    loop(15, lambda j: piece_copy(j + 1).wait_recv())
    for k in range(HEADS // 2):
        a, b = QG[2 * k].astype(F32), QG[2 * k + 1].astype(F32)
        for part in range(3):
            lanes = slice(part * 64, part * 64 + 64)
            to = part * width + k * 128
            qkvg_o[:, to : to + 128] = jnp.concatenate([a[:, lanes], b[:, lanes]], axis=1)
    for i in range(tiles):
        total = in_summed(1, i) + DSUM[:, i * TILE : (i + 1) * TILE]
        wait(IRD.at[i], id_[0, i], ("h",))
        ig_o[:, i * TILE : (i + 1) * TILE] = total + IRD[i].astype(F32)

    for flips in (("s",), ("l",), ("s", "l")):
        p = at(flips)
        for hp in range(2):
            wait(upg_o.at[:, quarter(p["s"], hp, p["l"])], uf_sem[flips, hp], flips)

    for d in sends:
        d.wait_send()

    def small_sent(j):
        for d in small_copy(j + 1, head):
            d.wait_send()
        grad_copy(j + 1).wait_send()

    loop(15, small_sent)
    loop(15, lambda j: piece_copy(j + 1).wait_send())


def hand_over(*refs):
    large, small, outs, sems = refs[:6], refs[6], refs[7:22], refs[22]
    copies = [pltpu.make_async_copy(a, b, sems.at[k]) for k, (a, b) in enumerate(zip(large, outs))]
    for c in copies:
        c.start()
    places = ((0, 0, 32), (0, 32, 32), (0, 64, 32), (2, 0, 128), (0, 96, 32), (1, 0, 32), (1, 32, 32), (1, 64, 32), (1, 96, 32))
    for ref, (row, lane, count) in zip(outs[6:], places):
        ref[...] = small[row : row + 1, lane : lane + count]
    for c in copies:
        c.wait()


def on_block(
    tokens, qkv_weight, out_weight, up_weight, down_weight,
    query_bias, value_bias, out_bias, up_bias, down_bias,
    norm1_gain, norm1_bias, norm2_gain, norm2_bias, cotangent,
):
    n, width = tokens.shape[1], tokens.shape[2]
    hidden = up_weight.shape[1] // 4
    group = 4 * n
    length = 8 * n
    tiles = width // TILE
    vectors = [
        v.reshape(1, -1)
        for v in (query_bias, value_bias, out_bias, up_bias, down_bias, norm1_gain, norm1_bias, norm2_gain, norm2_bias)
    ]

    def b(*shape):
        return pltpu.VMEM(shape, BF16)

    def f(*shape):
        return pltpu.VMEM(shape, F32)

    group_bufs = [b(2, tiles, 2, n // 2, TILE), b(2, tiles, 2, n // 2, TILE), b(2, tiles, n // 2, TILE), b(2, tiles, n // 2, TILE)]

    def scatter_bufs(rows):
        return [
            b(tiles, 2, 2, rows, TILE), b(tiles, 2, 2, rows, TILE),
            b(tiles, 2, rows, TILE), b(tiles, 2, rows, TILE),
            b(tiles, rows, TILE), b(tiles, rows, TILE),
            f(tiles, 2, 2, rows, TILE),
        ]

    sem = pltpu.SemaphoreType.DMA
    scratch = [
        f(8, 128), b(2, 2, 2, 2, n, width), b(HEADS, 32, 256), b(HEADS, 2, 32, 256), f(HEADS, 2, 8, 128),
        b(2, 2, 2, 32, width), b(2, 2, 2, 2, 2, 32, hidden), b(2, 2, 2, 128, width),
        b(2, length, 64), b(2, length, 64), b(2, length, 64), b(2, 192, length), f(2, 64, length), b(2, 64, length),
        f(2, 8, length), b(4, 2, 64, group // 2), b(2, 2, 64, group), b(2, 2, n, 256),
        *group_bufs, *group_bufs, f(2, tiles, 2, n // 2, TILE),
        b(2, 2, n, width), b(2, 2, 2, 128, group), b(2, 2, n, hidden), b(2, 2, 2, 128, group), f(2, 2, n, hidden),
        b(2, 2, n, width),
        f(n, width), f(n, width), f(n, width),
        b(2, 2, 64, group), b(2, 2, 64, group), b(2, length, 64), b(2, 64, length), f(2, length, 64), f(2, 64, length),
        b(2, length, 192), b(2, 192, length),
        *scatter_bufs(128), f(128, width),
        *scatter_bufs(128),
        *scatter_bufs(32),
        b(tiles, 2, 2, 2, n, TILE), b(tiles, 2, 2, n, TILE), b(tiles, 2, 2, n, TILE),
        b(tiles, 2, n, TILE), b(tiles, 2, n, TILE), b(tiles, n, TILE), b(tiles, n, TILE), f(tiles, 2, 2, 2, n, TILE),
        b(tiles, 2, 2, 32, 256), b(tiles, 2, 2, 32, 256), f(tiles, 2, 2, 2, 32, 192), b(2, 2, 2, 2, 32, 256), b(HEADS, 32, 256),
        f(8, width), f(8, hidden), f(8, width), f(32, 8, 128), f(HEADS, 2, 8, 128), f(2, 8, 128), f(8, 128),
        sem((300,)), sem((300,)), sem((16,)), sem((16,)), sem((16,)), sem((16,)), sem((32,)), sem((32,)),
    ]
    vmem = pl.BlockSpec(memory_space=pltpu.VMEM)
    shapes = [
        jax.ShapeDtypeStruct((n, width), BF16),
        jax.ShapeDtypeStruct((n, width), F32),
        jax.ShapeDtypeStruct((32, 3 * width), F32),
        jax.ShapeDtypeStruct((32, width), F32),
        jax.ShapeDtypeStruct((32, 4 * hidden), F32),
        jax.ShapeDtypeStruct((128, width), F32),
        jax.ShapeDtypeStruct((8, 128), F32),
    ]
    results = pl.pallas_call(
        layer_kernel,
        out_shape=shapes,
        in_specs=[vmem] * 15,
        out_specs=[vmem] * 7,
        scratch_shapes=scratch,
        compiler_params=pltpu.CompilerParams(
            collective_id=0, has_side_effects=True, vmem_limit_bytes=63 * 2**20
        ),
        name="layer",
    )(tokens[0], qkv_weight, out_weight, up_weight, down_weight, *vectors, cotangent[0])
    lengths = [v.shape[1] for v in vectors]
    everywhere = pl.BlockSpec(memory_space=pl.ANY)
    done = pl.pallas_call(
        hand_over,
        out_shape=shapes[:6] + [jax.ShapeDtypeStruct((1, k), F32) for k in lengths],
        in_specs=[vmem] * 7,
        out_specs=[everywhere] * 6 + [vmem] * 9,
        scratch_shapes=[sem((6,))],
        name="results",
    )(*results)
    return (
        done[0][None], done[1][None], *done[2:6], *(v.reshape(-1) for v in done[6:]),
    )


def solution(mesh):
    placed = (
        P(("seq", "fsdp"), "ctx", None),
        P(("seq", "ctx", "fsdp"), None),
        P(("seq", "ctx", "fsdp"), None),
        P(("seq", "ctx", "fsdp"), None),
        P(("seq", "ctx", "fsdp"), None),
        P(("seq", "ctx", "fsdp")),
        P(("seq", "ctx", "fsdp")),
        P(("seq", "ctx", "fsdp")),
        P(("seq", "ctx", "fsdp")),
        P(("seq", "ctx", "fsdp")),
        P(("seq", "ctx", "fsdp")),
        P(("seq", "ctx", "fsdp")),
        P(("seq", "ctx", "fsdp")),
        P(("seq", "ctx", "fsdp")),
        P(("seq", "fsdp"), "ctx", None),
    )
    fast = dict(mesh.shape) == {"seq": 2, "ctx": 8, "fsdp": 2}
    return jax.shard_map(
        on_block if fast else on_device,
        mesh=mesh,
        in_specs=placed,
        out_specs=(
            P(("seq", "fsdp"), "ctx", None),
            P(("seq", "fsdp"), "ctx", None),
            P(("seq", "ctx", "fsdp"), None),
            P(("seq", "ctx", "fsdp"), None),
            P(("seq", "ctx", "fsdp"), None),
            P(("seq", "ctx", "fsdp"), None),
            P(("seq", "ctx", "fsdp")),
            P(("seq", "ctx", "fsdp")),
            P(("seq", "ctx", "fsdp")),
            P(("seq", "ctx", "fsdp")),
            P(("seq", "ctx", "fsdp")),
            P(("seq", "ctx", "fsdp")),
            P(("seq", "ctx", "fsdp")),
            P(("seq", "ctx", "fsdp")),
            P(("seq", "ctx", "fsdp")),
        ),
        check_vma=False,
    )
```
